32 devices in a mesh: ctx: 4 (over z), tp: 4 (over x, core), pp: 2 (over y).
Axes of the slice: x: 2, y: 2, z: 4, core: 2. Of those that a mesh axis runs over, the one named last changes fastest.
Arguments:
- queries: bfloat16 [2, 512, 4096], P('pp', 'ctx', 'tp'), may hold values from -0.59765625 to 0.59765625
- key_input: bfloat16 [2, 512, 4096], P('pp', 'ctx', 'tp'), may hold values from -6 to 6
- values: bfloat16 [2, 512, 4096], P('pp', 'ctx', 'tp'), may hold values from -6 to 6
- log_decay: float32 [2, 512, 32], P('pp', 'ctx', 'tp'), may hold values from -1 to 0
- conv_weight: float32 [2, 4, 4096], P('pp', None, 'tp'), may hold values from -3 to 3
- out_grad: bfloat16 [2, 512, 4096], P('pp', 'ctx', 'tp'), may hold values from -6 to 6
Outputs:
- layer_output: bfloat16 [2, 512, 4096], P('pp', 'ctx', 'tp')
- input_grad_next: bfloat16 [2, 512, 4096], P('pp', 'ctx', 'tp')
The draws below stay inside these ranges and needn't reach their ends.
All inputs are finite; a program needn't handle non-finite values.
Results may differ from the reference program's by a relative error of at most 0.006.
The reference program's roundings to bfloat16 on the way count: a program that leaves them out, or rounds other values in their place, can miss the bound.
Values may be sent and summed in bfloat16 or wider, within the bound.
No kernel may reach another device: no remote copies, remote signals or barrier semaphores. Data moves between devices by JAX's collectives and lax.ppermute only.
A program may use at most 64 MiB of HBM per device.

```python
import math
import jax
import jax.numpy as jnp
from jax import lax

HEAD_COUNT = 32
HEAD_DIM = 128
KERNEL = 4
TOK_DEV = 128
SEQUENCE_LENGTH = 512
SECTION_COUNT = 2


def draw_log_decay(key, part):
    random_subkeys = jax.random.split(key, 7)
    slow_share = 0.5
    slow_heads = jax.random.uniform(random_subkeys[0], (SECTION_COUNT, 1, HEAD_COUNT)) < slow_share
    fast_scale = jnp.exp(jax.random.uniform(random_subkeys[1], (SECTION_COUNT, 1, HEAD_COUNT), minval=math.log(30.0), maxval=math.log(50.0)))
    slow_scale = SEQUENCE_LENGTH * jnp.exp(jax.random.uniform(random_subkeys[2], (SECTION_COUNT, 1, HEAD_COUNT), minval=math.log(2.0), maxval=math.log(6.0)))
    time_scale = jnp.where(slow_heads, slow_scale, fast_scale)
    block_count = SEQUENCE_LENGTH // TOK_DEV
    block_factor = jnp.exp(jax.random.uniform(random_subkeys[3], (SECTION_COUNT, block_count, 1, HEAD_COUNT), minval=math.log(0.5), maxval=math.log(2.0)))
    block_factor = jnp.broadcast_to(block_factor, (SECTION_COUNT, block_count, TOK_DEV, HEAD_COUNT)).reshape(SECTION_COUNT, SEQUENCE_LENGTH, HEAD_COUNT)
    position_factor = jnp.exp(jax.random.uniform(random_subkeys[4], (SECTION_COUNT, SEQUENCE_LENGTH, HEAD_COUNT), minval=math.log(0.5), maxval=math.log(2.0)))
    spike_impact = jax.random.uniform(random_subkeys[5], (SECTION_COUNT, SEQUENCE_LENGTH, HEAD_COUNT)) < 3.0 / SEQUENCE_LENGTH
    spike_penalty = jax.random.uniform(random_subkeys[6], (SECTION_COUNT, SEQUENCE_LENGTH, HEAD_COUNT), minval=0.2, maxval=0.5)
    stable_portion = -(block_factor * position_factor) / time_scale
    return (stable_portion + jnp.where(spike_impact, jnp.log(1.0 - spike_penalty), 0.0)).astype(jnp.float32)


def levels(stream_key, extent, pieces, low, high):
    level = 1.0
    for position, parts in pieces:
        steps = jax.random.uniform(jax.random.fold_in(jax.random.fold_in(stream_key, 6), position), (parts,), jnp.float32, low / len(pieces), high / len(pieces))
        level = level * jnp.repeat(jnp.exp(steps), extent[position] // parts).reshape((-1,) + (1,) * (len(extent) - 1 - position))
    return level


def normal_values(own_key, extent, deviation, limit, cuts=(), kind=jnp.bfloat16):
    entries = deviation * jax.random.normal(own_key, extent, jnp.float32)
    if cuts:
        entries = entries * levels(own_key, extent, cuts, -0.22, 0.18)
    return jnp.clip(entries, -limit, limit).astype(kind)


def setup_inputs(seed: int = 0) -> dict:
    arg_keys = jax.random.split(jax.random.key(seed), 7)
    queries = normal_values(arg_keys[0], (SECTION_COUNT, SEQUENCE_LENGTH, HEAD_COUNT * HEAD_DIM), 0.1, 0.59765625, ((0, 2), (1, 4), (2, 4)))
    key_input = normal_values(arg_keys[1], (SECTION_COUNT, SEQUENCE_LENGTH, HEAD_COUNT * HEAD_DIM), 1.0, 6.0, ((0, 2), (1, 4), (2, 4)))
    values = normal_values(arg_keys[2], (SECTION_COUNT, SEQUENCE_LENGTH, HEAD_COUNT * HEAD_DIM), 1.0, 6.0, ((0, 2), (1, 4), (2, 4)))
    log_decay = draw_log_decay(jax.random.fold_in(arg_keys[6], 71), 0)
    conv_weight = normal_values(arg_keys[4], (SECTION_COUNT, KERNEL, HEAD_COUNT * HEAD_DIM), KERNEL ** -0.5, 3.0, ((0, 2), (2, 4)), jnp.float32)
    out_grad = normal_values(arg_keys[5], (SECTION_COUNT, SEQUENCE_LENGTH, HEAD_COUNT * HEAD_DIM), 1.0, 6.0, ((0, 2), (1, 4), (2, 4)))
    return dict(queries=queries, key_input=key_input, values=values, log_decay=log_decay, conv_weight=conv_weight, out_grad=out_grad)


def to_half(value):
    return lax.optimization_barrier(value.astype(jnp.bfloat16)).astype(jnp.float32)

def decay_table(cum_decay):
    transposed = jnp.swapaxes(cum_decay, -1, -2)
    differ = transposed[..., :, None] - transposed[..., None, :]
    tok_rows = cum_decay.shape[-2]
    causal = jnp.arange(tok_rows)[:, None] >= jnp.arange(tok_rows)[None, :]
    return jnp.where(causal, jnp.exp(jnp.where(causal, differ, 0.0)), 0.0)

def one_section(section_in):
    queries, key_input, values, log_decay, conv_weight, out_grad = section_in
    seq_len = key_input.shape[0]
    feat_width = key_input.shape[1]
    blocks = seq_len // TOK_DEV
    tap_count = conv_weight.shape[0]
    width_all = HEAD_COUNT * HEAD_DIM
    padded = jnp.concatenate([jnp.zeros((tap_count - 1, feat_width), jnp.float32), key_input.astype(jnp.float32)], 0)
    conv_sum = jnp.zeros((seq_len, feat_width), jnp.float32)
    for tap_index in range(tap_count):
        start_row = tap_count - 1 - tap_index
        conv_sum = conv_sum + conv_weight[tap_index] * padded[start_row:start_row + seq_len]
    head_shape = (blocks, TOK_DEV, HEAD_COUNT, HEAD_DIM)
    key_blk = to_half(conv_sum).reshape(head_shape)
    query_tile_block = queries.astype(jnp.float32).reshape(head_shape)
    value_tile_block = values.astype(jnp.float32).reshape(head_shape)
    grad_blk = out_grad.astype(jnp.float32).reshape(head_shape)
    cum_decay = jnp.cumsum(log_decay.reshape(blocks, TOK_DEV, HEAD_COUNT), axis=1)
    block_total = cum_decay[:, -1]
    mixing = decay_table(cum_decay)
    scores = jnp.einsum('cthk,cshk->chts', query_tile_block, key_blk)
    weights = to_half(scores * mixing)
    weight_after = jnp.exp(block_total[:, None, :] - cum_decay)[..., None]
    keys_times_decay = to_half(key_blk * weight_after)
    block_state = jnp.einsum('cshk,cshv->chkv', keys_times_decay, value_tile_block)

    def forward_step(running, scan_item):
        decay_sum, block_sum = scan_item
        return (jnp.exp(decay_sum)[:, None, None] * running + block_sum, running)
    zero_state = jnp.zeros(block_state.shape[1:], jnp.float32)
    _, leading_rows = lax.scan(forward_step, zero_state, (block_total, block_state))
    opening_half = to_half(leading_rows)
    attended = jnp.einsum('chts,cshv->cthv', weights, value_tile_block)
    attended = attended + jnp.exp(cum_decay)[..., None] * jnp.einsum('cthk,chkv->cthv', query_tile_block, opening_half, precision=lax.Precision.HIGHEST)
    squares = lax.optimization_barrier(jnp.sum((attended * attended).reshape(blocks, TOK_DEV, width_all), -1))
    root_mean = jnp.sqrt(squares / width_all + 1e-06)
    normed = attended / root_mean[..., None, None]
    layer_output = normed.astype(jnp.bfloat16).reshape(seq_len, feat_width)
    shift_mean = lax.optimization_barrier(jnp.sum((grad_blk * normed).reshape(blocks, TOK_DEV, width_all), -1)) / width_all
    gradient_of_attended = to_half((grad_blk - normed * shift_mean[..., None, None]) / root_mean[..., None, None])
    queries_times_decay = to_half(query_tile_block * jnp.exp(cum_decay)[..., None])
    block_adjoint = jnp.einsum('cthk,cthv->chkv', queries_times_decay, gradient_of_attended)

    def backward_step(running, scan_item):
        decay_sum, adjoint = scan_item
        return (adjoint + jnp.exp(decay_sum)[:, None, None] * running, running)
    _, state_following = lax.scan(backward_step, zero_state, (block_total, block_adjoint), reverse=True)
    trailing_half = to_half(state_following)
    score_grad = to_half(jnp.einsum('cthv,cshv->chts', gradient_of_attended, value_tile_block) * mixing)
    query_grad = jnp.einsum('chts,cshk->cthk', score_grad, key_blk)
    query_grad = query_grad + jnp.exp(cum_decay)[..., None] * jnp.einsum('cthv,chkv->cthk', gradient_of_attended, opening_half, precision=lax.Precision.HIGHEST)
    ckey_grad = jnp.einsum('chts,cthk->cshk', score_grad, query_tile_block)
    ckey_grad = ckey_grad + weight_after * jnp.einsum('cshv,chkv->cshk', value_tile_block, trailing_half, precision=lax.Precision.HIGHEST)
    value_grad = jnp.einsum('chts,cthv->cshv', weights, gradient_of_attended)
    value_grad = value_grad + weight_after * jnp.einsum('cshk,chkv->cshv', key_blk, trailing_half, precision=lax.Precision.HIGHEST)
    grad_flat = ckey_grad.reshape(seq_len, feat_width)
    padded_grad = jnp.concatenate([grad_flat, jnp.zeros((tap_count - 1, feat_width), jnp.float32)], 0)
    key_grad = jnp.zeros((seq_len, feat_width), jnp.float32)
    for tap_index in range(tap_count):
        key_grad = key_grad + conv_weight[tap_index] * padded_grad[tap_index:tap_index + seq_len]
    input_grad = query_grad.reshape(seq_len, feat_width) + key_grad + value_grad.reshape(seq_len, feat_width)
    return (layer_output, input_grad.astype(jnp.bfloat16))

def send_back(section_grad):
    return jnp.concatenate([section_grad[1:], jnp.zeros_like(section_grad[:1])], 0)

def reference(queries, key_input, values, log_decay, conv_weight, out_grad):
    layer_output, input_grad = lax.map(one_section, (queries, key_input, values, log_decay, conv_weight, out_grad))
    return (layer_output, send_back(input_grad))
```

```python
import jax
import jax.numpy as jnp
from jax import lax
from jax.experimental import pallas as pl
from jax.experimental.pallas import tpu as pltpu
from jax.sharding import PartitionSpec as P

F32 = jnp.float32
BF16 = jnp.bfloat16
PAIR = 2
EDGE = 16


def call(kernel, outs, *args, scratch=(), flops=0):
    vmem = pl.BlockSpec(memory_space=pltpu.VMEM)
    moved = sum(a.size * a.dtype.itemsize for a in args) + sum(
        s.size * s.dtype.itemsize for s in outs
    )
    return pl.pallas_call(
        kernel,
        out_shape=outs,
        in_specs=[vmem] * len(args),
        out_specs=[vmem] * len(outs),
        scratch_shapes=scratch,
        compiler_params=pltpu.CompilerParams(vmem_limit_bytes=32 * 1024 * 1024),
        cost_estimate=pl.CostEstimate(flops=flops, bytes_accessed=moved, transcendentals=0),
    )(*args)


def shape(dims, dtype):
    return jax.ShapeDtypeStruct(dims, dtype)


def halves(size):
    mine = lax.rem(lax.axis_index("ctx"), PAIR)
    return (
        pl.ds(pl.multiple_of(mine * size, size), size),
        pl.ds(pl.multiple_of((1 - mine) * size, size), size),
    )


def dot(a, b, contract):
    return lax.dot_general(a, b, ((contract[:1], contract[1:]), ((), ())), preferred_element_type=F32)


def split3(x):
    hi = x.astype(BF16)
    rest = x - hi.astype(F32)
    mid = rest.astype(BF16)
    return hi, mid, (rest - mid.astype(F32)).astype(BF16)


def decay_rows(log_decay, mine, heads):
    rows = log_decay[0].T
    return jnp.where(mine == 0, rows[:heads], rows[heads:])


def pack_kernel(q, k, v, g, log_decay, out):
    rows, heads = q.shape[1], log_decay.shape[2] // PAIR
    width = q.shape[2] // PAIR
    _, other = halves(width)
    for i, ref in enumerate((k, v, q, g)):
        out[i * rows : (i + 1) * rows, :] = ref[0, :, other]
    mine = lax.rem(lax.axis_index("ctx"), PAIR)
    decay = decay_rows(log_decay, 1 - mine, heads)
    parts = [
        jnp.concatenate([part[h : h + 1] for h in range(heads)], 1).astype(F32)
        for part in split3(decay)
    ]
    parts.append(jnp.zeros((EDGE - 3, heads * rows), F32))
    out[4 * rows :, :] = jnp.concatenate(parts, 0).astype(BF16)


def join_kernel(
    got, edge, q, k, v, g, log_decay, taps, q2, kc2, v2, g2, cum, state, padded, decays
):
    rows, heads = q.shape[1], log_decay.shape[2] // PAIR
    width = q.shape[2] // PAIR
    dim = width // heads
    own, _ = halves(width)
    here, there = halves(rows)
    mine = lax.rem(lax.axis_index("ctx"), PAIR)
    for i, (ref, out) in enumerate(((v, v2), (q, q2), (g, g2))):
        out[here, :] = ref[0, :, own]
        out[there, :] = got[(i + 1) * rows : (i + 2) * rows, :]
    padded[:EDGE, :] = edge[...].astype(F32)
    start = pl.multiple_of(EDGE + mine * rows, EDGE)
    padded[pl.ds(start, rows), :] = k[0, :, own].astype(F32)
    start = pl.multiple_of(EDGE + (1 - mine) * rows, EDGE)
    padded[pl.ds(start, rows), :] = got[:rows, :].astype(F32)
    total = jnp.zeros((PAIR * rows, width), F32)
    for j in range(taps.shape[1]):
        total = total + taps[0, j : j + 1, own] * padded[EDGE - j : EDGE - j + PAIR * rows, :]
    kc2[...] = total.astype(BF16)

    decays[...] = jnp.zeros_like(decays)
    coded = got[4 * rows :, :].astype(F32)
    row = coded[0:1] + coded[1:2] + coded[2:3]
    decays[:heads, here] = decay_rows(log_decay, mine, heads)
    decays[:heads, there] = jnp.concatenate(
        [row[:, h * rows : (h + 1) * rows] for h in range(heads)], 0
    )
    size = PAIR * rows
    upto = lax.broadcasted_iota(jnp.int32, (size, size), 0) <= lax.broadcasted_iota(
        jnp.int32, (size, size), 1
    )
    upto = upto.astype(F32).astype(BF16)
    cum_rows = sum(dot(part, upto, (1, 0)) for part in split3(decays[...]))
    cum[...] = cum_rows
    cols = cum_rows.T
    after = jnp.exp(cols[size - 1 :, :] - cols)
    for h in range(heads):
        lanes = slice(h * dim, (h + 1) * dim)
        scaled = (kc2[:, lanes].astype(F32) * after[:, h : h + 1]).astype(BF16)
        state[lanes, :] = dot(scaled, v2[:, lanes], (0, 0)).astype(BF16)


def mixing_of(cum_rows, cols, h, size):
    differ = cols[:, h : h + 1] - cum_rows[h : h + 1, :]
    causal = lax.broadcasted_iota(jnp.int32, (size, size), 0) >= lax.broadcasted_iota(
        jnp.int32, (size, size), 1
    )
    return jnp.where(causal, jnp.exp(jnp.where(causal, differ, 0.0)), 0.0)


def local_kernel(q2, kc2, v2, cum, weights, inside):
    size, width = q2.shape
    heads, dim = weights.shape[0], width // weights.shape[0]
    cum_rows = cum[...]
    cols = cum_rows.T
    for h in range(heads):
        lanes = slice(h * dim, (h + 1) * dim)
        scores = dot(q2[:, lanes], kc2[:, lanes], (1, 1))
        w = (scores * mixing_of(cum_rows, cols, h, size)).astype(BF16)
        weights[h] = w
        inside[:, lanes] = dot(w, v2[:, lanes], (1, 0))


def attend_kernel(inside, q2, g2, cum, before, attended, sums):
    size, width = q2.shape
    dim = before.shape[1]
    heads = width // dim
    growth = jnp.exp(cum[...].T)
    squares = jnp.zeros((size, dim), F32)
    products = jnp.zeros((size, dim), F32)
    for h in range(heads):
        lanes = slice(h * dim, (h + 1) * dim)
        a = inside[:, lanes] + growth[:, h : h + 1] * dot(q2[:, lanes], before[lanes, :], (1, 0))
        attended[:, lanes] = a
        squares = squares + a * a
        products = products + a * g2[:, lanes].astype(F32)
    ones = jnp.ones((8, dim), F32)
    line = [
        lax.dot_general(
            ones, x, (((1,), (1,)), ((), ())), precision=lax.Precision.HIGHEST,
            preferred_element_type=F32,
        )[:1]
        for x in (squares, products)
    ]
    sums[...] = jnp.concatenate(line, 0)


def grad_kernel(width_all, n_sums, attended, q2, g2, cum, *refs):
    sums = refs[:n_sums]
    keep, send, grad, adjoint, normed = refs[n_sums:]
    size, width = q2.shape
    dim = adjoint.shape[1]
    heads = width // dim
    total = sum(ref[...] for ref in sums[1:]) + sums[0][...]
    inverse = 1.0 / jnp.sqrt(total[0:1] / width_all + 1e-06)
    shift = total[1:2] / width_all * inverse
    both = jnp.concatenate([inverse, shift, jnp.zeros((6, size), F32)], 0).T
    inverse, shift = both[:, 0:1], both[:, 1:2]
    growth = jnp.exp(cum[...].T)
    for h in range(heads):
        lanes = slice(h * dim, (h + 1) * dim)
        n = attended[:, lanes] * inverse
        normed[:, lanes] = n.astype(BF16)
        d = ((g2[:, lanes].astype(F32) - n * shift) * inverse).astype(BF16)
        grad[:, lanes] = d
        scaled = (q2[:, lanes].astype(F32) * growth[:, h : h + 1]).astype(BF16)
        adjoint[lanes, :] = dot(scaled, d, (0, 0)).astype(BF16)
    here, there = halves(size // PAIR)
    keep[...] = normed[here, :]
    send[...] = normed[there, :]


def inner_grad_kernel(q2, kc2, v2, grad, weights, cum, before, partial, key_grad, first):
    size, width = q2.shape
    dim = before.shape[1]
    heads = width // dim
    cum_rows = cum[...]
    cols = cum_rows.T
    growth = jnp.exp(cols)
    for h in range(heads):
        lanes = slice(h * dim, (h + 1) * dim)
        d = grad[:, lanes]
        scores = dot(d, v2[:, lanes], (1, 1)) * mixing_of(cum_rows, cols, h, size)
        scores = scores.astype(BF16)
        query_grad = dot(scores, kc2[:, lanes], (1, 0)) + growth[:, h : h + 1] * dot(
            d, before[lanes, :], (1, 1)
        )
        key_grad[:, lanes] = dot(scores, q2[:, lanes], (0, 0))
        partial[:, lanes] = query_grad + dot(weights[h], d, (0, 0))
    first[...] = key_grad[: first.shape[0], :]


def outer_grad_kernel(partial, key_grad, follow, kc2, v2, cum, behind, taps, keep, send, padded, done):
    size, width = partial.shape
    dim = behind.shape[1]
    heads = width // dim
    own, _ = halves(width)
    cols = cum[...].T
    after = jnp.exp(cols[size - 1 :, :] - cols)
    padded[size:, :] = follow[...]
    for h in range(heads):
        lanes = slice(h * dim, (h + 1) * dim)
        scale = after[:, h : h + 1]
        padded[:size, lanes] = key_grad[:, lanes] + scale * dot(
            v2[:, lanes], behind[lanes, :], (1, 1)
        )
        done[:, lanes] = partial[:, lanes] + scale * dot(kc2[:, lanes], behind[lanes, :], (1, 0))
    total = done[...]
    for j in range(taps.shape[1]):
        total = total + taps[0, j : j + 1, own] * padded[j : j + size, :]
    done[...] = total
    here, there = halves(size // PAIR)
    keep[...] = done[here, :].astype(BF16)
    send[...] = done[there, :].astype(BF16)


def place_kernel(kept, got, out):
    width = kept.shape[1]
    own, other = halves(width)
    out[0, :, own] = kept[...]
    out[0, :, other] = got[...]


def shifted(block, axis, distance):
    devices = range(lax.axis_size(axis))
    return lax.ppermute(block, axis, [(i - distance, i) for i in devices if i - distance in devices])


def swapped(block):
    return lax.ppermute(block, "ctx", [(i, i ^ 1) for i in range(lax.axis_size("ctx"))])


def to_earlier_section(block, flip):
    blocks, sections = lax.axis_size("ctx"), lax.axis_size("pp")
    route = [
        (c * sections + p, (c ^ flip) * sections + p - 1)
        for c in range(blocks)
        for p in range(1, sections)
    ]
    return lax.ppermute(block, ("ctx", "pp"), route)


def summed_parts(part):
    count = lax.axis_size("tp")
    pair = part + lax.ppermute(part, "tp", [(i, i ^ 1) for i in range(count)])
    parts = [pair]
    for k in range(2, count, 2):
        parts.append(lax.ppermute(pair, "tp", [(i, i ^ k) for i in range(count)]))
    total = sum(parts[1:]) + parts[0]
    return [total, swapped(total)]


def per_device(queries, key_input, values, log_decay, conv_weight, out_grad):
    rows, width = queries.shape[1], queries.shape[2] // PAIR
    heads = log_decay.shape[2] // PAIR
    dim = width // heads
    size = PAIR * rows
    supers = lax.axis_size("ctx") // PAIR
    width_all = queries.shape[2] * lax.axis_size("tp")
    ctx = lax.axis_size("ctx")

    edge = key_input[0, rows - EDGE :]
    near = lax.ppermute(edge[:, :width], "ctx", [(i, i + 1) for i in range(1, ctx - 1, 2)])
    far = lax.ppermute(edge[:, width:], "ctx", [(i, i + 2) for i in range(1, ctx - 2, 2)])
    edge = near + far

    bundle = call(
        pack_kernel,
        [shape((4 * rows + EDGE, width), BF16)],
        queries, key_input, values, out_grad, log_decay,
    )[0]
    got = swapped(bundle)
    q2, kc2, v2, g2, cum, state = call(
        join_kernel,
        [shape((size, width), BF16)] * 4 + [shape((8, size), F32), shape((width, dim), BF16)],
        got, edge, queries, key_input, values, out_grad, log_decay, conv_weight,
        scratch=[pltpu.VMEM((EDGE + size, width), F32), pltpu.VMEM((8, size), F32)],
    )
    carry = jnp.repeat(jnp.exp(cum[:heads, -1]), dim)[:, None]
    before = shifted(state, "ctx", PAIR)
    for _ in range(supers - 2):
        joined = state.astype(F32) + carry * before.astype(F32)
        before = shifted(joined.astype(BF16), "ctx", PAIR)

    weights, inside = call(
        local_kernel,
        [shape((heads, size, size), BF16), shape((size, width), F32)],
        q2, kc2, v2, cum,
        flops=4 * heads * size * size * dim,
    )
    attended, sums = call(
        attend_kernel,
        [shape((size, width), F32), shape((2, size), F32)],
        inside, q2, g2, cum, before,
    )
    parts = summed_parts(sums)
    keep, send, grad, adjoint = call(
        lambda *refs: grad_kernel(width_all, len(parts), *refs),
        [shape((rows, width), BF16)] * 2 + [shape((size, width), BF16), shape((width, dim), BF16)],
        attended, q2, g2, cum, *parts,
        scratch=[pltpu.VMEM((size, width), BF16)],
    )
    behind = shifted(adjoint, "ctx", -PAIR)
    for _ in range(supers - 2):
        joined = adjoint.astype(F32) + carry * behind.astype(F32)
        behind = shifted(joined.astype(BF16), "ctx", -PAIR)

    partial, key_grad, first = call(
        inner_grad_kernel,
        [shape((size, width), F32)] * 2 + [shape((8, width), F32)],
        q2, kc2, v2, grad, weights, cum, before,
        flops=10 * heads * size * size * dim,
    )
    if supers > 2:
        after = jnp.exp(cum[:heads, -1:] - cum[:heads, :8])
        state_part = jnp.einsum(
            "shv,hkv->shk",
            v2[:8].reshape(8, heads, dim),
            behind.reshape(heads, dim, dim),
            preferred_element_type=F32,
        )
        first = first + (after.T[:, :, None] * state_part).reshape(8, width)
    follow = shifted(first, "ctx", -PAIR)
    layer_output = call(
        place_kernel, [shape((1, rows, PAIR * width), BF16)], keep, swapped(send)
    )[0]
    keep, send = call(
        outer_grad_kernel,
        [shape((rows, width), BF16)] * 2,
        partial, key_grad, follow, kc2, v2, cum, behind, conv_weight,
        scratch=[pltpu.VMEM((size + 8, width), F32), pltpu.VMEM((size, width), F32)],
    )
    input_next = call(
        place_kernel,
        [shape((1, rows, PAIR * width), BF16)],
        to_earlier_section(keep, 0), to_earlier_section(send, 1),
    )[0]
    return (layer_output, input_next)


def solution(mesh):
    placed = (
        P("pp", "ctx", "tp"),
        P("pp", "ctx", "tp"),
        P("pp", "ctx", "tp"),
        P("pp", "ctx", "tp"),
        P("pp", None, "tp"),
        P("pp", "ctx", "tp"),
    )
    return jax.shard_map(
        per_device,
        mesh=mesh,
        in_specs=placed,
        out_specs=(P("pp", "ctx", "tp"), P("pp", "ctx", "tp")),
        check_vma=False,
    )
```

```python
import jax
import jax.numpy as jnp
from jax import lax
from jax.experimental import pallas as pl
from jax.experimental.pallas import tpu as pltpu
from jax.sharding import PartitionSpec as P

F32 = jnp.float32
BF16 = jnp.bfloat16
PAIR = 2
EDGE = 16


def call(kernel, outs, *args, scratch=(), flops=0, hbm=(), out_hbm=False):
    vmem = pl.BlockSpec(memory_space=pltpu.VMEM)
    moved = sum(a.size * a.dtype.itemsize for a in args) + sum(
        s.size * s.dtype.itemsize for s in outs
    )
    return pl.pallas_call(
        kernel,
        out_shape=outs,
        in_specs=[
            pl.BlockSpec(memory_space=pltpu.HBM) if i in hbm else vmem for i in range(len(args))
        ],
        out_specs=[pl.BlockSpec(memory_space=pltpu.HBM) if out_hbm else vmem] * len(outs),
        scratch_shapes=scratch,
        compiler_params=pltpu.CompilerParams(vmem_limit_bytes=32 * 1024 * 1024),
        cost_estimate=pl.CostEstimate(flops=flops, bytes_accessed=moved, transcendentals=0),
    )(*args)


def shape(dims, dtype):
    return jax.ShapeDtypeStruct(dims, dtype)


def halves(size):
    mine = lax.rem(lax.axis_index("ctx"), PAIR)
    return (
        pl.ds(pl.multiple_of(mine * size, size), size),
        pl.ds(pl.multiple_of((1 - mine) * size, size), size),
    )


def dot(a, b, contract):
    return lax.dot_general(a, b, ((contract[:1], contract[1:]), ((), ())), preferred_element_type=F32)


def split3(x):
    hi = x.astype(BF16)
    rest = x - hi.astype(F32)
    mid = rest.astype(BF16)
    return hi, mid, (rest - mid.astype(F32)).astype(BF16)


def decay_rows(log_decay, mine, heads):
    rows = log_decay[0]
    return jnp.where(mine == 0, rows[:heads], rows[heads:])


def copy_all(pairs, sems):
    copies = [pltpu.make_async_copy(src, to, sems.at[i]) for i, (src, to) in enumerate(pairs)]
    for copy in copies:
        copy.start()
    return copies


def pack_kernel(k, v, log_decay, first, sems):
    rows, heads = k.shape[1], log_decay.shape[1] // PAIR
    _, other = halves(k.shape[2] // PAIR)
    copies = copy_all(
        [(ref.at[0, :, other], first.at[i * rows : (i + 1) * rows, :]) for i, ref in enumerate((k, v))],
        sems,
    )
    mine = lax.rem(lax.axis_index("ctx"), PAIR)
    decay = decay_rows(log_decay, 1 - mine, heads)
    parts = [
        jnp.concatenate([part[h : h + 1] for h in range(heads)], 1).astype(F32)
        for part in split3(decay)
    ]
    parts.append(jnp.zeros((EDGE - 3, heads * rows), F32))
    first[2 * rows :, :] = jnp.concatenate(parts, 0).astype(BF16)
    for copy in copies:
        copy.wait()


def pack_more_kernel(q, k, v, g, _, second, own, sems):
    rows = q.shape[1]
    lanes_own, other = halves(q.shape[2] // PAIR)
    pairs = [
        (ref.at[0, :, other], second.at[i * rows : (i + 1) * rows, :]) for i, ref in enumerate((q, g))
    ]
    pairs += [
        (ref.at[0, :, lanes_own], own.at[i * rows : (i + 1) * rows, :])
        for i, ref in enumerate((k, v, q, g))
    ]
    for copy in copy_all(pairs, sems):
        copy.wait()


def join_kernel(got, near, far, own, log_decay, taps, kc2, v2, cum, state, padded, decays):
    rows, heads = log_decay.shape[2], log_decay.shape[1] // PAIR
    width = own.shape[1]
    dim = width // heads
    size = PAIR * rows
    lanes_own, _ = halves(width)
    here, there = halves(rows)
    mine = lax.rem(lax.axis_index("ctx"), PAIR)
    v2[here, :] = own[rows : 2 * rows, :]
    v2[there, :] = got[rows : 2 * rows, :]
    edge = jnp.where(mine == 0, near[...].astype(F32), far[...].astype(F32))
    padded[:EDGE, :] = jnp.where(lax.axis_index("ctx") < PAIR, 0.0, edge)
    start = pl.multiple_of(EDGE + mine * rows, EDGE)
    padded[pl.ds(start, rows), :] = own[:rows, :].astype(F32)
    start = pl.multiple_of(EDGE + (1 - mine) * rows, EDGE)
    padded[pl.ds(start, rows), :] = got[:rows, :].astype(F32)
    total = jnp.zeros((size, width), F32)
    for j in range(taps.shape[1]):
        total = total + taps[0, j : j + 1, lanes_own] * padded[EDGE - j : EDGE - j + size, :]
    kc2[...] = total.astype(BF16)

    decays[...] = jnp.zeros_like(decays)
    coded = got[2 * rows :, :].astype(F32)
    row = coded[0:1] + coded[1:2] + coded[2:3]
    decays[:heads, here] = decay_rows(log_decay, mine, heads)
    decays[:heads, there] = jnp.concatenate(
        [row[:, h * rows : (h + 1) * rows] for h in range(heads)], 0
    )
    upto = lax.broadcasted_iota(jnp.int32, (size, size), 0) <= lax.broadcasted_iota(
        jnp.int32, (size, size), 1
    )
    upto = upto.astype(F32).astype(BF16)
    cum_rows = sum(dot(part, upto, (1, 0)) for part in split3(decays[...]))
    cum[...] = cum_rows
    cols = cum_rows.T
    after = jnp.exp(cols[size - 1 :, :] - cols)
    for h in range(heads):
        lanes = slice(h * dim, (h + 1) * dim)
        scaled = (kc2[:, lanes].astype(F32) * after[:, h : h + 1]).astype(BF16)
        state[lanes, :] = dot(scaled, v2[:, lanes], (0, 0)).astype(BF16)


def mixing_of(cum_rows, cols, h, size):
    differ = cols[:, h : h + 1] - cum_rows[h : h + 1, :]
    causal = lax.broadcasted_iota(jnp.int32, (size, size), 0) >= lax.broadcasted_iota(
        jnp.int32, (size, size), 1
    )
    return jnp.where(causal, jnp.exp(jnp.where(causal, differ, 0.0)), 0.0)


def local_kernel(got, own, kc2, v2, cum, q2, g2, weights, inside):
    size, width = q2.shape
    heads, dim = weights.shape[0], width // weights.shape[0]
    rows = size // PAIR
    here, there = halves(rows)
    q2[here, :] = own[2 * rows : 3 * rows, :]
    q2[there, :] = got[:rows, :]
    g2[here, :] = own[3 * rows :, :]
    g2[there, :] = got[rows:, :]
    cum_rows = cum[...]
    cols = cum_rows.T
    for h in range(heads):
        lanes = slice(h * dim, (h + 1) * dim)
        scores = dot(q2[:, lanes], kc2[:, lanes], (1, 1))
        w = (scores * mixing_of(cum_rows, cols, h, size)).astype(BF16)
        weights[h] = w
        inside[:, lanes] = dot(w, v2[:, lanes], (1, 0))


def unless(flag, block):
    return jnp.where(flag, jnp.zeros_like(block), block)


def attend_kernel(inside, q2, g2, cum, before, attended, sums):
    size, width = q2.shape
    dim = before.shape[1]
    heads = width // dim
    start = lax.axis_index("ctx") < PAIR
    growth = jnp.exp(cum[...].T)
    squares = jnp.zeros((size, dim), F32)
    products = jnp.zeros((size, dim), F32)
    for h in range(heads):
        lanes = slice(h * dim, (h + 1) * dim)
        carried = dot(q2[:, lanes], unless(start, before[lanes, :]), (1, 0))
        a = inside[:, lanes] + growth[:, h : h + 1] * carried
        attended[:, lanes] = a
        squares = squares + a * a
        products = products + a * g2[:, lanes].astype(F32)
    ones = jnp.ones((8, dim), F32)
    line = [
        lax.dot_general(
            ones, x, (((1,), (1,)), ((), ())), precision=lax.Precision.HIGHEST,
            preferred_element_type=F32,
        )[:1]
        for x in (squares, products)
    ]
    sums[...] = jnp.concatenate(line, 0)


def grad_kernel(width_all, attended, q2, v2, g2, cum, *refs):
    *sums, scales, grad, adjoint = refs
    size, width = q2.shape
    dim = adjoint.shape[1]
    heads = width // dim
    total = sum(ref[...] for ref in sums[1:]) + sums[0][...]
    inverse = 1.0 / jnp.sqrt(total[0:1] / width_all + 1e-06)
    shift = total[1:2] / width_all * inverse
    both = jnp.concatenate([inverse, shift, jnp.zeros((6, size), F32)], 0)
    scales[...] = both
    both = both.T
    inverse, shift = both[:, 0:1], both[:, 1:2]
    cum_rows = cum[...]
    cols = cum_rows.T
    growth = jnp.exp(cols)
    causal = lax.broadcasted_iota(jnp.int32, (EDGE, size), 0) <= lax.broadcasted_iota(
        jnp.int32, (EDGE, size), 1
    )
    heads_rows = []
    for h in range(heads):
        lanes = slice(h * dim, (h + 1) * dim)
        n = attended[:, lanes] * inverse
        d = ((g2[:, lanes].astype(F32) - n * shift) * inverse).astype(BF16)
        grad[:, lanes] = d
        scaled = (q2[:, lanes].astype(F32) * growth[:, h : h + 1]).astype(BF16)
        adjoint[lanes, :] = dot(scaled, d, (0, 0)).astype(BF16)
        differ = cum_rows[h : h + 1, :] - cols[:EDGE, h : h + 1]
        mixing = jnp.where(causal, jnp.exp(jnp.where(causal, differ, 0.0)), 0.0)
        scores = (dot(v2[:EDGE, lanes], d, (1, 1)) * mixing).astype(BF16)
        top = dot(scores, q2[:, lanes], (1, 0))
        heads_rows.append(top[:8])
    adjoint[width:, :] = jnp.concatenate([top[:4] for top in heads_rows], 0).astype(BF16)


def inner_grad_kernel(
    attended, scales, q2, kc2, v2, grad, weights, cum, before,
    keep, send, partial, key_grad, normed,
):
    size, width = q2.shape
    dim = before.shape[1]
    heads = width // dim
    start = lax.axis_index("ctx") < PAIR
    inverse = scales[...].T[:, 0:1]
    cum_rows = cum[...]
    cols = cum_rows.T
    growth = jnp.exp(cols)
    for h in range(heads):
        lanes = slice(h * dim, (h + 1) * dim)
        normed[:, lanes] = (attended[:, lanes] * inverse).astype(BF16)
        d = grad[:, lanes]
        scores = dot(d, v2[:, lanes], (1, 1)) * mixing_of(cum_rows, cols, h, size)
        scores = scores.astype(BF16)
        query_grad = dot(scores, kc2[:, lanes], (1, 0)) + growth[:, h : h + 1] * dot(
            d, unless(start, before[lanes, :]), (1, 1)
        )
        key_grad[:, lanes] = dot(scores, q2[:, lanes], (0, 0))
        partial[:, lanes] = query_grad + dot(weights[h], d, (0, 0))
    here, there = halves(size // PAIR)
    keep[...] = normed[here, :]
    send[...] = normed[there, :]


def outer_grad_kernel(
    last, partial, key_grad, kc2, v2, cum, behind, more, taps, keep, send, padded, done
):
    size, width = partial.shape
    dim = behind.shape[1]
    heads = width // dim
    own, _ = halves(width)
    ends = lax.axis_index("ctx") >= last
    tops = behind[width:, :].astype(F32)
    cols = cum[...].T
    after = jnp.exp(cols[size - 1 :, :] - cols)
    for h in range(heads):
        lanes = slice(h * dim, (h + 1) * dim)
        scale = after[:, h : h + 1]
        state = unless(ends, behind[lanes, :])
        padded[:size, lanes] = key_grad[:, lanes] + scale * dot(v2[:, lanes], state, (1, 1))
        done[:, lanes] = partial[:, lanes] + scale * dot(kc2[:, lanes], state, (1, 0))
        top = jnp.concatenate([tops[4 * h : 4 * h + 4], jnp.zeros((4, dim), F32)], 0)
        padded[size:, lanes] = unless(ends, top) + more[:, lanes]
    total = done[...]
    for j in range(taps.shape[1]):
        total = total + taps[0, j : j + 1, own] * padded[j : j + size, :]
    done[...] = total
    here, there = halves(size // PAIR)
    first = lax.axis_index("pp") == 0
    keep[...] = unless(first, done[here, :]).astype(BF16)
    send[...] = unless(first, done[there, :]).astype(BF16)


def place_kernel(kept, got, out, sems):
    own, other = halves(kept.shape[1])
    for copy in copy_all([(kept, out.at[0, :, own]), (got, out.at[0, :, other])], sems):
        copy.wait()


def placed(kept, got):
    rows, width = kept.shape
    return call(
        place_kernel,
        [shape((1, rows, PAIR * width), BF16)],
        kept, got,
        scratch=[pltpu.SemaphoreType.DMA((2,))],
        out_hbm=True,
    )[0]


def turned(block, axis, distance):
    count = lax.axis_size(axis)
    return lax.ppermute(block, axis, [(i, (i + distance) % count) for i in range(count)])


def swapped(block):
    return lax.ppermute(block, "ctx", [(i, i ^ 1) for i in range(lax.axis_size("ctx"))])


def to_earlier_section(block, flip):
    blocks, sections = lax.axis_size("ctx"), lax.axis_size("pp")
    route = [
        (c * sections + p, (c ^ flip) * sections + (p - 1) % sections)
        for c in range(blocks)
        for p in range(sections)
    ]
    return lax.ppermute(block, ("ctx", "pp"), route)


def summed_parts(part):
    blocks, count = lax.axis_size("ctx"), lax.axis_size("tp")
    pair = part + lax.ppermute(part, "tp", [(i, i ^ 1) for i in range(count)])
    parts = [pair]
    for flip in range(PAIR):
        for k in range(0, count, 2):
            if flip or k:
                route = [
                    (c * count + t, (c ^ flip) * count + (t + k) % count)
                    for c in range(blocks)
                    for t in range(count)
                ]
                parts.append(lax.ppermute(pair, ("ctx", "tp"), route))
    return parts


def per_device(queries, key_input, values, log_decay, conv_weight, out_grad):
    rows, width = queries.shape[1], queries.shape[2] // PAIR
    heads = log_decay.shape[2] // PAIR
    dim = width // heads
    size = PAIR * rows
    blocks = lax.axis_size("ctx")
    supers = blocks // PAIR
    width_all = queries.shape[2] * lax.axis_size("tp")
    log_decay = jnp.swapaxes(log_decay, 1, 2)
    arrays = (queries, key_input, values, out_grad)
    queries, key_input, values, out_grad = (
        pltpu.with_memory_space_constraint(x, pltpu.HBM) for x in arrays
    )

    first = call(
        pack_kernel,
        [shape((2 * rows + EDGE, width), BF16)],
        key_input, values, log_decay,
        scratch=[pltpu.SemaphoreType.DMA((2,))],
        hbm=range(2),
    )[0]
    got = swapped(first)
    edge = arrays[1][0, rows - EDGE :]
    near = lax.ppermute(edge[:, :width], "ctx", [(i, i + 1) for i in range(1, blocks - 1, 2)])
    far = lax.ppermute(edge[:, width:], "ctx", [(i, i + 2) for i in range(1, blocks - 2, 2)])
    second, own = call(
        pack_more_kernel,
        [shape((2 * rows, width), BF16), shape((4 * rows, width), BF16)],
        queries, key_input, values, out_grad, first[2 * rows :],
        scratch=[pltpu.SemaphoreType.DMA((6,))],
        hbm=range(4),
    )
    got_more = swapped(second)
    kc2, v2, cum, state = call(
        join_kernel,
        [shape((size, width), BF16)] * 2 + [shape((8, size), F32), shape((width, dim), BF16)],
        got, near, far, own, log_decay, conv_weight,
        scratch=[pltpu.VMEM((EDGE + size, width), F32), pltpu.VMEM((8, size), F32)],
    )
    carry = jnp.repeat(jnp.exp(cum[:heads, -1]), dim)[:, None]
    pair_index = lax.axis_index("ctx") // PAIR
    before = turned(state, "ctx", PAIR)
    for _ in range(supers - 2):
        earlier = unless(pair_index == 0, before).astype(F32)
        joined = state.astype(F32) + carry * earlier
        before = turned(joined.astype(BF16), "ctx", PAIR)

    q2, g2, weights, inside = call(
        local_kernel,
        [shape((size, width), BF16)] * 2
        + [shape((heads, size, size), BF16), shape((size, width), F32)],
        got_more, own, kc2, v2, cum,
        flops=4 * heads * size * size * dim,
    )
    attended, sums = call(
        attend_kernel,
        [shape((size, width), F32), shape((2, size), F32)],
        inside, q2, g2, cum, before,
    )
    parts = summed_parts(sums)
    scales, grad, adjoint = call(
        lambda *refs: grad_kernel(width_all, *refs),
        [shape((8, size), F32), shape((size, width), BF16),
         shape((width + 4 * heads, dim), BF16)],
        attended, q2, v2, g2, cum, *parts,
    )
    behind = turned(adjoint, "ctx", -PAIR)
    more = jnp.zeros((8, width), F32)
    for step in range(supers - 2):
        later = unless(pair_index == supers - 1, behind[:width]).astype(F32)
        joined = adjoint[:width].astype(F32) + carry * later
        moved = turned(joined.astype(BF16), "ctx", -PAIR)
        behind = jnp.concatenate([moved, behind[width:]], 0)
    if supers > 2:
        after = jnp.exp(cum[:heads, -1:] - cum[:heads, :8])
        state_part = jnp.einsum(
            "shv,hkv->shk",
            v2[:8].reshape(8, heads, dim),
            unless(pair_index == supers - 1, behind[:width]).reshape(heads, dim, dim),
            preferred_element_type=F32,
        )
        more = turned((after.T[:, :, None] * state_part).reshape(8, width), "ctx", -PAIR)
        more = unless(pair_index == supers - 1, more)

    keep, send, partial, key_grad = call(
        inner_grad_kernel,
        [shape((rows, width), BF16)] * 2 + [shape((size, width), F32)] * 2,
        attended, scales, q2, kc2, v2, grad, weights, cum, before,
        scratch=[pltpu.VMEM((size, width), BF16)],
        flops=10 * heads * size * size * dim,
    )
    layer_output = placed(keep, swapped(send))
    keep, send = call(
        lambda *refs: outer_grad_kernel(blocks - PAIR, *refs),
        [shape((rows, width), BF16)] * 2,
        partial, key_grad, kc2, v2, cum, behind, more, conv_weight,
        scratch=[pltpu.VMEM((size + 8, width), F32), pltpu.VMEM((size, width), F32)],
    )
    input_next = placed(to_earlier_section(keep, 0), to_earlier_section(send, 1))
    return (layer_output, input_next)


def solution(mesh):
    placed = (
        P("pp", "ctx", "tp"),
        P("pp", "ctx", "tp"),
        P("pp", "ctx", "tp"),
        P("pp", "ctx", "tp"),
        P("pp", None, "tp"),
        P("pp", "ctx", "tp"),
    )
    return jax.shard_map(
        per_device,
        mesh=mesh,
        in_specs=placed,
        out_specs=(P("pp", "ctx", "tp"), P("pp", "ctx", "tp")),
        check_vma=False,
    )
```

```python
import jax
import jax.numpy as jnp
from jax import lax
from jax.experimental import pallas as pl
from jax.experimental.pallas import tpu as pltpu
from jax.sharding import PartitionSpec as P

F32 = jnp.float32
BF16 = jnp.bfloat16
PAIR = 2
EDGE = 16
PARTS = 1


def call(kernel, outs, *args, scratch=(), flops=0, hbm=(), out_hbm=False, alias=()):
    vmem = pl.BlockSpec(memory_space=pltpu.VMEM)
    moved = sum(a.size * a.dtype.itemsize for a in args) + sum(
        s.size * s.dtype.itemsize for s in outs
    )
    return pl.pallas_call(
        kernel,
        out_shape=outs,
        in_specs=[
            pl.BlockSpec(memory_space=pltpu.HBM) if i in hbm else vmem for i in range(len(args))
        ],
        out_specs=[pl.BlockSpec(memory_space=pltpu.HBM) if out_hbm else vmem] * len(outs),
        scratch_shapes=scratch,
        input_output_aliases=dict(alias),
        compiler_params=pltpu.CompilerParams(vmem_limit_bytes=32 * 1024 * 1024),
        cost_estimate=pl.CostEstimate(flops=flops, bytes_accessed=moved, transcendentals=0),
    )(*args)


def shape(dims, dtype):
    return jax.ShapeDtypeStruct(dims, dtype)


def halves(size):
    mine = lax.rem(lax.axis_index("ctx"), PAIR)
    return (
        pl.ds(pl.multiple_of(mine * size, size), size),
        pl.ds(pl.multiple_of((1 - mine) * size, size), size),
    )


def dot(a, b, contract):
    return lax.dot_general(a, b, ((contract[:1], contract[1:]), ((), ())), preferred_element_type=F32)


def split3(x):
    hi = x.astype(BF16)
    rest = x - hi.astype(F32)
    mid = rest.astype(BF16)
    return hi, mid, (rest - mid.astype(F32)).astype(BF16)


def decay_rows(log_decay, mine, heads):
    rows = log_decay[0]
    return jnp.where(mine == 0, rows[:heads], rows[heads:])


def copy_all(pairs, sems):
    copies = [pltpu.make_async_copy(src, to, sems.at[i]) for i, (src, to) in enumerate(pairs)]
    for copy in copies:
        copy.start()
    return copies


def pack_kernel(k, v, log_decay, first, decays, sems):
    rows, heads = k.shape[1], log_decay.shape[1] // PAIR
    _, other = halves(k.shape[2] // PAIR)
    copies = copy_all(
        [(log_decay, decays)]
        + [(ref.at[0, :, other], first.at[i * rows : (i + 1) * rows, :]) for i, ref in enumerate((k, v))],
        sems,
    )
    copies[0].wait()
    mine = lax.rem(lax.axis_index("ctx"), PAIR)
    decay = decay_rows(decays, 1 - mine, heads)
    parts = [
        jnp.concatenate([part[h : h + 1] for h in range(heads)], 1).astype(F32)
        for part in split3(decay)
    ]
    parts.append(jnp.zeros((EDGE - 3, heads * rows), F32))
    first[2 * rows :, :] = jnp.concatenate(parts, 0).astype(BF16)
    for copy in copies[1:]:
        copy.wait()


def pack_more_kernel(q, k, v, g, _, second, own, sems):
    rows = q.shape[1]
    lanes_own, other = halves(q.shape[2] // PAIR)
    pairs = [
        (ref.at[0, :, other], second.at[i * rows : (i + 1) * rows, :]) for i, ref in enumerate((q, g))
    ]
    pairs += [
        (ref.at[0, :, lanes_own], own.at[i * rows : (i + 1) * rows, :])
        for i, ref in enumerate((k, v, q, g))
    ]
    for copy in copy_all(pairs, sems):
        copy.wait()


def join_kernel(got, own, log_decay, taps, *refs):
    *edges, kc2, v2, cum, state, top, padded, decays = refs
    rows, heads = log_decay.shape[2], log_decay.shape[1] // PAIR
    width = own.shape[1]
    dim = width // heads
    size = PAIR * rows
    lanes_own, _ = halves(width)
    here, there = halves(rows)
    mine = lax.rem(lax.axis_index("ctx"), PAIR)
    v2[here, :] = own[rows : 2 * rows, :]
    v2[there, :] = got[rows : 2 * rows, :]
    padded[:EDGE, :] = edges[0][...].astype(F32) if edges else jnp.zeros((EDGE, width), F32)
    start = pl.multiple_of(EDGE + mine * rows, EDGE)
    padded[pl.ds(start, rows), :] = own[:rows, :].astype(F32)
    start = pl.multiple_of(EDGE + (1 - mine) * rows, EDGE)
    padded[pl.ds(start, rows), :] = got[:rows, :].astype(F32)
    total = jnp.zeros((size, width), F32)
    for j in range(taps.shape[1]):
        total = total + taps[0, j : j + 1, lanes_own] * padded[EDGE - j : EDGE - j + size, :]
    kc2[...] = total.astype(BF16)
    top[...] = total[:EDGE]

    decays[...] = jnp.zeros_like(decays)
    coded = got[2 * rows :, :].astype(F32)
    row = coded[0:1] + coded[1:2] + coded[2:3]
    decays[:heads, here] = decay_rows(log_decay, mine, heads)
    decays[:heads, there] = jnp.concatenate(
        [row[:, h * rows : (h + 1) * rows] for h in range(heads)], 0
    )
    upto = lax.broadcasted_iota(jnp.int32, (size, size), 0) <= lax.broadcasted_iota(
        jnp.int32, (size, size), 1
    )
    upto = upto.astype(F32).astype(BF16)
    cum_rows = sum(dot(part, upto, (1, 0)) for part in split3(decays[...]))
    cum[...] = cum_rows
    cols = cum_rows.T
    after = jnp.exp(cols[size - 1 :, :] - cols)
    for h in range(heads):
        lanes = slice(h * dim, (h + 1) * dim)
        scaled = (kc2[:, lanes].astype(F32) * after[:, h : h + 1]).astype(BF16)
        state[lanes, :] = dot(scaled, v2[:, lanes], (0, 0)).astype(BF16)
    last = padded[EDGE + size - 4 : EDGE + size, :]
    state[width:, :] = jnp.concatenate(
        [last[:, h * dim : (h + 1) * dim] for h in range(heads)], 0
    ).astype(BF16)


def mixing_of(cum_rows, cols, h, first=0, last=None):
    differ = cols[:, h : h + 1] - cum_rows[h : h + 1, :last]
    at = lax.broadcasted_iota(jnp.int32, differ.shape, 1)
    causal = (lax.broadcasted_iota(jnp.int32, differ.shape, 0) >= at) & (at >= first)
    return jnp.where(causal, jnp.exp(jnp.where(causal, differ, 0.0)), 0.0)


def local_kernel(got, own, kc2, v2, cum, q2, g2, weights, inside):
    size, width = q2.shape
    heads, dim = weights.shape[0], width // weights.shape[0]
    rows = size // PAIR
    here, there = halves(rows)
    q2[here, :] = own[2 * rows : 3 * rows, :]
    q2[there, :] = got[:rows, :]
    g2[here, :] = own[3 * rows :, :]
    g2[there, :] = got[rows:, :]
    cum_rows = cum[...]
    cols = cum_rows.T
    for h in range(heads):
        lanes = slice(h * dim, (h + 1) * dim)
        scores = dot(q2[:, lanes], kc2[:, lanes], (1, 1))
        w = (scores * mixing_of(cum_rows, cols, h, EDGE)).astype(BF16)
        weights[h] = w
        inside[:, lanes] = dot(w, v2[:, lanes], (1, 0))


def unless(flag, block):
    return jnp.where(flag, jnp.zeros_like(block), block)


def attend_kernel(
    kc2, weights, inside, q2, g2, v2, cum, before, top, taps,
    kc2_whole, weights_whole, attended, sums, lead,
):
    size, width = q2.shape
    dim = before.shape[1]
    heads = width // dim
    start = lax.axis_index("ctx") < PAIR
    own, _ = halves(width)
    cum_rows = cum[...]
    cols = cum_rows.T
    growth = jnp.exp(cols)
    tail = unless(start, before[width:, :].astype(F32))
    lead[...] = jnp.zeros_like(lead)
    for h in range(heads):
        lead[4:8, h * dim : (h + 1) * dim] = tail[4 * h : 4 * h + 4]
    fixed = top[:8, :]
    for j in range(1, taps.shape[1]):
        fixed = fixed + taps[0, j : j + 1, own] * lead[8 - j : 16 - j, :]
    fixed = jnp.concatenate([fixed, top[8:, :]], 0).astype(BF16)
    kc2_whole[:EDGE, :] = fixed
    squares = jnp.zeros((size, dim), F32)
    products = jnp.zeros((size, dim), F32)
    for h in range(heads):
        lanes = slice(h * dim, (h + 1) * dim)
        carried = dot(q2[:, lanes], unless(start, before[lanes, :]), (1, 0))
        scores = dot(q2[:, lanes], fixed[:, lanes], (1, 1))
        w = (scores * mixing_of(cum_rows, cols, h, 0, EDGE)).astype(BF16)
        weights_whole[h, :, :EDGE] = w
        a = inside[:, lanes] + dot(w, v2[:EDGE, lanes], (1, 0)) + growth[:, h : h + 1] * carried
        attended[:, lanes] = a
        squares = squares + a * a
        products = products + a * g2[:, lanes].astype(F32)
    ones = jnp.ones((8, dim), F32)
    line = [
        lax.dot_general(
            ones, x, (((1,), (1,)), ((), ())), precision=lax.Precision.HIGHEST,
            preferred_element_type=F32,
        )[:1]
        for x in (squares, products)
    ]
    sums[...] = jnp.concatenate(line, 0)


def grad_kernel(width_all, attended, q2, v2, g2, cum, *refs):
    *sums, scales, grad = refs[:-PARTS]
    adjoints = refs[-PARTS:]
    size, width = q2.shape
    dim = adjoints[0].shape[1]
    heads = width // dim
    total = sum(ref[...] for ref in sums[1:]) + sums[0][...]
    inverse = 1.0 / jnp.sqrt(total[0:1] / width_all + 1e-06)
    shift = total[1:2] / width_all * inverse
    both = jnp.concatenate([inverse, shift, jnp.zeros((6, size), F32)], 0)
    scales[...] = both
    both = both.T
    inverse, shift = both[:, 0:1], both[:, 1:2]
    cum_rows = cum[...]
    cols = cum_rows.T
    growth = jnp.exp(cols)
    causal = lax.broadcasted_iota(jnp.int32, (EDGE, size), 0) <= lax.broadcasted_iota(
        jnp.int32, (EDGE, size), 1
    )
    heads_rows = []
    for h in range(heads):
        lanes = slice(h * dim, (h + 1) * dim)
        n = attended[:, lanes] * inverse
        d = ((g2[:, lanes].astype(F32) - n * shift) * inverse).astype(BF16)
        grad[:, lanes] = d
        scaled = (q2[:, lanes].astype(F32) * growth[:, h : h + 1]).astype(BF16)
        part, at = divmod(h, heads // PARTS)
        adjoints[part][at * dim : (at + 1) * dim, :] = dot(scaled, d, (0, 0)).astype(BF16)
        differ = cum_rows[h : h + 1, :] - cols[:EDGE, h : h + 1]
        mixing = jnp.where(causal, jnp.exp(jnp.where(causal, differ, 0.0)), 0.0)
        scores = (dot(v2[:EDGE, lanes], d, (1, 1)) * mixing).astype(BF16)
        top = dot(scores, q2[:, lanes], (1, 0))
        heads_rows.append(top[:8])
    for i, adjoint in enumerate(adjoints):
        tops = [top[:4] for top in heads_rows[i * heads // PARTS : (i + 1) * heads // PARTS]]
        if 4 * len(tops) < EDGE:
            tops.append(jnp.zeros((EDGE - 4 * len(tops), dim), F32))
        adjoint[width // PARTS :, :] = jnp.concatenate(tops, 0).astype(BF16)


def inner_grad_kernel(
    attended, scales, q2, kc2, v2, grad, weights, cum, before,
    keep, send, partial, key_grad, normed,
):
    size, width = q2.shape
    dim = before.shape[1]
    heads = width // dim
    start = lax.axis_index("ctx") < PAIR
    inverse = scales[...].T[:, 0:1]
    cum_rows = cum[...]
    cols = cum_rows.T
    growth = jnp.exp(cols)
    for h in range(heads):
        lanes = slice(h * dim, (h + 1) * dim)
        normed[:, lanes] = (attended[:, lanes] * inverse).astype(BF16)
        d = grad[:, lanes]
        scores = dot(d, v2[:, lanes], (1, 1)) * mixing_of(cum_rows, cols, h)
        scores = scores.astype(BF16)
        query_grad = dot(scores, kc2[:, lanes], (1, 0)) + growth[:, h : h + 1] * dot(
            d, unless(start, before[lanes, :]), (1, 1)
        )
        key_grad[:, lanes] = dot(scores, q2[:, lanes], (0, 0))
        partial[:, lanes] = query_grad + dot(weights[h], d, (0, 0))
    here, there = halves(size // PAIR)
    keep[...] = normed[here, :]
    send[...] = normed[there, :]


def outer_grad_kernel(
    last, part, partial, key_grad, kc2, v2, cum, behind, more, taps, keep, send, padded, done
):
    size, width = partial.shape
    dim = behind.shape[1]
    heads = width // dim // PARTS
    chunk = width // PARTS
    mine = lax.rem(lax.axis_index("ctx"), PAIR)
    own = pl.ds(pl.multiple_of(mine * width + part * chunk, chunk), chunk)
    ends = lax.axis_index("ctx") >= last
    tops = unless(ends, behind[chunk:, :].astype(F32))
    cols = cum[...].T
    after = jnp.exp(cols[size - 1 :, :] - cols)
    for h in range(heads):
        at = part * heads + h
        lanes = slice(at * dim, (at + 1) * dim)
        here = slice(h * dim, (h + 1) * dim)
        scale = after[:, at : at + 1]
        state = unless(ends, behind[here, :])
        padded[:size, here] = key_grad[:, lanes] + scale * dot(v2[:, lanes], state, (1, 1))
        done[:, here] = partial[:, lanes] + scale * dot(kc2[:, lanes], state, (1, 0))
        top = jnp.concatenate([tops[4 * h : 4 * h + 4], jnp.zeros((4, dim), F32)], 0)
        padded[size:, here] = top + more[:, lanes]
    total = done[...]
    for j in range(taps.shape[1]):
        total = total + taps[0, j : j + 1, own] * padded[j : j + size, :]
    done[...] = total
    here, there = halves(size // PAIR)
    first = lax.axis_index("pp") == 0
    keep[...] = unless(first, done[here, :]).astype(BF16)
    send[...] = unless(first, done[there, :]).astype(BF16)


def place_kernel(*refs):
    *pieces, out, sems = refs
    kept, got = pieces[: len(pieces) // 2], pieces[len(pieces) // 2 :]
    width = kept[0].shape[1]
    mine = lax.rem(lax.axis_index("ctx"), PAIR)
    pairs = []
    for half, parts in ((mine, kept), (1 - mine, got)):
        for i, part in enumerate(parts):
            start = pl.multiple_of((half * len(parts) + i) * width, width)
            pairs.append((part, out.at[0, :, pl.ds(start, width)]))
    for copy in copy_all(pairs, sems):
        copy.wait()


def placed(kept, got):
    pieces = kept + got
    rows = kept[0].shape[0]
    return call(
        place_kernel,
        [shape((1, rows, sum(piece.shape[1] for piece in pieces)), BF16)],
        *pieces,
        scratch=[pltpu.SemaphoreType.DMA((len(pieces),))],
        out_hbm=True,
    )[0]


def turned(block, axis, distance):
    count = lax.axis_size(axis)
    return lax.ppermute(block, axis, [(i, (i + distance) % count) for i in range(count)])


def swapped(block):
    return lax.ppermute(block, "ctx", [(i, i ^ 1) for i in range(lax.axis_size("ctx"))])


def to_earlier_section(block, flip):
    blocks, sections = lax.axis_size("ctx"), lax.axis_size("pp")
    route = [
        (c * sections + p, (c ^ flip) * sections + (p - 1) % sections)
        for c in range(blocks)
        for p in range(sections)
    ]
    return lax.ppermute(block, ("ctx", "pp"), route)


def summed_parts(part):
    blocks, count = lax.axis_size("ctx"), lax.axis_size("tp")
    pair = part + lax.ppermute(part, "tp", [(i, i ^ 1) for i in range(count)])
    parts = [pair]
    for flip in range(PAIR):
        for k in range(0, count, 2):
            if flip or k:
                route = [
                    (c * count + t, (c ^ flip) * count + (t + k) % count)
                    for c in range(blocks)
                    for t in range(count)
                ]
                parts.append(lax.ppermute(pair, ("ctx", "tp"), route))
    return parts


def per_device(queries, key_input, values, log_decay, conv_weight, out_grad):
    rows, width = queries.shape[1], queries.shape[2] // PAIR
    heads = log_decay.shape[2] // PAIR
    dim = width // heads
    size = PAIR * rows
    blocks = lax.axis_size("ctx")
    supers = blocks // PAIR
    width_all = queries.shape[2] * lax.axis_size("tp")
    log_decay = jnp.swapaxes(log_decay, 1, 2)
    arrays = (queries, key_input, values, out_grad, log_decay)
    queries, key_input, values, out_grad, decays = (
        pltpu.with_memory_space_constraint(x, pltpu.HBM) for x in arrays
    )

    first = call(
        pack_kernel,
        [shape((2 * rows + EDGE, width), BF16)],
        key_input, values, decays,
        scratch=[pltpu.VMEM(log_decay.shape, F32), pltpu.SemaphoreType.DMA((3,))],
        hbm=range(3),
    )[0]
    got = swapped(first)
    edges = ()
    if supers > 2:
        edge = arrays[1][0, rows - EDGE :]
        near = lax.ppermute(edge[:, :width], "ctx", [(i, i + 1) for i in range(1, blocks - 1, 2)])
        far = lax.ppermute(edge[:, width:], "ctx", [(i, i + 2) for i in range(1, blocks - 2, 2)])
        edges = (near + far,)
    second, own = call(
        pack_more_kernel,
        [shape((2 * rows, width), BF16), shape((4 * rows, width), BF16)],
        queries, key_input, values, out_grad, first[2 * rows :],
        scratch=[pltpu.SemaphoreType.DMA((6,))],
        hbm=range(4),
    )
    got_more = swapped(second)
    kc2, v2, cum, state, top = call(
        join_kernel,
        [shape((size, width), BF16)] * 2
        + [shape((8, size), F32), shape((width + 4 * heads, dim), BF16), shape((EDGE, width), F32)],
        got, own, log_decay, conv_weight, *edges,
        scratch=[pltpu.VMEM((EDGE + size, width), F32), pltpu.VMEM((8, size), F32)],
    )
    carry = jnp.repeat(jnp.exp(cum[:heads, -1]), dim)[:, None]
    pair_index = lax.axis_index("ctx") // PAIR
    before = turned(state, "ctx", PAIR)
    for _ in range(supers - 2):
        earlier = unless(pair_index == 0, before[:width]).astype(F32)
        joined = state[:width].astype(F32) + carry * earlier
        moved = turned(joined.astype(BF16), "ctx", PAIR)
        before = jnp.concatenate([moved, before[width:]], 0)

    q2, g2, weights, inside = call(
        local_kernel,
        [shape((size, width), BF16)] * 2
        + [shape((heads, size, size), BF16), shape((size, width), F32)],
        got_more, own, kc2, v2, cum,
        flops=4 * heads * size * size * dim,
    )
    kc2, weights, attended, sums = call(
        attend_kernel,
        [shape(kc2.shape, BF16), shape(weights.shape, BF16),
         shape((size, width), F32), shape((2, size), F32)],
        kc2, weights, inside, q2, g2, v2, cum, before, top, conv_weight,
        scratch=[pltpu.VMEM((EDGE, width), F32)],
        alias=((0, 0), (1, 1)),
    )
    parts = summed_parts(sums)
    chunk = width // PARTS
    scales, grad, *adjoints = call(
        lambda *refs: grad_kernel(width_all, *refs),
        [shape((8, size), F32), shape((size, width), BF16)]
        + [shape((chunk + EDGE, dim), BF16)] * PARTS,
        attended, q2, v2, g2, cum, *parts,
    )
    last_pair = pair_index == supers - 1
    behind = []
    for i, adjoint in enumerate(adjoints):
        moved = turned(adjoint, "ctx", -PAIR)
        for _ in range(supers - 2):
            later = unless(last_pair, moved[:chunk]).astype(F32)
            joined = adjoint[:chunk].astype(F32) + carry[i * chunk : (i + 1) * chunk] * later
            state = turned(joined.astype(BF16), "ctx", -PAIR)
            moved = jnp.concatenate([state, moved[chunk:]], 0)
        behind.append(moved)
    more = jnp.zeros((8, width), F32)
    if supers > 2:
        after = jnp.exp(cum[:heads, -1:] - cum[:heads, :8])
        states = jnp.concatenate([part[:chunk] for part in behind], 0)
        state_part = jnp.einsum(
            "shv,hkv->shk",
            v2[:8].reshape(8, heads, dim),
            unless(last_pair, states).reshape(heads, dim, dim),
            preferred_element_type=F32,
        )
        more = turned((after.T[:, :, None] * state_part).reshape(8, width), "ctx", -PAIR)
        more = unless(last_pair, more)

    keep, send, partial, key_grad = call(
        inner_grad_kernel,
        [shape((rows, width), BF16)] * 2 + [shape((size, width), F32)] * 2,
        attended, scales, q2, kc2, v2, grad, weights, cum, before,
        scratch=[pltpu.VMEM((size, width), BF16)],
        flops=10 * heads * size * size * dim,
    )
    layer_output = placed([keep], [swapped(send)])
    kept, got = [], []
    for i in range(PARTS):
        keep, send = call(
            lambda *refs, i=i: outer_grad_kernel(blocks - PAIR, i, *refs),
            [shape((rows, chunk), BF16)] * 2,
            partial, key_grad, kc2, v2, cum, behind[i], more, conv_weight,
            scratch=[pltpu.VMEM((size + 8, chunk), F32), pltpu.VMEM((size, chunk), F32)],
        )
        kept.append(to_earlier_section(keep, 0))
        got.append(to_earlier_section(send, 1))
    return (layer_output, placed(kept, got))


def solution(mesh):
    placed = (
        P("pp", "ctx", "tp"),
        P("pp", "ctx", "tp"),
        P("pp", "ctx", "tp"),
        P("pp", "ctx", "tp"),
        P("pp", None, "tp"),
        P("pp", "ctx", "tp"),
    )
    return jax.shard_map(
        per_device,
        mesh=mesh,
        in_specs=placed,
        out_specs=(P("pp", "ctx", "tp"), P("pp", "ctx", "tp")),
        check_vma=False,
    )
```

```python
import jax
import jax.numpy as jnp
from jax import lax
from jax.experimental import pallas as pl
from jax.experimental.pallas import tpu as pltpu
from jax.sharding import PartitionSpec as P

F32 = jnp.float32
BF16 = jnp.bfloat16
PAIR = 2
EDGE = 16
LEAD = 4
STEPS = 2
PARTS = 1


def call(kernel, outs, *args, scratch=(), flops=0, hbm=(), out_hbm=False, alias=()):
    vmem = pl.BlockSpec(memory_space=pltpu.VMEM)
    moved = sum(a.size * a.dtype.itemsize for a in args) + sum(
        s.size * s.dtype.itemsize for s in outs
    )
    return pl.pallas_call(
        kernel,
        out_shape=outs,
        in_specs=[
            pl.BlockSpec(memory_space=pltpu.HBM) if i in hbm else vmem for i in range(len(args))
        ],
        out_specs=[pl.BlockSpec(memory_space=pltpu.HBM) if out_hbm else vmem] * len(outs),
        scratch_shapes=scratch,
        input_output_aliases=dict(alias),
        compiler_params=pltpu.CompilerParams(vmem_limit_bytes=32 * 1024 * 1024),
        cost_estimate=pl.CostEstimate(flops=flops, bytes_accessed=moved, transcendentals=0),
    )(*args)


def shape(dims, dtype):
    return jax.ShapeDtypeStruct(dims, dtype)


def halves(size):
    mine = lax.rem(lax.axis_index("ctx"), PAIR)
    return (
        pl.ds(pl.multiple_of(mine * size, size), size),
        pl.ds(pl.multiple_of((1 - mine) * size, size), size),
    )


def dot(a, b, contract):
    return lax.dot_general(a, b, ((contract[:1], contract[1:]), ((), ())), preferred_element_type=F32)


def split3(x):
    hi = x.astype(BF16)
    rest = x - hi.astype(F32)
    mid = rest.astype(BF16)
    return hi, mid, (rest - mid.astype(F32)).astype(BF16)


def half_rows(rows, mine, heads):
    return jnp.where(mine == 0, rows[:heads], rows[heads:])


def copy_all(pairs, sems):
    copies = [pltpu.make_async_copy(src, to, sems.at[i]) for i, (src, to) in enumerate(pairs)]
    for copy in copies:
        copy.start()
    return copies


def step_lanes(width, chunk, step, mine):
    return pl.ds(pl.multiple_of(mine * width + step * chunk, chunk), chunk)


def pack_kernel(k, v, log_decay, *refs):
    *outs, cum, decays, sems = refs
    first = outs[0]
    rows, heads = k.shape[1], log_decay.shape[1] // PAIR
    mine = lax.rem(lax.axis_index("ctx"), PAIR)
    chunk = first.shape[1]
    pairs = [(log_decay, decays)]
    for step, out in enumerate(outs):
        other = step_lanes(k.shape[2] // PAIR, chunk, step, 1 - mine)
        for i, ref in enumerate((k, v)):
            pairs.append((ref.at[0, :, other], out.at[i * rows : (i + 1) * rows, :]))
    copies = copy_all(pairs, sems)
    copies[0].wait()
    upto = lax.broadcasted_iota(jnp.int32, (rows, rows), 0) <= lax.broadcasted_iota(
        jnp.int32, (rows, rows), 1
    )
    upto = upto.astype(F32).astype(BF16)
    sums = sum(dot(part, upto, (1, 0)) for part in split3(decays[0]))
    cum[...] = sums
    line = chunk // rows
    parts = [
        jnp.concatenate([part[h : h + 1] for h in range(at, at + line)], 1).astype(F32)
        for part in split3(half_rows(sums, 1 - mine, heads))
        for at in range(0, heads, line)
    ]
    parts.append(jnp.zeros((EDGE - len(parts), chunk), F32))
    first[2 * rows :, :] = jnp.concatenate(parts, 0).astype(BF16)
    for copy in copies[1:]:
        copy.wait()


def pack_more_kernel(q, k, v, g, _, second, third, own, sems):
    rows = q.shape[1]
    lanes_own, other = halves(q.shape[2] // PAIR)
    pairs = [(q.at[0, :, other], second), (g.at[0, :, other], third)]
    pairs += [
        (ref.at[0, :, lanes_own], own.at[i * rows : (i + 1) * rows, :])
        for i, ref in enumerate((k, v, q, g))
    ]
    for copy in copy_all(pairs, sems):
        copy.wait()


def join_step(step, got, own, taps, edges, cum_rows, kc2, v2, top, state, padded):
    size, width = kc2.shape
    rows, chunk = size // PAIR, got.shape[1]
    dim = state.shape[1]
    heads = chunk // dim
    here, there = halves(rows)
    mine = lax.rem(lax.axis_index("ctx"), PAIR)
    lanes = slice(step * chunk, (step + 1) * chunk)
    v2[here, lanes] = own[rows : 2 * rows, lanes]
    v2[there, lanes] = got[rows : 2 * rows, :]
    padded[:EDGE, :] = edges[0][:, lanes].astype(F32) if edges else jnp.zeros((EDGE, chunk), F32)
    start = pl.multiple_of(EDGE + mine * rows, EDGE)
    padded[pl.ds(start, rows), :] = own[:rows, lanes].astype(F32)
    start = pl.multiple_of(EDGE + (1 - mine) * rows, EDGE)
    padded[pl.ds(start, rows), :] = got[:rows, :].astype(F32)
    total = jnp.zeros((size, chunk), F32)
    taps_at = step_lanes(width, chunk, step, mine)
    for j in range(taps.shape[1]):
        total = total + taps[0, j : j + 1, taps_at] * padded[EDGE - j : EDGE - j + size, :]
    keys = total.astype(BF16)
    kc2[:, lanes] = keys
    top[:, lanes] = total[:EDGE]
    cols = cum_rows.T
    after = jnp.exp(cols[size - 1 :, :] - cols)
    keys = keys.astype(F32)
    for h in range(heads):
        at = step * heads + h
        scaled = (keys[:, h * dim : (h + 1) * dim] * after[:, at : at + 1]).astype(BF16)
        sums = dot(scaled, v2[:, at * dim : (at + 1) * dim], (0, 0))
        state[h * dim : (h + 1) * dim, :] = sums.astype(BF16)
    last = padded[EDGE + size - LEAD : EDGE + size, :]
    last = [last[:, h * dim : (h + 1) * dim] for h in range(heads)]
    if LEAD * heads < EDGE:
        last.append(jnp.zeros((EDGE - LEAD * heads, dim), F32))
    state[chunk:, :] = jnp.concatenate(last, 0).astype(BF16)


def join_kernel(got, own, own_cum, taps, *refs):
    *edges, kc2, v2, top, state, cum, padded = refs
    rows, heads = own_cum.shape[1], own_cum.shape[0] // PAIR
    mine = lax.rem(lax.axis_index("ctx"), PAIR)
    coded = got[2 * rows :, :].astype(F32)
    lines = heads * rows // coded.shape[1]
    row = coded[:lines] + coded[lines : 2 * lines] + coded[2 * lines : 3 * lines]
    per_line = heads // lines
    other_rows = jnp.concatenate(
        [
            row[h // per_line : h // per_line + 1, h % per_line * rows : (h % per_line + 1) * rows]
            for h in range(heads)
        ],
        0,
    )
    own_rows = half_rows(own_cum[...], mine, heads)
    front = jnp.where(mine == 0, own_rows, other_rows)
    back = jnp.where(mine == 0, other_rows, own_rows) + front[:, rows - 1 :]
    cum_rows = jnp.concatenate([front, back], 1)
    cum_rows = jnp.concatenate([cum_rows, jnp.zeros((8 - heads, PAIR * rows), F32)], 0)
    cum[...] = cum_rows
    join_step(0, got, own, taps, edges, cum_rows, kc2, v2, top, state, padded)


def join_next_kernel(step, _kc2, _v2, _top, got, own, cum, taps, *refs):
    *edges, kc2, v2, top, state, padded = refs
    join_step(step, got, own, taps, edges, cum[...], kc2, v2, top, state, padded)


def mixing_of(cum_rows, cols, h, first=0):
    differ = cols[:, h : h + 1] - cum_rows[h : h + 1, :]
    at = lax.broadcasted_iota(jnp.int32, differ.shape, 1)
    causal = (lax.broadcasted_iota(jnp.int32, differ.shape, 0) >= at) & (at >= first)
    return jnp.where(causal, jnp.exp(jnp.where(causal, differ, 0.0)), 0.0)


def lead_mixing_of(cum_rows, cols, heads):
    wide = (cols.shape[0], heads * LEAD)
    lane = lax.broadcasted_iota(jnp.int32, wide, 1)
    late = jnp.zeros(wide, F32)
    for h in range(heads):
        late = jnp.where(lane // LEAD == h, cols[:, h : h + 1], late)
    early = jnp.concatenate([cum_rows[h : h + 1, :LEAD] for h in range(heads)], 1)
    causal = lax.broadcasted_iota(jnp.int32, wide, 0) >= lane % LEAD
    return jnp.where(causal, jnp.exp(jnp.where(causal, late - early, 0.0)), 0.0)


def block_diagonal(rows, dim, heads, first=0):
    wide = jnp.concatenate([rows] * heads, 0)
    head = lax.broadcasted_iota(jnp.int32, wide.shape, 0) // LEAD
    lane = lax.broadcasted_iota(jnp.int32, wide.shape, 1) // dim + first
    return jnp.where(head == lane, wide, 0.0).astype(BF16)


def local_kernel(got, got_g, own, kc2, v2, cum, q2, g2, weights, inside, lead_mixing, lead_values):
    size, width = q2.shape
    heads, dim = weights.shape[0], width // weights.shape[0]
    rows = size // PAIR
    here, there = halves(rows)
    q2[here, :] = own[2 * rows : 3 * rows, :]
    q2[there, :] = got[...]
    g2[here, :] = own[3 * rows :, :]
    g2[there, :] = got_g[...]
    cum_rows = cum[...]
    cols = cum_rows.T
    lead_mixing[...] = lead_mixing_of(cum_rows, cols, heads)
    lead_values[...] = block_diagonal(v2[:EDGE, :].astype(F32)[:LEAD], dim, heads)
    for h in range(heads):
        lanes = slice(h * dim, (h + 1) * dim)
        scores = dot(q2[:, lanes], kc2[:, lanes], (1, 1))
        w = (scores * mixing_of(cum_rows, cols, h, LEAD)).astype(BF16)
        weights[h] = w
        inside[:, lanes] = dot(w, v2[:, lanes], (1, 0))


def unless(flag, block):
    return jnp.where(flag, jnp.zeros_like(block), block)


def attend_kernel(step, *refs):
    kc2, inside, q2, g2, cum, top, taps, lead_mixing, lead_values, before, *refs = refs
    *carried, kc2_whole, attended, lead_weights, out, reach = refs
    size, width = q2.shape
    dim = before.shape[1]
    heads = width // dim
    chunk = width // STEPS
    lanes = slice(step * chunk, (step + 1) * chunk)
    mine = lax.rem(lax.axis_index("ctx"), PAIR)
    start = lax.axis_index("ctx") < PAIR
    tail = unless(start, before[chunk:, :].astype(F32))
    reach[...] = jnp.zeros_like(reach)
    for h in range(chunk // dim):
        reach[LEAD : 2 * LEAD, h * dim : (h + 1) * dim] = tail[LEAD * h : LEAD * (h + 1)]
    fixed = top[: 2 * LEAD, lanes]
    taps_at = step_lanes(width, chunk, step, mine)
    for j in range(1, taps.shape[1]):
        fixed = fixed + taps[0, j : j + 1, taps_at] * reach[2 * LEAD - j : 4 * LEAD - j, :]
    rows = jnp.concatenate([fixed, top[2 * LEAD :, lanes]], 0)
    kc2_whole[:EDGE, lanes] = rows.astype(BF16)
    lead_keys = block_diagonal(fixed[:LEAD], dim, heads, step * chunk // dim)
    lead = (dot(q2[:, lanes], lead_keys, (1, 1)) * lead_mixing[...]).astype(BF16)
    lead_weights[...] = lead
    growth = jnp.exp(cum[...].T)
    squares = carried[0][0] if carried else jnp.zeros((size, dim), F32)
    products = carried[0][1] if carried else jnp.zeros((size, dim), F32)
    for h in range(chunk // dim):
        at = step * chunk // dim + h
        here = slice(at * dim, (at + 1) * dim)
        state = unless(start, before[h * dim : (h + 1) * dim, :])
        a = inside[:, here] + dot(lead, lead_values[:, here], (1, 0))
        a = a + growth[:, at : at + 1] * dot(q2[:, here], state, (1, 0))
        attended[:, here] = a
        squares = squares + a * a
        products = products + a * g2[:, here].astype(F32)
    if step < STEPS - 1:
        out[0] = squares
        out[1] = products
        return
    ones = jnp.ones((8, dim), BF16)
    both = jnp.concatenate([squares, products], 0)
    line = sum(dot(ones, part, (1, 1)) for part in split3(both))[:1]
    out[...] = jnp.concatenate([line[:, :size], line[:, size:]], 0)


def grad_kernel(width_all, attended, q2, lead_mixing, lead_values, g2, cum, *refs):
    *sums, scales, grad = refs[:-PARTS]
    adjoints = refs[-PARTS:]
    size, width = q2.shape
    dim = adjoints[0].shape[1]
    heads = width // dim
    total = sum(ref[...] for ref in sums[1:]) + sums[0][...]
    inverse = 1.0 / jnp.sqrt(total[0:1] / width_all + 1e-06)
    shift = total[1:2] / width_all * inverse
    both = jnp.concatenate([inverse, shift, jnp.zeros((6, size), F32)], 0)
    scales[...] = both
    both = both.T
    inverse, shift = both[:, 0:1], both[:, 1:2]
    growth = jnp.exp(cum[...].T)
    for h in range(heads):
        lanes = slice(h * dim, (h + 1) * dim)
        n = attended[:, lanes] * inverse
        d = ((g2[:, lanes].astype(F32) - n * shift) * inverse).astype(BF16)
        grad[:, lanes] = d
        scaled = (q2[:, lanes].astype(F32) * growth[:, h : h + 1]).astype(BF16)
        part, at = divmod(h, heads // PARTS)
        adjoints[part][at * dim : (at + 1) * dim, :] = dot(scaled, d, (0, 0)).astype(BF16)
    scores = (dot(grad[...], lead_values[...], (1, 1)) * lead_mixing[...]).astype(BF16)
    tops = dot(scores, q2[...], (0, 0))
    per_part = heads // PARTS
    for i, adjoint in enumerate(adjoints):
        rows = [
            tops[LEAD * h : LEAD * (h + 1), h * dim : (h + 1) * dim]
            for h in range(i * per_part, (i + 1) * per_part)
        ]
        if LEAD * per_part < EDGE:
            rows.append(jnp.zeros((EDGE - LEAD * per_part, dim), F32))
        adjoint[width // PARTS :, :] = jnp.concatenate(rows, 0).astype(BF16)


def inner_grad_kernel(
    attended, scales, q2, kc2, v2, grad, weights, cum, *refs
):
    before, lead_weights = refs[:STEPS], refs[STEPS : 2 * STEPS]
    keep, send, partial, key_grad, normed = refs[2 * STEPS :]
    size, width = q2.shape
    dim = before[0].shape[1]
    heads = width // dim
    per_step = heads // STEPS
    start = lax.axis_index("ctx") < PAIR
    inverse = scales[...].T[:, 0:1]
    cum_rows = cum[...]
    cols = cum_rows.T
    growth = jnp.exp(cols)
    for h in range(heads):
        lanes = slice(h * dim, (h + 1) * dim)
        normed[:, lanes] = (attended[:, lanes] * inverse).astype(BF16)
        d = grad[:, lanes]
        scores = dot(d, v2[:, lanes], (1, 1)) * mixing_of(cum_rows, cols, h)
        scores = scores.astype(BF16)
        step, at = divmod(h, per_step)
        state = unless(start, before[step][at * dim : (at + 1) * dim, :])
        query_grad = dot(scores, kc2[:, lanes], (1, 0)) + growth[:, h : h + 1] * dot(
            d, state, (1, 1)
        )
        key_grad[:, lanes] = dot(scores, q2[:, lanes], (0, 0))
        partial[:, lanes] = query_grad + dot(weights[h], d, (0, 0))
    lead = sum(ref[...].astype(F32) for ref in lead_weights).astype(BF16)
    lead = dot(lead, grad[...], (0, 0))
    for h in range(heads):
        lanes = slice(h * dim, (h + 1) * dim)
        partial[:LEAD, lanes] = partial[:LEAD, lanes] + lead[LEAD * h : LEAD * (h + 1), lanes]
    here, there = halves(size // PAIR)
    keep[...] = normed[here, :]
    send[...] = normed[there, :]


def outer_grad_kernel(
    last, part, partial, key_grad, kc2, v2, cum, behind, more, taps, keep, send, padded, done
):
    size, width = partial.shape
    dim = behind.shape[1]
    heads = width // dim // PARTS
    chunk = width // PARTS
    mine = lax.rem(lax.axis_index("ctx"), PAIR)
    own = pl.ds(pl.multiple_of(mine * width + part * chunk, chunk), chunk)
    ends = lax.axis_index("ctx") >= last
    tops = unless(ends, behind[chunk:, :].astype(F32))
    cols = cum[...].T
    after = jnp.exp(cols[size - 1 :, :] - cols)
    for h in range(heads):
        at = part * heads + h
        lanes = slice(at * dim, (at + 1) * dim)
        here = slice(h * dim, (h + 1) * dim)
        scale = after[:, at : at + 1]
        state = unless(ends, behind[here, :])
        padded[:size, here] = key_grad[:, lanes] + scale * dot(v2[:, lanes], state, (1, 1))
        done[:, here] = partial[:, lanes] + scale * dot(kc2[:, lanes], state, (1, 0))
        top = jnp.concatenate([tops[4 * h : 4 * h + 4], jnp.zeros((4, dim), F32)], 0)
        padded[size:, here] = top + more[:, lanes]
    total = done[...]
    for j in range(taps.shape[1]):
        total = total + taps[0, j : j + 1, own] * padded[j : j + size, :]
    done[...] = total
    here, there = halves(size // PAIR)
    first = lax.axis_index("pp") == 0
    keep[...] = unless(first, done[here, :]).astype(BF16)
    send[...] = unless(first, done[there, :]).astype(BF16)


def place_kernel(*refs):
    *pieces, out, sems = refs
    kept, got = pieces[: len(pieces) // 2], pieces[len(pieces) // 2 :]
    width = kept[0].shape[1]
    mine = lax.rem(lax.axis_index("ctx"), PAIR)
    pairs = []
    for half, parts in ((mine, kept), (1 - mine, got)):
        for i, part in enumerate(parts):
            start = pl.multiple_of((half * len(parts) + i) * width, width)
            pairs.append((part, out.at[0, :, pl.ds(start, width)]))
    for copy in copy_all(pairs, sems):
        copy.wait()


def placed(kept, got):
    pieces = kept + got
    rows = kept[0].shape[0]
    return call(
        place_kernel,
        [shape((1, rows, sum(piece.shape[1] for piece in pieces)), BF16)],
        *pieces,
        scratch=[pltpu.SemaphoreType.DMA((len(pieces),))],
        out_hbm=True,
    )[0]


def turned(block, axis, distance):
    count = lax.axis_size(axis)
    return lax.ppermute(block, axis, [(i, (i + distance) % count) for i in range(count)])


def swapped(block):
    return lax.ppermute(block, "ctx", [(i, i ^ 1) for i in range(lax.axis_size("ctx"))])


def to_earlier_section(block, flip):
    blocks, sections = lax.axis_size("ctx"), lax.axis_size("pp")
    route = [
        (c * sections + p, (c ^ flip) * sections + (p - 1) % sections)
        for c in range(blocks)
        for p in range(sections)
    ]
    return lax.ppermute(block, ("ctx", "pp"), route)


def summed_parts(part):
    blocks, count = lax.axis_size("ctx"), lax.axis_size("tp")
    pair = part + lax.ppermute(part, "tp", [(i, i ^ 1) for i in range(count)])
    parts = [pair]
    ways = [(flip, k) for k in range(2, count, 2) for flip in range(PAIR)] + [(1, 0)]
    for flip, k in ways:
        route = [
            (c * count + t, (c ^ flip) * count + (t + k) % count)
            for c in range(blocks)
            for t in range(count)
        ]
        parts.append(lax.ppermute(pair, ("ctx", "tp"), route))
    return parts


def per_device(queries, key_input, values, log_decay, conv_weight, out_grad):
    rows, width = queries.shape[1], queries.shape[2] // PAIR
    heads = log_decay.shape[2] // PAIR
    dim = width // heads
    size = PAIR * rows
    blocks = lax.axis_size("ctx")
    supers = blocks // PAIR
    width_all = queries.shape[2] * lax.axis_size("tp")
    log_decay = jnp.swapaxes(log_decay, 1, 2)
    arrays = (queries, key_input, values, out_grad, log_decay)
    queries, key_input, values, out_grad, decays = (
        pltpu.with_memory_space_constraint(x, pltpu.HBM) for x in arrays
    )

    step_width = width // STEPS
    *packed, own_cum = call(
        pack_kernel,
        [shape((2 * rows + EDGE, step_width), BF16)]
        + [shape((2 * rows, step_width), BF16)] * (STEPS - 1)
        + [shape((PAIR * heads, rows), F32)],
        key_input, values, decays,
        scratch=[pltpu.VMEM(log_decay.shape, F32), pltpu.SemaphoreType.DMA((1 + 2 * STEPS,))],
        hbm=range(3),
    )
    got = [swapped(part) for part in packed]
    edges = ()
    if supers > 2:
        edge = arrays[1][0, rows - EDGE :]
        near = lax.ppermute(edge[:, :width], "ctx", [(i, i + 1) for i in range(1, blocks - 1, 2)])
        far = lax.ppermute(edge[:, width:], "ctx", [(i, i + 2) for i in range(1, blocks - 2, 2)])
        edges = (near + far,)
    second, third, own = call(
        pack_more_kernel,
        [shape((rows, width), BF16)] * 2 + [shape((4 * rows, width), BF16)],
        queries, key_input, values, out_grad, packed[0][2 * rows :],
        scratch=[pltpu.SemaphoreType.DMA((6,))],
        hbm=range(4),
    )
    got_q, got_g = swapped(second), swapped(third)
    joined = [
        shape((size, width), BF16), shape((size, width), BF16), shape((EDGE, width), F32),
        shape((step_width + EDGE, dim), BF16),
    ]
    room = [pltpu.VMEM((EDGE + size, step_width), F32)]
    kc2, v2, top, state, cum = call(
        join_kernel,
        joined + [shape((8, size), F32)],
        got[0], own, own_cum, conv_weight, *edges,
        scratch=room,
    )
    states = [state]
    for step in range(1, STEPS):
        kc2, v2, top, state = call(
            lambda *refs, step=step: join_next_kernel(step, *refs),
            joined,
            kc2, v2, top, got[step], own, cum, conv_weight, *edges,
            scratch=room,
            alias=((0, 0), (1, 1), (2, 2)),
        )
        states.append(state)
    carry = jnp.repeat(jnp.exp(cum[:heads, -1]), dim)[:, None]
    pair_index = lax.axis_index("ctx") // PAIR
    before = []
    for step, state in enumerate(states):
        moved = turned(state, "ctx", PAIR)
        for _ in range(supers - 2):
            earlier = unless(pair_index == 0, moved[:step_width]).astype(F32)
            earlier = carry[step * step_width : (step + 1) * step_width] * earlier
            earlier = (state[:step_width].astype(F32) + earlier).astype(BF16)
            moved = jnp.concatenate([turned(earlier, "ctx", PAIR), moved[step_width:]], 0)
        before.append(moved)

    q2, g2, weights, inside, lead_mixing, lead_values = call(
        local_kernel,
        [shape((size, width), BF16)] * 2
        + [shape((heads, size, size), BF16), shape((size, width), F32)]
        + [shape((size, LEAD * heads), F32), shape((LEAD * heads, width), BF16)],
        got_q, got_g, own, kc2, v2, cum,
        flops=4 * heads * size * size * dim,
    )
    lead_weights, carried = [], []
    for step in range(STEPS):
        last = step == STEPS - 1
        kc2, inside, lead, sums = call(
            lambda *refs, step=step: attend_kernel(step, *refs),
            [shape(kc2.shape, BF16), shape((size, width), F32), shape((size, LEAD * heads), BF16),
             shape((2, size) if last else (2, size, dim), F32)],
            kc2, inside, q2, g2, cum, top, conv_weight, lead_mixing, lead_values,
            before[step], *carried,
            scratch=[pltpu.VMEM((4 * LEAD, step_width), F32)],
            alias=((0, 0), (1, 1)),
        )
        lead_weights.append(lead)
        carried = [sums]
    attended = inside
    parts = summed_parts(sums)
    chunk = width // PARTS
    scales, grad, *adjoints = call(
        lambda *refs: grad_kernel(width_all, *refs),
        [shape((8, size), F32), shape((size, width), BF16)]
        + [shape((chunk + EDGE, dim), BF16)] * PARTS,
        attended, q2, lead_mixing, lead_values, g2, cum, *parts,
    )
    last_pair = pair_index == supers - 1
    behind = []
    for i, adjoint in enumerate(adjoints):
        moved = turned(adjoint, "ctx", -PAIR)
        for _ in range(supers - 2):
            later = unless(last_pair, moved[:chunk]).astype(F32)
            joined = adjoint[:chunk].astype(F32) + carry[i * chunk : (i + 1) * chunk] * later
            state = turned(joined.astype(BF16), "ctx", -PAIR)
            moved = jnp.concatenate([state, moved[chunk:]], 0)
        behind.append(moved)
    more = jnp.zeros((8, width), F32)
    if supers > 2:
        after = jnp.exp(cum[:heads, -1:] - cum[:heads, :8])
        states = jnp.concatenate([part[:chunk] for part in behind], 0)
        state_part = jnp.einsum(
            "shv,hkv->shk",
            v2[:8].reshape(8, heads, dim),
            unless(last_pair, states).reshape(heads, dim, dim),
            preferred_element_type=F32,
        )
        more = turned((after.T[:, :, None] * state_part).reshape(8, width), "ctx", -PAIR)
        more = unless(last_pair, more)

    keep, send, partial, key_grad = call(
        inner_grad_kernel,
        [shape((rows, width), BF16)] * 2 + [shape((size, width), F32)] * 2,
        attended, scales, q2, kc2, v2, grad, weights, cum, *before, *lead_weights,
        scratch=[pltpu.VMEM((size, width), BF16)],
        flops=10 * heads * size * size * dim,
    )
    layer_output = placed([keep], [swapped(send)])
    kept, got = [], []
    for i in range(PARTS):
        keep, send = call(
            lambda *refs, i=i: outer_grad_kernel(blocks - PAIR, i, *refs),
            [shape((rows, chunk), BF16)] * 2,
            partial, key_grad, kc2, v2, cum, behind[i], more, conv_weight,
            scratch=[pltpu.VMEM((size + 8, chunk), F32), pltpu.VMEM((size, chunk), F32)],
        )
        kept.append(to_earlier_section(keep, 0))
        got.append(to_earlier_section(send, 1))
    return (layer_output, placed(kept, got))


def solution(mesh):
    placed = (
        P("pp", "ctx", "tp"),
        P("pp", "ctx", "tp"),
        P("pp", "ctx", "tp"),
        P("pp", "ctx", "tp"),
        P("pp", None, "tp"),
        P("pp", "ctx", "tp"),
    )
    return jax.shard_map(
        per_device,
        mesh=mesh,
        in_specs=placed,
        out_specs=(P("pp", "ctx", "tp"), P("pp", "ctx", "tp")),
        check_vma=False,
    )
```

```python
import jax
import jax.numpy as jnp
from jax import lax
from jax.experimental import pallas as pl
from jax.experimental.pallas import tpu as pltpu
from jax.sharding import PartitionSpec as P

F32 = jnp.float32
BF16 = jnp.bfloat16
PAIR = 2
EDGE = 16
LEAD = 4
STEPS = 2
PARTS = 1


def call(kernel, outs, *args, scratch=(), flops=0, hbm=(), out_hbm=False, alias=()):
    vmem = pl.BlockSpec(memory_space=pltpu.VMEM)
    moved = sum(a.size * a.dtype.itemsize for a in args) + sum(
        s.size * s.dtype.itemsize for s in outs
    )
    return pl.pallas_call(
        kernel,
        out_shape=outs,
        in_specs=[
            pl.BlockSpec(memory_space=pltpu.HBM) if i in hbm else vmem for i in range(len(args))
        ],
        out_specs=[pl.BlockSpec(memory_space=pltpu.HBM) if out_hbm else vmem] * len(outs),
        scratch_shapes=scratch,
        input_output_aliases=dict(alias),
        compiler_params=pltpu.CompilerParams(vmem_limit_bytes=32 * 1024 * 1024),
        cost_estimate=pl.CostEstimate(flops=flops, bytes_accessed=moved, transcendentals=0),
    )(*args)


def shape(dims, dtype):
    return jax.ShapeDtypeStruct(dims, dtype)


def halves(size):
    mine = lax.rem(lax.axis_index("ctx"), PAIR)
    return (
        pl.ds(pl.multiple_of(mine * size, size), size),
        pl.ds(pl.multiple_of((1 - mine) * size, size), size),
    )


def dot(a, b, contract):
    return lax.dot_general(a, b, ((contract[:1], contract[1:]), ((), ())), preferred_element_type=F32)


def split3(x):
    hi = x.astype(BF16)
    rest = x - hi.astype(F32)
    mid = rest.astype(BF16)
    return hi, mid, (rest - mid.astype(F32)).astype(BF16)


def half_rows(rows, mine, heads):
    return jnp.where(mine == 0, rows[:heads], rows[heads:])


def copy_all(pairs, sems):
    copies = [pltpu.make_async_copy(src, to, sems.at[i]) for i, (src, to) in enumerate(pairs)]
    for copy in copies:
        copy.start()
    return copies


def step_lanes(width, chunk, step, mine):
    return pl.ds(pl.multiple_of(mine * width + step * chunk, chunk), chunk)


def pack_kernel(k, v, log_decay, *refs):
    *outs, cum, decays, sems = refs
    first = outs[0]
    rows, heads = k.shape[1], log_decay.shape[1] // PAIR
    mine = lax.rem(lax.axis_index("ctx"), PAIR)
    chunk = first.shape[1]
    pairs = [(log_decay, decays)]
    for step, out in enumerate(outs):
        other = step_lanes(k.shape[2] // PAIR, chunk, step, 1 - mine)
        for i, ref in enumerate((k, v)):
            pairs.append((ref.at[0, :, other], out.at[i * rows : (i + 1) * rows, :]))
    copies = copy_all(pairs, sems)
    copies[0].wait()
    upto = lax.broadcasted_iota(jnp.int32, (rows, rows), 0) <= lax.broadcasted_iota(
        jnp.int32, (rows, rows), 1
    )
    upto = upto.astype(F32).astype(BF16)
    sums = sum(dot(part, upto, (1, 0)) for part in split3(decays[0]))
    cum[...] = sums
    line = chunk // rows
    parts = [
        jnp.concatenate([part[h : h + 1] for h in range(at, at + line)], 1).astype(F32)
        for part in split3(half_rows(sums, 1 - mine, heads))
        for at in range(0, heads, line)
    ]
    parts.append(jnp.zeros((EDGE - len(parts), chunk), F32))
    first[2 * rows :, :] = jnp.concatenate(parts, 0).astype(BF16)
    for copy in copies[1:]:
        copy.wait()


def pack_more_kernel(q, k, v, g, _, second, third, own, sems):
    rows = q.shape[1]
    lanes_own, other = halves(q.shape[2] // PAIR)
    pairs = [(q.at[0, :, other], second), (g.at[0, :, other], third)]
    pairs += [
        (ref.at[0, :, lanes_own], own.at[i * rows : (i + 1) * rows, :])
        for i, ref in enumerate((k, v, q, g))
    ]
    for copy in copy_all(pairs, sems):
        copy.wait()


def join_step(step, got, own, taps, edges, cum_rows, kc2, v2, top, ks2, state, padded):
    size, width = kc2.shape
    rows, chunk = size // PAIR, got.shape[1]
    dim = state.shape[1]
    heads = chunk // dim
    here, there = halves(rows)
    mine = lax.rem(lax.axis_index("ctx"), PAIR)
    lanes = slice(step * chunk, (step + 1) * chunk)
    v2[here, lanes] = own[rows : 2 * rows, lanes]
    v2[there, lanes] = got[rows : 2 * rows, :]
    padded[:EDGE, :] = edges[0][:, lanes].astype(F32) if edges else jnp.zeros((EDGE, chunk), F32)
    start = pl.multiple_of(EDGE + mine * rows, EDGE)
    padded[pl.ds(start, rows), :] = own[:rows, lanes].astype(F32)
    start = pl.multiple_of(EDGE + (1 - mine) * rows, EDGE)
    padded[pl.ds(start, rows), :] = got[:rows, :].astype(F32)
    total = jnp.zeros((size, chunk), F32)
    taps_at = step_lanes(width, chunk, step, mine)
    for j in range(taps.shape[1]):
        total = total + taps[0, j : j + 1, taps_at] * padded[EDGE - j : EDGE - j + size, :]
    keys = total.astype(BF16)
    kc2[:, lanes] = keys
    top[:, lanes] = total[:EDGE]
    cols = cum_rows.T
    after = jnp.exp(cols[size - 1 :, :] - cols)
    keys = keys.astype(F32)
    for h in range(heads):
        at = step * heads + h
        scaled = (keys[:, h * dim : (h + 1) * dim] * after[:, at : at + 1]).astype(BF16)
        ks2[:, at * dim : (at + 1) * dim] = scaled
        sums = dot(scaled, v2[:, at * dim : (at + 1) * dim], (0, 0))
        state[h * dim : (h + 1) * dim, :] = sums.astype(BF16)
    last = padded[EDGE + size - LEAD : EDGE + size, :]
    last = [last[:, h * dim : (h + 1) * dim] for h in range(heads)]
    if LEAD * heads < EDGE:
        last.append(jnp.zeros((EDGE - LEAD * heads, dim), F32))
    state[chunk:, :] = jnp.concatenate(last, 0).astype(BF16)


def join_kernel(got, own, own_cum, taps, *refs):
    *edges, kc2, v2, top, ks2, state, cum, padded = refs
    rows, heads = own_cum.shape[1], own_cum.shape[0] // PAIR
    mine = lax.rem(lax.axis_index("ctx"), PAIR)
    coded = got[2 * rows :, :].astype(F32)
    lines = heads * rows // coded.shape[1]
    row = coded[:lines] + coded[lines : 2 * lines] + coded[2 * lines : 3 * lines]
    per_line = heads // lines
    other_rows = jnp.concatenate(
        [
            row[h // per_line : h // per_line + 1, h % per_line * rows : (h % per_line + 1) * rows]
            for h in range(heads)
        ],
        0,
    )
    own_rows = half_rows(own_cum[...], mine, heads)
    front = jnp.where(mine == 0, own_rows, other_rows)
    back = jnp.where(mine == 0, other_rows, own_rows) + front[:, rows - 1 :]
    cum_rows = jnp.concatenate([front, back], 1)
    cum_rows = jnp.concatenate([cum_rows, jnp.zeros((8 - heads, PAIR * rows), F32)], 0)
    cum[...] = cum_rows
    join_step(0, got, own, taps, edges, cum_rows, kc2, v2, top, ks2, state, padded)


def join_next_kernel(step, _kc2, _v2, _top, _ks2, got, own, cum, taps, *refs):
    *edges, kc2, v2, top, ks2, state, padded = refs
    join_step(step, got, own, taps, edges, cum[...], kc2, v2, top, ks2, state, padded)


def mixing_of(cum_rows, cols, h, first=0):
    differ = cols[:, h : h + 1] - cum_rows[h : h + 1, :]
    at = lax.broadcasted_iota(jnp.int32, differ.shape, 1)
    causal = (lax.broadcasted_iota(jnp.int32, differ.shape, 0) >= at) & (at >= first)
    return jnp.where(causal, jnp.exp(jnp.where(causal, differ, 0.0)), 0.0)


def lead_mixing_of(cum_rows, cols, heads):
    wide = (cols.shape[0], heads * LEAD)
    lane = lax.broadcasted_iota(jnp.int32, wide, 1)
    late = jnp.zeros(wide, F32)
    for h in range(heads):
        late = jnp.where(lane // LEAD == h, cols[:, h : h + 1], late)
    early = jnp.concatenate([cum_rows[h : h + 1, :LEAD] for h in range(heads)], 1)
    causal = lax.broadcasted_iota(jnp.int32, wide, 0) >= lane % LEAD
    return jnp.where(causal, jnp.exp(jnp.where(causal, late - early, 0.0)), 0.0)


def block_diagonal(rows, dim, heads, first=0):
    wide = jnp.concatenate([rows] * heads, 0)
    head = lax.broadcasted_iota(jnp.int32, wide.shape, 0) // LEAD
    lane = lax.broadcasted_iota(jnp.int32, wide.shape, 1) // dim + first
    return jnp.where(head == lane, wide, 0.0).astype(BF16)


def local_kernel(got, own, kc2, v2, cum, q2, qs2, weights, inside, lead_mixing, lead_values):
    size, width = q2.shape
    heads, dim = weights.shape[0], width // weights.shape[0]
    rows = size // PAIR
    here, there = halves(rows)
    q2[here, :] = own[2 * rows : 3 * rows, :]
    q2[there, :] = got[...]
    cum_rows = cum[...]
    cols = cum_rows.T
    growth = jnp.exp(cols)
    lead_mixing[...] = lead_mixing_of(cum_rows, cols, heads)
    lead_values[...] = block_diagonal(v2[:EDGE, :].astype(F32)[:LEAD], dim, heads)
    for h in range(heads):
        lanes = slice(h * dim, (h + 1) * dim)
        qs2[:, lanes] = (q2[:, lanes].astype(F32) * growth[:, h : h + 1]).astype(BF16)
        scores = dot(q2[:, lanes], kc2[:, lanes], (1, 1))
        w = (scores * mixing_of(cum_rows, cols, h, LEAD)).astype(BF16)
        weights[h] = w
        inside[:, lanes] = dot(w, v2[:, lanes], (1, 0))


def unless(flag, block):
    return jnp.where(flag, jnp.zeros_like(block), block)


def attend_kernel(step, *refs):
    kc2, inside, q2, qs2, top, taps, lead_mixing, lead_values, before, *refs = refs
    kc2_whole, attended, lead_weights, reach = refs
    size, width = q2.shape
    dim = before.shape[1]
    heads = width // dim
    chunk = width // STEPS
    lanes = slice(step * chunk, (step + 1) * chunk)
    mine = lax.rem(lax.axis_index("ctx"), PAIR)
    start = lax.axis_index("ctx") < PAIR
    tail = unless(start, before[chunk:, :].astype(F32))
    reach[...] = jnp.zeros_like(reach)
    for h in range(chunk // dim):
        reach[LEAD : 2 * LEAD, h * dim : (h + 1) * dim] = tail[LEAD * h : LEAD * (h + 1)]
    fixed = top[: 2 * LEAD, lanes]
    taps_at = step_lanes(width, chunk, step, mine)
    for j in range(1, taps.shape[1]):
        fixed = fixed + taps[0, j : j + 1, taps_at] * reach[2 * LEAD - j : 4 * LEAD - j, :]
    rows = jnp.concatenate([fixed, top[2 * LEAD :, lanes]], 0)
    kc2_whole[:EDGE, lanes] = rows.astype(BF16)
    lead_keys = block_diagonal(fixed[:LEAD], dim, heads, step * chunk // dim)
    lead = (dot(q2[:, lanes], lead_keys, (1, 1)) * lead_mixing[...]).astype(BF16)
    lead_weights[...] = lead
    for h in range(chunk // dim):
        at = step * chunk // dim + h
        here = slice(at * dim, (at + 1) * dim)
        state = unless(start, before[h * dim : (h + 1) * dim, :])
        a = inside[:, here] + dot(lead, lead_values[:, here], (1, 0))
        attended[:, here] = a + dot(qs2[:, here], state, (1, 0))


def sums_kernel(dim, attended, own, got, g2, sums):
    size, width = attended.shape
    rows = size // PAIR
    here, there = halves(rows)
    g2[here, :] = own[3 * rows :, :]
    g2[there, :] = got[...]
    squares = jnp.zeros((size, dim), F32)
    products = jnp.zeros((size, dim), F32)
    for at in range(0, width, dim):
        a = attended[:, at : at + dim]
        squares = squares + a * a
        products = products + a * g2[:, at : at + dim].astype(F32)
    ones = jnp.ones((8, dim), BF16)
    both = jnp.concatenate([squares, products], 0)
    line = sum(dot(ones, part, (1, 1)) for part in split3(both))[:1]
    sums[...] = jnp.concatenate([line[:, :size], line[:, size:]], 0)


def grad_kernel(width_all, attended, q2, qs2, lead_mixing, lead_values, g2, *refs):
    *sums, scales, grad = refs[:-PARTS]
    adjoints = refs[-PARTS:]
    size, width = q2.shape
    dim = adjoints[0].shape[1]
    heads = width // dim
    total = sum(ref[...] for ref in sums[1:]) + sums[0][...]
    inverse = 1.0 / jnp.sqrt(total[0:1] / width_all + 1e-06)
    shift = total[1:2] / width_all * inverse
    both = jnp.concatenate([inverse, shift * inverse * inverse, jnp.zeros((6, size), F32)], 0)
    scales[...] = both
    both = both.T
    inverse, pull = both[:, 0:1], both[:, 1:2]
    for h in range(heads):
        lanes = slice(h * dim, (h + 1) * dim)
        d = (g2[:, lanes].astype(F32) * inverse - attended[:, lanes] * pull).astype(BF16)
        grad[:, lanes] = d
        part, at = divmod(h, heads // PARTS)
        adjoints[part][at * dim : (at + 1) * dim, :] = dot(qs2[:, lanes], d, (0, 0)).astype(BF16)
    scores = (dot(grad[...], lead_values[...], (1, 1)) * lead_mixing[...]).astype(BF16)
    tops = dot(scores, q2[...], (0, 0))
    per_part = heads // PARTS
    for i, adjoint in enumerate(adjoints):
        rows = [
            tops[LEAD * h : LEAD * (h + 1), h * dim : (h + 1) * dim]
            for h in range(i * per_part, (i + 1) * per_part)
        ]
        if LEAD * per_part < EDGE:
            rows.append(jnp.zeros((EDGE - LEAD * per_part, dim), F32))
        adjoint[width // PARTS :, :] = jnp.concatenate(rows, 0).astype(BF16)


def inner_grad_kernel(
    attended, scales, q2, kc2, v2, grad, weights, cum, *refs
):
    before, lead_weights = refs[:STEPS], refs[STEPS : 2 * STEPS]
    keep, send, partial, key_grad, vs2, normed = refs[2 * STEPS :]
    size, width = q2.shape
    dim = before[0].shape[1]
    heads = width // dim
    per_step = heads // STEPS
    start = lax.axis_index("ctx") < PAIR
    inverse = scales[...].T[:, 0:1]
    cum_rows = cum[...]
    cols = cum_rows.T
    growth = jnp.exp(cols)
    after = jnp.exp(cols[size - 1 :, :] - cols)
    for h in range(heads):
        lanes = slice(h * dim, (h + 1) * dim)
        vs2[:, lanes] = (v2[:, lanes].astype(F32) * after[:, h : h + 1]).astype(BF16)
        normed[:, lanes] = (attended[:, lanes] * inverse).astype(BF16)
        d = grad[:, lanes]
        scores = dot(d, v2[:, lanes], (1, 1)) * mixing_of(cum_rows, cols, h)
        scores = scores.astype(BF16)
        step, at = divmod(h, per_step)
        state = unless(start, before[step][at * dim : (at + 1) * dim, :])
        query_grad = dot(scores, kc2[:, lanes], (1, 0)) + growth[:, h : h + 1] * dot(
            d, state, (1, 1)
        )
        key_grad[:, lanes] = dot(scores, q2[:, lanes], (0, 0))
        partial[:, lanes] = query_grad + dot(weights[h], d, (0, 0))
    lead = sum(ref[...].astype(F32) for ref in lead_weights).astype(BF16)
    lead = dot(lead, grad[...], (0, 0))
    for h in range(heads):
        lanes = slice(h * dim, (h + 1) * dim)
        partial[:LEAD, lanes] = partial[:LEAD, lanes] + lead[LEAD * h : LEAD * (h + 1), lanes]
    here, there = halves(size // PAIR)
    keep[...] = normed[here, :]
    send[...] = normed[there, :]


def outer_grad_kernel(
    last, part, partial, key_grad, ks2, vs2, behind, more, taps, keep, send, padded, done
):
    size, width = partial.shape
    dim = behind.shape[1]
    heads = width // dim // PARTS
    chunk = width // PARTS
    mine = lax.rem(lax.axis_index("ctx"), PAIR)
    own = pl.ds(pl.multiple_of(mine * width + part * chunk, chunk), chunk)
    ends = lax.axis_index("ctx") >= last
    tops = unless(ends, behind[chunk:, :].astype(F32))
    for h in range(heads):
        at = part * heads + h
        lanes = slice(at * dim, (at + 1) * dim)
        here = slice(h * dim, (h + 1) * dim)
        state = unless(ends, behind[here, :])
        padded[:size, here] = key_grad[:, lanes] + dot(vs2[:, lanes], state, (1, 1))
        done[:, here] = partial[:, lanes] + dot(ks2[:, lanes], state, (1, 0))
        top = jnp.concatenate([tops[4 * h : 4 * h + 4], jnp.zeros((4, dim), F32)], 0)
        padded[size:, here] = top + more[:, lanes]
    total = done[...]
    for j in range(taps.shape[1]):
        total = total + taps[0, j : j + 1, own] * padded[j : j + size, :]
    done[...] = total
    here, there = halves(size // PAIR)
    first = lax.axis_index("pp") == 0
    keep[...] = unless(first, done[here, :]).astype(BF16)
    send[...] = unless(first, done[there, :]).astype(BF16)


def place_kernel(*refs):
    *pieces, out, sems = refs
    got, kept = pieces[: len(pieces) // 2], pieces[len(pieces) // 2 :]
    width = kept[0].shape[1]
    mine = lax.rem(lax.axis_index("ctx"), PAIR)
    pairs = []
    for half, parts in ((mine, kept), (1 - mine, got)):
        for i, part in enumerate(parts):
            start = pl.multiple_of((half * len(parts) + i) * width, width)
            pairs.append((part, out.at[0, :, pl.ds(start, width)]))
    for copy in copy_all(pairs, sems):
        copy.wait()


def placed(kept, got):
    pieces = got + kept
    rows = kept[0].shape[0]
    return call(
        place_kernel,
        [shape((1, rows, sum(piece.shape[1] for piece in pieces)), BF16)],
        *pieces,
        scratch=[pltpu.SemaphoreType.DMA((len(pieces),))],
        out_hbm=True,
    )[0]


def turned(block, axis, distance):
    count = lax.axis_size(axis)
    return lax.ppermute(block, axis, [(i, (i + distance) % count) for i in range(count)])


def swapped(block):
    return lax.ppermute(block, "ctx", [(i, i ^ 1) for i in range(lax.axis_size("ctx"))])


def to_earlier_section(block, flip):
    blocks, sections = lax.axis_size("ctx"), lax.axis_size("pp")
    route = [
        (c * sections + p, (c ^ flip) * sections + (p - 1) % sections)
        for c in range(blocks)
        for p in range(sections)
    ]
    return lax.ppermute(block, ("ctx", "pp"), route)


def summed_parts(part):
    blocks, count = lax.axis_size("ctx"), lax.axis_size("tp")
    pair = part + lax.ppermute(part, "tp", [(i, i ^ 1) for i in range(count)])
    parts = [pair]
    ways = [(flip, k) for k in range(2, count, 2) for flip in range(PAIR)] + [(1, 0)]
    for flip, k in ways:
        route = [
            (c * count + t, (c ^ flip) * count + (t + k) % count)
            for c in range(blocks)
            for t in range(count)
        ]
        parts.append(lax.ppermute(pair, ("ctx", "tp"), route))
    return parts


def per_device(queries, key_input, values, log_decay, conv_weight, out_grad):
    rows, width = queries.shape[1], queries.shape[2] // PAIR
    heads = log_decay.shape[2] // PAIR
    dim = width // heads
    size = PAIR * rows
    blocks = lax.axis_size("ctx")
    supers = blocks // PAIR
    width_all = queries.shape[2] * lax.axis_size("tp")
    log_decay = jnp.swapaxes(log_decay, 1, 2)
    arrays = (queries, key_input, values, out_grad, log_decay)
    queries, key_input, values, out_grad, decays = (
        pltpu.with_memory_space_constraint(x, pltpu.HBM) for x in arrays
    )

    step_width = width // STEPS
    *packed, own_cum = call(
        pack_kernel,
        [shape((2 * rows + EDGE, step_width), BF16)]
        + [shape((2 * rows, step_width), BF16)] * (STEPS - 1)
        + [shape((PAIR * heads, rows), F32)],
        key_input, values, decays,
        scratch=[pltpu.VMEM(log_decay.shape, F32), pltpu.SemaphoreType.DMA((1 + 2 * STEPS,))],
        hbm=range(3),
    )
    got = [swapped(part) for part in packed]
    edges = ()
    if supers > 2:
        edge = arrays[1][0, rows - EDGE :]
        near = lax.ppermute(edge[:, :width], "ctx", [(i, i + 1) for i in range(1, blocks - 1, 2)])
        far = lax.ppermute(edge[:, width:], "ctx", [(i, i + 2) for i in range(1, blocks - 2, 2)])
        edges = (near + far,)
    second, third, own = call(
        pack_more_kernel,
        [shape((rows, width), BF16)] * 2 + [shape((4 * rows, width), BF16)],
        queries, key_input, values, out_grad, packed[0][2 * rows :],
        scratch=[pltpu.SemaphoreType.DMA((6,))],
        hbm=range(4),
    )
    got_q, got_g = swapped(second), swapped(third)
    joined = [
        shape((size, width), BF16), shape((size, width), BF16), shape((EDGE, width), F32),
        shape((size, width), BF16), shape((step_width + EDGE, dim), BF16),
    ]
    room = [pltpu.VMEM((EDGE + size, step_width), F32)]
    kc2, v2, top, ks2, state, cum = call(
        join_kernel,
        joined + [shape((8, size), F32)],
        got[0], own, own_cum, conv_weight, *edges,
        scratch=room,
    )
    states = [state]
    for step in range(1, STEPS):
        kc2, v2, top, ks2, state = call(
            lambda *refs, step=step: join_next_kernel(step, *refs),
            joined,
            kc2, v2, top, ks2, got[step], own, cum, conv_weight, *edges,
            scratch=room,
            alias=((0, 0), (1, 1), (2, 2), (3, 3)),
        )
        states.append(state)
    carry = jnp.repeat(jnp.exp(cum[:heads, -1]), dim)[:, None]
    pair_index = lax.axis_index("ctx") // PAIR
    before = []
    for step, state in enumerate(states):
        moved = turned(state, "ctx", PAIR)
        for _ in range(supers - 2):
            earlier = unless(pair_index == 0, moved[:step_width]).astype(F32)
            earlier = carry[step * step_width : (step + 1) * step_width] * earlier
            earlier = (state[:step_width].astype(F32) + earlier).astype(BF16)
            moved = jnp.concatenate([turned(earlier, "ctx", PAIR), moved[step_width:]], 0)
        before.append(moved)

    q2, qs2, weights, inside, lead_mixing, lead_values = call(
        local_kernel,
        [shape((size, width), BF16)] * 2
        + [shape((heads, size, size), BF16), shape((size, width), F32)]
        + [shape((size, LEAD * heads), F32), shape((LEAD * heads, width), BF16)],
        got_q, own, kc2, v2, cum,
        flops=4 * heads * size * size * dim,
    )
    lead_weights = []
    for step in range(STEPS):
        kc2, inside, lead = call(
            lambda *refs, step=step: attend_kernel(step, *refs),
            [shape(kc2.shape, BF16), shape((size, width), F32), shape((size, LEAD * heads), BF16)],
            kc2, inside, q2, qs2, top, conv_weight, lead_mixing, lead_values, before[step],
            scratch=[pltpu.VMEM((4 * LEAD, step_width), F32)],
            alias=((0, 0), (1, 1)),
        )
        lead_weights.append(lead)
    attended = inside
    g2, sums = call(
        lambda *refs: sums_kernel(dim, *refs),
        [shape((size, width), BF16), shape((2, size), F32)],
        attended, own, got_g,
    )
    parts = summed_parts(sums)
    chunk = width // PARTS
    scales, grad, *adjoints = call(
        lambda *refs: grad_kernel(width_all, *refs),
        [shape((8, size), F32), shape((size, width), BF16)]
        + [shape((chunk + EDGE, dim), BF16)] * PARTS,
        attended, q2, qs2, lead_mixing, lead_values, g2, *parts,
    )
    last_pair = pair_index == supers - 1
    behind = []
    for i, adjoint in enumerate(adjoints):
        moved = turned(adjoint, "ctx", -PAIR)
        for _ in range(supers - 2):
            later = unless(last_pair, moved[:chunk]).astype(F32)
            joined = adjoint[:chunk].astype(F32) + carry[i * chunk : (i + 1) * chunk] * later
            state = turned(joined.astype(BF16), "ctx", -PAIR)
            moved = jnp.concatenate([state, moved[chunk:]], 0)
        behind.append(moved)
    more = jnp.zeros((8, width), F32)
    if supers > 2:
        after = jnp.exp(cum[:heads, -1:] - cum[:heads, :8])
        states = jnp.concatenate([part[:chunk] for part in behind], 0)
        state_part = jnp.einsum(
            "shv,hkv->shk",
            v2[:8].reshape(8, heads, dim),
            unless(last_pair, states).reshape(heads, dim, dim),
            preferred_element_type=F32,
        )
        more = turned((after.T[:, :, None] * state_part).reshape(8, width), "ctx", -PAIR)
        more = unless(last_pair, more)

    keep, send, partial, key_grad, vs2 = call(
        inner_grad_kernel,
        [shape((rows, width), BF16)] * 2
        + [shape((size, width), F32)] * 2
        + [shape((size, width), BF16)],
        attended, scales, q2, kc2, v2, grad, weights, cum, *before, *lead_weights,
        scratch=[pltpu.VMEM((size, width), BF16)],
        flops=10 * heads * size * size * dim,
    )
    layer_output = placed([keep], [swapped(send)])
    kept, got = [], []
    for i in range(PARTS):
        keep, send = call(
            lambda *refs, i=i: outer_grad_kernel(blocks - PAIR, i, *refs),
            [shape((rows, chunk), BF16)] * 2,
            partial, key_grad, ks2, vs2, behind[i], more, conv_weight,
            scratch=[pltpu.VMEM((size + 8, chunk), F32), pltpu.VMEM((size, chunk), F32)],
        )
        got.append(to_earlier_section(send, 1))
        kept.append(to_earlier_section(keep, 0))
    return (layer_output, placed(kept, got))


def solution(mesh):
    placed = (
        P("pp", "ctx", "tp"),
        P("pp", "ctx", "tp"),
        P("pp", "ctx", "tp"),
        P("pp", "ctx", "tp"),
        P("pp", None, "tp"),
        P("pp", "ctx", "tp"),
    )
    return jax.shard_map(
        per_device,
        mesh=mesh,
        in_specs=placed,
        out_specs=(P("pp", "ctx", "tp"), P("pp", "ctx", "tp")),
        check_vma=False,
    )
```

```python
import jax
import jax.numpy as jnp
from jax import lax
from jax.experimental import pallas as pl
from jax.experimental.pallas import tpu as pltpu
from jax.sharding import PartitionSpec as P

F32 = jnp.float32
BF16 = jnp.bfloat16
PAIR = 2
EDGE = 16
LEAD = 4
STEPS = 2
PARTS = 1


def call(kernel, outs, *args, scratch=(), flops=0, hbm=(), out_hbm=False, alias=()):
    vmem = pl.BlockSpec(memory_space=pltpu.VMEM)
    moved = sum(a.size * a.dtype.itemsize for a in args) + sum(
        s.size * s.dtype.itemsize for s in outs
    )
    return pl.pallas_call(
        kernel,
        out_shape=outs,
        in_specs=[
            pl.BlockSpec(memory_space=pltpu.HBM) if i in hbm else vmem for i in range(len(args))
        ],
        out_specs=[pl.BlockSpec(memory_space=pltpu.HBM) if out_hbm else vmem] * len(outs),
        scratch_shapes=scratch,
        input_output_aliases=dict(alias),
        compiler_params=pltpu.CompilerParams(vmem_limit_bytes=32 * 1024 * 1024),
        cost_estimate=pl.CostEstimate(flops=flops, bytes_accessed=moved, transcendentals=0),
    )(*args)


def shape(dims, dtype):
    return jax.ShapeDtypeStruct(dims, dtype)


def halves(size):
    mine = lax.rem(lax.axis_index("ctx"), PAIR)
    return (
        pl.ds(pl.multiple_of(mine * size, size), size),
        pl.ds(pl.multiple_of((1 - mine) * size, size), size),
    )


def dot(a, b, contract):
    return lax.dot_general(a, b, ((contract[:1], contract[1:]), ((), ())), preferred_element_type=F32)


def split3(x):
    hi = x.astype(BF16)
    rest = x - hi.astype(F32)
    mid = rest.astype(BF16)
    return hi, mid, (rest - mid.astype(F32)).astype(BF16)


def half_rows(rows, mine, heads):
    return jnp.where(mine == 0, rows[:heads], rows[heads:])


def copy_all(pairs, sems):
    copies = [pltpu.make_async_copy(src, to, sems.at[i]) for i, (src, to) in enumerate(pairs)]
    for copy in copies:
        copy.start()
    return copies


def step_lanes(width, chunk, step, mine):
    return pl.ds(pl.multiple_of(mine * width + step * chunk, chunk), chunk)


def pack_kernel(k, v, log_decay, *refs):
    *outs, cum, decays, sems = refs
    first = outs[0]
    rows, heads = k.shape[1], log_decay.shape[1] // PAIR
    mine = lax.rem(lax.axis_index("ctx"), PAIR)
    chunk = first.shape[1]
    pairs = [(log_decay, decays)]
    for step, out in enumerate(outs):
        other = step_lanes(k.shape[2] // PAIR, chunk, step, 1 - mine)
        for i, ref in enumerate((k, v)):
            pairs.append((ref.at[0, :, other], out.at[i * rows : (i + 1) * rows, :]))
    copies = copy_all(pairs, sems)
    copies[0].wait()
    upto = lax.broadcasted_iota(jnp.int32, (rows, rows), 0) <= lax.broadcasted_iota(
        jnp.int32, (rows, rows), 1
    )
    upto = upto.astype(F32).astype(BF16)
    sums = sum(dot(part, upto, (1, 0)) for part in split3(decays[0]))
    cum[...] = sums
    line = chunk // rows
    parts = [
        jnp.concatenate([part[h : h + 1] for h in range(at, at + line)], 1).astype(F32)
        for part in split3(half_rows(sums, 1 - mine, heads))
        for at in range(0, heads, line)
    ]
    parts.append(jnp.zeros((EDGE - len(parts), chunk), F32))
    first[2 * rows :, :] = jnp.concatenate(parts, 0).astype(BF16)
    for copy in copies[1:]:
        copy.wait()


def pack_more_kernel(q, k, v, g, _, second, third, own, sems):
    rows = q.shape[1]
    lanes_own, other = halves(q.shape[2] // PAIR)
    pairs = [(q.at[0, :, other], second), (g.at[0, :, other], third)]
    pairs += [
        (ref.at[0, :, lanes_own], own.at[i * rows : (i + 1) * rows, :])
        for i, ref in enumerate((k, v, q, g))
    ]
    for copy in copy_all(pairs, sems):
        copy.wait()


def join_step(step, got, own, taps, edges, cum_rows, kc2, v2, top, ks2, state, padded):
    size, width = kc2.shape
    rows, chunk = size // PAIR, got.shape[1]
    dim = state.shape[1]
    heads = chunk // dim
    here, there = halves(rows)
    mine = lax.rem(lax.axis_index("ctx"), PAIR)
    lanes = slice(step * chunk, (step + 1) * chunk)
    v2[here, lanes] = own[rows : 2 * rows, lanes]
    v2[there, lanes] = got[rows : 2 * rows, :]
    padded[:EDGE, :] = edges[0][:, lanes].astype(F32) if edges else jnp.zeros((EDGE, chunk), F32)
    start = pl.multiple_of(EDGE + mine * rows, EDGE)
    padded[pl.ds(start, rows), :] = own[:rows, lanes].astype(F32)
    start = pl.multiple_of(EDGE + (1 - mine) * rows, EDGE)
    padded[pl.ds(start, rows), :] = got[:rows, :].astype(F32)
    total = jnp.zeros((size, chunk), F32)
    taps_at = step_lanes(width, chunk, step, mine)
    for j in range(taps.shape[1]):
        total = total + taps[0, j : j + 1, taps_at] * padded[EDGE - j : EDGE - j + size, :]
    keys = total.astype(BF16)
    kc2[:, lanes] = keys
    top[:, lanes] = total[:EDGE]
    cols = cum_rows.T
    after = jnp.exp(cols[size - 1 :, :] - cols)
    keys = keys.astype(F32)
    for h in range(heads):
        at = step * heads + h
        scaled = (keys[:, h * dim : (h + 1) * dim] * after[:, at : at + 1]).astype(BF16)
        ks2[:, at * dim : (at + 1) * dim] = scaled
        sums = dot(scaled, v2[:, at * dim : (at + 1) * dim], (0, 0))
        state[h * dim : (h + 1) * dim, :] = sums.astype(BF16)
    last = padded[EDGE + size - LEAD : EDGE + size, :]
    last = [last[:, h * dim : (h + 1) * dim] for h in range(heads)]
    if LEAD * heads < EDGE:
        last.append(jnp.zeros((EDGE - LEAD * heads, dim), F32))
    state[chunk:, :] = jnp.concatenate(last, 0).astype(BF16)


def join_kernel(got, own, own_cum, taps, *refs):
    *edges, kc2, v2, top, ks2, state, cum, padded = refs
    rows, heads = own_cum.shape[1], own_cum.shape[0] // PAIR
    mine = lax.rem(lax.axis_index("ctx"), PAIR)
    coded = got[2 * rows :, :].astype(F32)
    lines = heads * rows // coded.shape[1]
    row = coded[:lines] + coded[lines : 2 * lines] + coded[2 * lines : 3 * lines]
    per_line = heads // lines
    other_rows = jnp.concatenate(
        [
            row[h // per_line : h // per_line + 1, h % per_line * rows : (h % per_line + 1) * rows]
            for h in range(heads)
        ],
        0,
    )
    own_rows = half_rows(own_cum[...], mine, heads)
    front = jnp.where(mine == 0, own_rows, other_rows)
    back = jnp.where(mine == 0, other_rows, own_rows) + front[:, rows - 1 :]
    cum_rows = jnp.concatenate([front, back], 1)
    cum_rows = jnp.concatenate([cum_rows, jnp.zeros((8 - heads, PAIR * rows), F32)], 0)
    cum[...] = cum_rows
    join_step(0, got, own, taps, edges, cum_rows, kc2, v2, top, ks2, state, padded)


def join_next_kernel(step, _kc2, _v2, _top, _ks2, got, own, cum, taps, *refs):
    *edges, kc2, v2, top, ks2, state, padded = refs
    join_step(step, got, own, taps, edges, cum[...], kc2, v2, top, ks2, state, padded)


def mixing_of(cum_rows, cols, h, first=0):
    differ = cols[:, h : h + 1] - cum_rows[h : h + 1, :]
    at = lax.broadcasted_iota(jnp.int32, differ.shape, 1)
    causal = (lax.broadcasted_iota(jnp.int32, differ.shape, 0) >= at) & (at >= first)
    return jnp.where(causal, jnp.exp(jnp.where(causal, differ, 0.0)), 0.0)


def lead_mixing_of(cum_rows, cols, heads):
    wide = (cols.shape[0], heads * LEAD)
    lane = lax.broadcasted_iota(jnp.int32, wide, 1)
    late = jnp.zeros(wide, F32)
    for h in range(heads):
        late = jnp.where(lane // LEAD == h, cols[:, h : h + 1], late)
    early = jnp.concatenate([cum_rows[h : h + 1, :LEAD] for h in range(heads)], 1)
    causal = lax.broadcasted_iota(jnp.int32, wide, 0) >= lane % LEAD
    return jnp.where(causal, jnp.exp(jnp.where(causal, late - early, 0.0)), 0.0)


def block_diagonal(rows, dim, heads, first=0):
    wide = jnp.concatenate([rows] * heads, 0)
    head = lax.broadcasted_iota(jnp.int32, wide.shape, 0) // LEAD
    lane = lax.broadcasted_iota(jnp.int32, wide.shape, 1) // dim + first
    return jnp.where(head == lane, wide, 0.0).astype(BF16)


def local_kernel(got, own, kc2, v2, cum, q2, qs2, weights, inside, lead_mixing, lead_values):
    size, width = q2.shape
    heads, dim = weights.shape[0], width // weights.shape[0]
    rows = size // PAIR
    here, there = halves(rows)
    q2[here, :] = own[2 * rows : 3 * rows, :]
    q2[there, :] = got[...]
    cum_rows = cum[...]
    cols = cum_rows.T
    growth = jnp.exp(cols)
    lead_mixing[...] = lead_mixing_of(cum_rows, cols, heads)
    lead_values[...] = block_diagonal(v2[:EDGE, :].astype(F32)[:LEAD], dim, heads)
    for h in range(heads):
        lanes = slice(h * dim, (h + 1) * dim)
        qs2[:, lanes] = (q2[:, lanes].astype(F32) * growth[:, h : h + 1]).astype(BF16)
        scores = dot(q2[:, lanes], kc2[:, lanes], (1, 1))
        w = (scores * mixing_of(cum_rows, cols, h, LEAD)).astype(BF16)
        weights[h] = w
        inside[:, lanes] = dot(w, v2[:, lanes], (1, 0))


def unless(flag, block):
    return jnp.where(flag, jnp.zeros_like(block), block)


def attend_kernel(step, *refs):
    kc2, inside, q2, qs2, top, taps, lead_mixing, lead_values, before, *refs = refs
    kc2_whole, attended, lead_weights, reach = refs
    size, width = q2.shape
    dim = before.shape[1]
    heads = width // dim
    chunk = width // STEPS
    lanes = slice(step * chunk, (step + 1) * chunk)
    mine = lax.rem(lax.axis_index("ctx"), PAIR)
    start = lax.axis_index("ctx") < PAIR
    tail = unless(start, before[chunk:, :].astype(F32))
    reach[...] = jnp.zeros_like(reach)
    for h in range(chunk // dim):
        reach[LEAD : 2 * LEAD, h * dim : (h + 1) * dim] = tail[LEAD * h : LEAD * (h + 1)]
    fixed = top[: 2 * LEAD, lanes]
    taps_at = step_lanes(width, chunk, step, mine)
    for j in range(1, taps.shape[1]):
        fixed = fixed + taps[0, j : j + 1, taps_at] * reach[2 * LEAD - j : 4 * LEAD - j, :]
    rows = jnp.concatenate([fixed, top[2 * LEAD :, lanes]], 0)
    kc2_whole[:EDGE, lanes] = rows.astype(BF16)
    lead_keys = block_diagonal(fixed[:LEAD], dim, heads, step * chunk // dim)
    lead = (dot(q2[:, lanes], lead_keys, (1, 1)) * lead_mixing[...]).astype(BF16)
    lead_weights[...] = lead
    for h in range(chunk // dim):
        at = step * chunk // dim + h
        here = slice(at * dim, (at + 1) * dim)
        state = unless(start, before[h * dim : (h + 1) * dim, :])
        a = inside[:, here] + dot(lead, lead_values[:, here], (1, 0))
        attended[:, here] = a + dot(qs2[:, here], state, (1, 0))


def sums_kernel(dim, attended, own, got, g2, sums):
    size, width = attended.shape
    rows = size // PAIR
    here, there = halves(rows)
    g2[here, :] = own[3 * rows :, :]
    g2[there, :] = got[...]
    squares = jnp.zeros((size, dim), F32)
    products = jnp.zeros((size, dim), F32)
    for at in range(0, width, dim):
        a = attended[:, at : at + dim]
        squares = squares + a * a
        products = products + a * g2[:, at : at + dim].astype(F32)
    ones = jnp.ones((8, dim), BF16)
    both = jnp.concatenate([squares, products], 0)
    line = sum(dot(ones, part, (1, 1)) for part in split3(both))[:1]
    sums[...] = jnp.concatenate([line[:, :size], line[:, size:]], 0)


def grad_kernel(width_all, attended, q2, qs2, lead_mixing, lead_values, g2, *refs):
    *sums, scales, grad = refs[:-PARTS]
    adjoints = refs[-PARTS:]
    size, width = q2.shape
    dim = adjoints[0].shape[1]
    heads = width // dim
    total = sum(ref[...] for ref in sums[1:]) + sums[0][...]
    inverse = 1.0 / jnp.sqrt(total[0:1] / width_all + 1e-06)
    shift = total[1:2] / width_all * inverse
    both = jnp.concatenate([inverse, shift * inverse * inverse, jnp.zeros((6, size), F32)], 0)
    scales[...] = both
    both = both.T
    inverse, pull = both[:, 0:1], both[:, 1:2]
    for h in range(heads):
        lanes = slice(h * dim, (h + 1) * dim)
        d = (g2[:, lanes].astype(F32) * inverse - attended[:, lanes] * pull).astype(BF16)
        grad[:, lanes] = d
        part, at = divmod(h, heads // PARTS)
        adjoints[part][at * dim : (at + 1) * dim, :] = dot(qs2[:, lanes], d, (0, 0)).astype(BF16)
    scores = (dot(grad[...], lead_values[...], (1, 1)) * lead_mixing[...]).astype(BF16)
    tops = dot(scores, q2[...], (0, 0))
    per_part = heads // PARTS
    for i, adjoint in enumerate(adjoints):
        rows = [
            tops[LEAD * h : LEAD * (h + 1), h * dim : (h + 1) * dim]
            for h in range(i * per_part, (i + 1) * per_part)
        ]
        if LEAD * per_part < EDGE:
            rows.append(jnp.zeros((EDGE - LEAD * per_part, dim), F32))
        adjoint[width // PARTS :, :] = jnp.concatenate(rows, 0).astype(BF16)


def inner_grad_kernel(
    attended, scales, q2, kc2, v2, grad, weights, cum, *refs
):
    before, lead_weights = refs[:STEPS], refs[STEPS : 2 * STEPS]
    keep, send, partial, key_grad, vs2, normed = refs[2 * STEPS :]
    size, width = q2.shape
    dim = before[0].shape[1]
    heads = width // dim
    per_step = heads // STEPS
    start = lax.axis_index("ctx") < PAIR
    inverse = scales[...].T[:, 0:1]
    cum_rows = cum[...]
    cols = cum_rows.T
    growth = jnp.exp(cols)
    after = jnp.exp(cols[size - 1 :, :] - cols)
    for h in range(heads):
        lanes = slice(h * dim, (h + 1) * dim)
        vs2[:, lanes] = (v2[:, lanes].astype(F32) * after[:, h : h + 1]).astype(BF16)
        normed[:, lanes] = (attended[:, lanes] * inverse).astype(BF16)
        d = grad[:, lanes]
        scores = dot(d, v2[:, lanes], (1, 1)) * mixing_of(cum_rows, cols, h)
        scores = scores.astype(BF16)
        step, at = divmod(h, per_step)
        state = unless(start, before[step][at * dim : (at + 1) * dim, :])
        query_grad = dot(scores, kc2[:, lanes], (1, 0)) + growth[:, h : h + 1] * dot(
            d, state, (1, 1)
        )
        key_grad[:, lanes] = dot(scores, q2[:, lanes], (0, 0))
        partial[:, lanes] = query_grad + dot(weights[h], d, (0, 0))
    lead = sum(ref[...].astype(F32) for ref in lead_weights).astype(BF16)
    lead = dot(lead, grad[...], (0, 0))
    for h in range(heads):
        lanes = slice(h * dim, (h + 1) * dim)
        partial[:LEAD, lanes] = partial[:LEAD, lanes] + lead[LEAD * h : LEAD * (h + 1), lanes]
    here, there = halves(size // PAIR)
    keep[...] = normed[here, :]
    send[...] = normed[there, :]


def outer_grad_kernel(
    last, part, partial, key_grad, ks2, vs2, behind, more, taps, keep, send, padded, done
):
    size, width = partial.shape
    dim = behind.shape[1]
    heads = width // dim // PARTS
    chunk = width // PARTS
    mine = lax.rem(lax.axis_index("ctx"), PAIR)
    own = pl.ds(pl.multiple_of(mine * width + part * chunk, chunk), chunk)
    ends = lax.axis_index("ctx") >= last
    tops = unless(ends, behind[chunk:, :].astype(F32))
    for h in range(heads):
        at = part * heads + h
        lanes = slice(at * dim, (at + 1) * dim)
        here = slice(h * dim, (h + 1) * dim)
        state = unless(ends, behind[here, :])
        padded[:size, here] = key_grad[:, lanes] + dot(vs2[:, lanes], state, (1, 1))
        done[:, here] = partial[:, lanes] + dot(ks2[:, lanes], state, (1, 0))
        top = jnp.concatenate([tops[4 * h : 4 * h + 4], jnp.zeros((4, dim), F32)], 0)
        padded[size:, here] = top + more[:, lanes]
    total = done[...]
    for j in range(taps.shape[1]):
        total = total + taps[0, j : j + 1, own] * padded[j : j + size, :]
    done[...] = total
    here, there = halves(size // PAIR)
    first = lax.axis_index("pp") == 0
    keep[...] = unless(first, done[here, :]).astype(BF16)
    send[...] = unless(first, done[there, :]).astype(BF16)


def place_kernel(*refs):
    *pieces, out, sems = refs
    kept, got = pieces[: len(pieces) // 2], pieces[len(pieces) // 2 :]
    width = kept[0].shape[1]
    mine = lax.rem(lax.axis_index("ctx"), PAIR)
    pairs = []
    for half, parts in ((mine, kept), (1 - mine, got)):
        for i, part in enumerate(parts):
            start = pl.multiple_of((half * len(parts) + i) * width, width)
            pairs.append((part, out.at[0, :, pl.ds(start, width)]))
    for copy in copy_all(pairs, sems):
        copy.wait()


def placed(kept, got):
    pieces = kept + got
    rows = kept[0].shape[0]
    return call(
        place_kernel,
        [shape((1, rows, sum(piece.shape[1] for piece in pieces)), BF16)],
        *pieces,
        scratch=[pltpu.SemaphoreType.DMA((len(pieces),))],
        out_hbm=True,
    )[0]


def turned(block, axis, distance):
    count = lax.axis_size(axis)
    return lax.ppermute(block, axis, [(i, (i + distance) % count) for i in range(count)])


def swapped(block):
    return lax.ppermute(block, "ctx", [(i, i ^ 1) for i in range(lax.axis_size("ctx"))])


def to_earlier_section(block, flip):
    blocks, sections = lax.axis_size("ctx"), lax.axis_size("pp")
    route = [
        (c * sections + p, (c ^ flip) * sections + (p - 1) % sections)
        for c in range(blocks)
        for p in range(sections)
    ]
    return lax.ppermute(block, ("ctx", "pp"), route)


def summed_parts(part):
    blocks, count = lax.axis_size("ctx"), lax.axis_size("tp")

    def neighbour(block):
        return lax.ppermute(block, "tp", [(i, i ^ 1) for i in range(count)])

    def fetched(block, *ways):
        route = [
            (c * count + t, (c ^ ways[t % len(ways)][0]) * count + (t + ways[t % len(ways)][1]) % count)
            for c in range(blocks)
            for t in range(count)
        ]
        return lax.ppermute(block, ("ctx", "tp"), route)

    pair = part + neighbour(part)
    ways = [(1, 0)] + [(flip, k) for k in range(2, count, 2) for flip in (0, 1)]
    shared = [fetched(pair, *ways[i : i + 2]) for i in range(0, len(ways) - 1, 2)]
    parts = [pair, fetched(pair, ways[-1])]
    for block in shared:
        parts += [block, neighbour(block)]
    return parts


def per_device(queries, key_input, values, log_decay, conv_weight, out_grad):
    rows, width = queries.shape[1], queries.shape[2] // PAIR
    heads = log_decay.shape[2] // PAIR
    dim = width // heads
    size = PAIR * rows
    blocks = lax.axis_size("ctx")
    supers = blocks // PAIR
    width_all = queries.shape[2] * lax.axis_size("tp")
    log_decay = jnp.swapaxes(log_decay, 1, 2)
    arrays = (queries, key_input, values, out_grad, log_decay)
    queries, key_input, values, out_grad, decays = (
        pltpu.with_memory_space_constraint(x, pltpu.HBM) for x in arrays
    )

    step_width = width // STEPS
    *packed, own_cum = call(
        pack_kernel,
        [shape((2 * rows + EDGE, step_width), BF16)]
        + [shape((2 * rows, step_width), BF16)] * (STEPS - 1)
        + [shape((PAIR * heads, rows), F32)],
        key_input, values, decays,
        scratch=[pltpu.VMEM(log_decay.shape, F32), pltpu.SemaphoreType.DMA((1 + 2 * STEPS,))],
        hbm=range(3),
    )
    got = [swapped(part) for part in packed]
    edges = ()
    if supers > 2:
        edge = arrays[1][0, rows - EDGE :]
        near = lax.ppermute(edge[:, :width], "ctx", [(i, i + 1) for i in range(1, blocks - 1, 2)])
        far = lax.ppermute(edge[:, width:], "ctx", [(i, i + 2) for i in range(1, blocks - 2, 2)])
        edges = (near + far,)
    second, third, own = call(
        pack_more_kernel,
        [shape((rows, width), BF16)] * 2 + [shape((4 * rows, width), BF16)],
        queries, key_input, values, out_grad, packed[0][2 * rows :],
        scratch=[pltpu.SemaphoreType.DMA((6,))],
        hbm=range(4),
    )
    got_q, got_g = swapped(second), swapped(third)
    joined = [
        shape((size, width), BF16), shape((size, width), BF16), shape((EDGE, width), F32),
        shape((size, width), BF16), shape((step_width + EDGE, dim), BF16),
    ]
    room = [pltpu.VMEM((EDGE + size, step_width), F32)]
    kc2, v2, top, ks2, state, cum = call(
        join_kernel,
        joined + [shape((8, size), F32)],
        got[0], own, own_cum, conv_weight, *edges,
        scratch=room,
    )
    states = [state]
    for step in range(1, STEPS):
        kc2, v2, top, ks2, state = call(
            lambda *refs, step=step: join_next_kernel(step, *refs),
            joined,
            kc2, v2, top, ks2, got[step], own, cum, conv_weight, *edges,
            scratch=room,
            alias=((0, 0), (1, 1), (2, 2), (3, 3)),
        )
        states.append(state)
    carry = jnp.repeat(jnp.exp(cum[:heads, -1]), dim)[:, None]
    pair_index = lax.axis_index("ctx") // PAIR
    before = []
    for step, state in enumerate(states):
        moved = turned(state, "ctx", PAIR)
        for _ in range(supers - 2):
            earlier = unless(pair_index == 0, moved[:step_width]).astype(F32)
            earlier = carry[step * step_width : (step + 1) * step_width] * earlier
            earlier = (state[:step_width].astype(F32) + earlier).astype(BF16)
            moved = jnp.concatenate([turned(earlier, "ctx", PAIR), moved[step_width:]], 0)
        before.append(moved)

    q2, qs2, weights, inside, lead_mixing, lead_values = call(
        local_kernel,
        [shape((size, width), BF16)] * 2
        + [shape((heads, size, size), BF16), shape((size, width), F32)]
        + [shape((size, LEAD * heads), F32), shape((LEAD * heads, width), BF16)],
        got_q, own, kc2, v2, cum,
        flops=4 * heads * size * size * dim,
    )
    lead_weights = []
    for step in range(STEPS):
        kc2, inside, lead = call(
            lambda *refs, step=step: attend_kernel(step, *refs),
            [shape(kc2.shape, BF16), shape((size, width), F32), shape((size, LEAD * heads), BF16)],
            kc2, inside, q2, qs2, top, conv_weight, lead_mixing, lead_values, before[step],
            scratch=[pltpu.VMEM((4 * LEAD, step_width), F32)],
            alias=((0, 0), (1, 1)),
        )
        lead_weights.append(lead)
    attended = inside
    g2, sums = call(
        lambda *refs: sums_kernel(dim, *refs),
        [shape((size, width), BF16), shape((2, size), F32)],
        attended, own, got_g,
    )
    parts = summed_parts(sums)
    chunk = width // PARTS
    scales, grad, *adjoints = call(
        lambda *refs: grad_kernel(width_all, *refs),
        [shape((8, size), F32), shape((size, width), BF16)]
        + [shape((chunk + EDGE, dim), BF16)] * PARTS,
        attended, q2, qs2, lead_mixing, lead_values, g2, *parts,
    )
    last_pair = pair_index == supers - 1
    behind = []
    for i, adjoint in enumerate(adjoints):
        moved = turned(adjoint, "ctx", -PAIR)
        for _ in range(supers - 2):
            later = unless(last_pair, moved[:chunk]).astype(F32)
            joined = adjoint[:chunk].astype(F32) + carry[i * chunk : (i + 1) * chunk] * later
            state = turned(joined.astype(BF16), "ctx", -PAIR)
            moved = jnp.concatenate([state, moved[chunk:]], 0)
        behind.append(moved)
    more = jnp.zeros((8, width), F32)
    if supers > 2:
        after = jnp.exp(cum[:heads, -1:] - cum[:heads, :8])
        states = jnp.concatenate([part[:chunk] for part in behind], 0)
        state_part = jnp.einsum(
            "shv,hkv->shk",
            v2[:8].reshape(8, heads, dim),
            unless(last_pair, states).reshape(heads, dim, dim),
            preferred_element_type=F32,
        )
        more = turned((after.T[:, :, None] * state_part).reshape(8, width), "ctx", -PAIR)
        more = unless(last_pair, more)

    keep, send, partial, key_grad, vs2 = call(
        inner_grad_kernel,
        [shape((rows, width), BF16)] * 2
        + [shape((size, width), F32)] * 2
        + [shape((size, width), BF16)],
        attended, scales, q2, kc2, v2, grad, weights, cum, *before, *lead_weights,
        scratch=[pltpu.VMEM((size, width), BF16)],
        flops=10 * heads * size * size * dim,
    )
    layer_output = placed([keep], [swapped(send)])
    kept, got = [], []
    for i in range(PARTS):
        keep, send = call(
            lambda *refs, i=i: outer_grad_kernel(blocks - PAIR, i, *refs),
            [shape((rows, chunk), BF16)] * 2,
            partial, key_grad, ks2, vs2, behind[i], more, conv_weight,
            scratch=[pltpu.VMEM((size + 8, chunk), F32), pltpu.VMEM((size, chunk), F32)],
        )
        kept.append(to_earlier_section(keep, 0))
        got.append(to_earlier_section(send, 1))
    return (layer_output, placed(kept, got))


def solution(mesh):
    placed = (
        P("pp", "ctx", "tp"),
        P("pp", "ctx", "tp"),
        P("pp", "ctx", "tp"),
        P("pp", "ctx", "tp"),
        P("pp", None, "tp"),
        P("pp", "ctx", "tp"),
    )
    return jax.shard_map(
        per_device,
        mesh=mesh,
        in_specs=placed,
        out_specs=(P("pp", "ctx", "tp"), P("pp", "ctx", "tp")),
        check_vma=False,
    )
```

```python
import jax
import jax.numpy as jnp
from jax import lax
from jax.experimental import pallas as pl
from jax.experimental.pallas import tpu as pltpu
from jax.sharding import PartitionSpec as P

F32 = jnp.float32
BF16 = jnp.bfloat16
PAIR = 2
EDGE = 16
LEAD = 4
STEPS = 2
PARTS = 1


def call(kernel, outs, *args, scratch=(), flops=0, hbm=(), out_hbm=False, alias=()):
    vmem = pl.BlockSpec(memory_space=pltpu.VMEM)
    moved = sum(a.size * a.dtype.itemsize for a in args) + sum(
        s.size * s.dtype.itemsize for s in outs
    )
    return pl.pallas_call(
        kernel,
        out_shape=outs,
        in_specs=[
            pl.BlockSpec(memory_space=pltpu.HBM) if i in hbm else vmem for i in range(len(args))
        ],
        out_specs=[pl.BlockSpec(memory_space=pltpu.HBM) if out_hbm else vmem] * len(outs),
        scratch_shapes=scratch,
        input_output_aliases=dict(alias),
        compiler_params=pltpu.CompilerParams(vmem_limit_bytes=32 * 1024 * 1024),
        cost_estimate=pl.CostEstimate(flops=flops, bytes_accessed=moved, transcendentals=0),
    )(*args)


def shape(dims, dtype):
    return jax.ShapeDtypeStruct(dims, dtype)


def halves(size):
    mine = lax.rem(lax.axis_index("ctx"), PAIR)
    return (
        pl.ds(pl.multiple_of(mine * size, size), size),
        pl.ds(pl.multiple_of((1 - mine) * size, size), size),
    )


def dot(a, b, contract):
    return lax.dot_general(a, b, ((contract[:1], contract[1:]), ((), ())), preferred_element_type=F32)


def split3(x):
    hi = x.astype(BF16)
    rest = x - hi.astype(F32)
    mid = rest.astype(BF16)
    return hi, mid, (rest - mid.astype(F32)).astype(BF16)


def half_rows(rows, mine, heads):
    return jnp.where(mine == 0, rows[:heads], rows[heads:])


def copy_all(pairs, sems):
    copies = [pltpu.make_async_copy(src, to, sems.at[i]) for i, (src, to) in enumerate(pairs)]
    for copy in copies:
        copy.start()
    return copies


def step_lanes(width, chunk, step, mine):
    return pl.ds(pl.multiple_of(mine * width + step * chunk, chunk), chunk)


def pack_kernel(k, v, log_decay, *refs):
    *outs, cum, decays, sems = refs
    first = outs[0]
    rows, heads = k.shape[1], log_decay.shape[1] // PAIR
    mine = lax.rem(lax.axis_index("ctx"), PAIR)
    chunk = first.shape[1]
    pairs = [(log_decay, decays)]
    for step, out in enumerate(outs):
        other = step_lanes(k.shape[2] // PAIR, chunk, step, 1 - mine)
        for i, ref in enumerate((k, v)):
            pairs.append((ref.at[0, :, other], out.at[i * rows : (i + 1) * rows, :]))
    copies = copy_all(pairs, sems)
    copies[0].wait()
    upto = lax.broadcasted_iota(jnp.int32, (rows, rows), 0) <= lax.broadcasted_iota(
        jnp.int32, (rows, rows), 1
    )
    upto = upto.astype(F32).astype(BF16)
    sums = sum(dot(part, upto, (1, 0)) for part in split3(decays[0]))
    cum[...] = sums
    line = chunk // rows
    parts = [
        jnp.concatenate([part[h : h + 1] for h in range(at, at + line)], 1).astype(F32)
        for part in split3(half_rows(sums, 1 - mine, heads))
        for at in range(0, heads, line)
    ]
    parts.append(jnp.zeros((EDGE - len(parts), chunk), F32))
    first[2 * rows :, :] = jnp.concatenate(parts, 0).astype(BF16)
    for copy in copies[1:]:
        copy.wait()


def pack_more_kernel(q, k, v, g, _, second, third, own, sems):
    rows = q.shape[1]
    lanes_own, other = halves(q.shape[2] // PAIR)
    pairs = [(q.at[0, :, other], second), (g.at[0, :, other], third)]
    pairs += [
        (ref.at[0, :, lanes_own], own.at[i * rows : (i + 1) * rows, :])
        for i, ref in enumerate((k, v, q, g))
    ]
    for copy in copy_all(pairs, sems):
        copy.wait()


def join_step(step, got, own, taps, edges, cum_rows, kc2, v2, top, ks2, state, padded):
    size, width = kc2.shape
    rows, chunk = size // PAIR, got.shape[1]
    dim = state.shape[1]
    heads = chunk // dim
    here, there = halves(rows)
    mine = lax.rem(lax.axis_index("ctx"), PAIR)
    lanes = slice(step * chunk, (step + 1) * chunk)
    v2[here, lanes] = own[rows : 2 * rows, lanes]
    v2[there, lanes] = got[rows : 2 * rows, :]
    padded[:EDGE, :] = edges[0][:, lanes].astype(F32) if edges else jnp.zeros((EDGE, chunk), F32)
    start = pl.multiple_of(EDGE + mine * rows, EDGE)
    padded[pl.ds(start, rows), :] = own[:rows, lanes].astype(F32)
    start = pl.multiple_of(EDGE + (1 - mine) * rows, EDGE)
    padded[pl.ds(start, rows), :] = got[:rows, :].astype(F32)
    total = jnp.zeros((size, chunk), F32)
    taps_at = step_lanes(width, chunk, step, mine)
    for j in range(taps.shape[1]):
        total = total + taps[0, j : j + 1, taps_at] * padded[EDGE - j : EDGE - j + size, :]
    keys = total.astype(BF16)
    kc2[:, lanes] = keys
    top[:, lanes] = total[:EDGE]
    cols = cum_rows.T
    after = jnp.exp(cols[size - 1 :, :] - cols)
    keys = keys.astype(F32)
    for h in range(heads):
        at = step * heads + h
        scaled = (keys[:, h * dim : (h + 1) * dim] * after[:, at : at + 1]).astype(BF16)
        ks2[:, at * dim : (at + 1) * dim] = scaled
        sums = dot(scaled, v2[:, at * dim : (at + 1) * dim], (0, 0))
        state[h * dim : (h + 1) * dim, :] = sums.astype(BF16)
    last = padded[EDGE + size - LEAD : EDGE + size, :]
    last = [last[:, h * dim : (h + 1) * dim] for h in range(heads)]
    if LEAD * heads < EDGE:
        last.append(jnp.zeros((EDGE - LEAD * heads, dim), F32))
    state[chunk:, :] = jnp.concatenate(last, 0).astype(BF16)


def join_kernel(got, own, own_cum, taps, *refs):
    *edges, kc2, v2, top, ks2, state, cum, padded = refs
    rows, heads = own_cum.shape[1], own_cum.shape[0] // PAIR
    mine = lax.rem(lax.axis_index("ctx"), PAIR)
    coded = got[2 * rows :, :].astype(F32)
    lines = heads * rows // coded.shape[1]
    row = coded[:lines] + coded[lines : 2 * lines] + coded[2 * lines : 3 * lines]
    per_line = heads // lines
    other_rows = jnp.concatenate(
        [
            row[h // per_line : h // per_line + 1, h % per_line * rows : (h % per_line + 1) * rows]
            for h in range(heads)
        ],
        0,
    )
    own_rows = half_rows(own_cum[...], mine, heads)
    front = jnp.where(mine == 0, own_rows, other_rows)
    back = jnp.where(mine == 0, other_rows, own_rows) + front[:, rows - 1 :]
    cum_rows = jnp.concatenate([front, back], 1)
    cum_rows = jnp.concatenate([cum_rows, jnp.zeros((8 - heads, PAIR * rows), F32)], 0)
    cum[...] = cum_rows
    join_step(0, got, own, taps, edges, cum_rows, kc2, v2, top, ks2, state, padded)


def join_next_kernel(step, _kc2, _v2, _top, _ks2, got, own, cum, taps, *refs):
    *edges, kc2, v2, top, ks2, state, padded = refs
    join_step(step, got, own, taps, edges, cum[...], kc2, v2, top, ks2, state, padded)


def mixing_of(cum_rows, cols, h, first=0):
    differ = cols[:, h : h + 1] - cum_rows[h : h + 1, :]
    at = lax.broadcasted_iota(jnp.int32, differ.shape, 1)
    causal = (lax.broadcasted_iota(jnp.int32, differ.shape, 0) >= at) & (at >= first)
    return jnp.where(causal, jnp.exp(jnp.where(causal, differ, 0.0)), 0.0)


def lead_mixing_of(cum_rows, cols, heads):
    wide = (cols.shape[0], heads * LEAD)
    lane = lax.broadcasted_iota(jnp.int32, wide, 1)
    late = jnp.zeros(wide, F32)
    for h in range(heads):
        late = jnp.where(lane // LEAD == h, cols[:, h : h + 1], late)
    early = jnp.concatenate([cum_rows[h : h + 1, :LEAD] for h in range(heads)], 1)
    causal = lax.broadcasted_iota(jnp.int32, wide, 0) >= lane % LEAD
    return jnp.where(causal, jnp.exp(jnp.where(causal, late - early, 0.0)), 0.0)


def block_diagonal(rows, dim, heads, first=0):
    wide = jnp.concatenate([rows] * heads, 0)
    head = lax.broadcasted_iota(jnp.int32, wide.shape, 0) // LEAD
    lane = lax.broadcasted_iota(jnp.int32, wide.shape, 1) // dim + first
    return jnp.where(head == lane, wide, 0.0).astype(BF16)


def local_kernel(got, own, kc2, v2, cum, q2, qs2, weights, inside, lead_mixing, lead_values):
    size, width = q2.shape
    heads, dim = weights.shape[0], width // weights.shape[0]
    rows = size // PAIR
    here, there = halves(rows)
    q2[here, :] = own[2 * rows : 3 * rows, :]
    q2[there, :] = got[...]
    cum_rows = cum[...]
    cols = cum_rows.T
    growth = jnp.exp(cols)
    lead_mixing[...] = lead_mixing_of(cum_rows, cols, heads)
    lead_values[...] = block_diagonal(v2[:EDGE, :].astype(F32)[:LEAD], dim, heads)
    for h in range(heads):
        lanes = slice(h * dim, (h + 1) * dim)
        qs2[:, lanes] = (q2[:, lanes].astype(F32) * growth[:, h : h + 1]).astype(BF16)
        scores = dot(q2[:, lanes], kc2[:, lanes], (1, 1))
        w = (scores * mixing_of(cum_rows, cols, h, LEAD)).astype(BF16)
        weights[h] = w
        inside[:, lanes] = dot(w, v2[:, lanes], (1, 0))


def unless(flag, block):
    return jnp.where(flag, jnp.zeros_like(block), block)


def attend_kernel(step, *refs):
    kc2, inside, q2, qs2, top, taps, lead_mixing, lead_values, before, *refs = refs
    kc2_whole, attended, lead_weights, reach = refs
    size, width = q2.shape
    dim = before.shape[1]
    heads = width // dim
    chunk = width // STEPS
    lanes = slice(step * chunk, (step + 1) * chunk)
    mine = lax.rem(lax.axis_index("ctx"), PAIR)
    start = lax.axis_index("ctx") < PAIR
    tail = unless(start, before[chunk:, :].astype(F32))
    reach[...] = jnp.zeros_like(reach)
    for h in range(chunk // dim):
        reach[LEAD : 2 * LEAD, h * dim : (h + 1) * dim] = tail[LEAD * h : LEAD * (h + 1)]
    fixed = top[: 2 * LEAD, lanes]
    taps_at = step_lanes(width, chunk, step, mine)
    for j in range(1, taps.shape[1]):
        fixed = fixed + taps[0, j : j + 1, taps_at] * reach[2 * LEAD - j : 4 * LEAD - j, :]
    rows = jnp.concatenate([fixed, top[2 * LEAD :, lanes]], 0)
    kc2_whole[:EDGE, lanes] = rows.astype(BF16)
    lead_keys = block_diagonal(fixed[:LEAD], dim, heads, step * chunk // dim)
    lead = (dot(q2[:, lanes], lead_keys, (1, 1)) * lead_mixing[...]).astype(BF16)
    lead_weights[...] = lead
    for h in range(chunk // dim):
        at = step * chunk // dim + h
        here = slice(at * dim, (at + 1) * dim)
        state = unless(start, before[h * dim : (h + 1) * dim, :])
        a = inside[:, here] + dot(lead, lead_values[:, here], (1, 0))
        attended[:, here] = a + dot(qs2[:, here], state, (1, 0))


def sums_kernel(dim, attended, own, got, g2, sums):
    size, width = attended.shape
    rows = size // PAIR
    here, there = halves(rows)
    g2[here, :] = own[3 * rows :, :]
    g2[there, :] = got[...]
    squares = jnp.zeros((size, dim), F32)
    products = jnp.zeros((size, dim), F32)
    for at in range(0, width, dim):
        a = attended[:, at : at + dim]
        squares = squares + a * a
        products = products + a * g2[:, at : at + dim].astype(F32)
    ones = jnp.ones((8, dim), BF16)
    both = jnp.concatenate([squares, products], 0)
    line = sum(dot(ones, part, (1, 1)) for part in split3(both))[:1]
    sums[...] = jnp.concatenate([line[:, :size], line[:, size:]], 0)


def grad_kernel(width_all, attended, q2, qs2, lead_mixing, lead_values, g2, *refs):
    *sums, scales, grad = refs[:-PARTS]
    adjoints = refs[-PARTS:]
    size, width = q2.shape
    dim = adjoints[0].shape[1]
    heads = width // dim
    total = sum(ref[...] for ref in sums[1:]) + sums[0][...]
    inverse = 1.0 / jnp.sqrt(total[0:1] / width_all + 1e-06)
    shift = total[1:2] / width_all * inverse
    both = jnp.concatenate([inverse, shift * inverse * inverse, jnp.zeros((6, size), F32)], 0)
    scales[...] = both
    both = both.T
    inverse, pull = both[:, 0:1], both[:, 1:2]
    for h in range(heads):
        lanes = slice(h * dim, (h + 1) * dim)
        d = (g2[:, lanes].astype(F32) * inverse - attended[:, lanes] * pull).astype(BF16)
        grad[:, lanes] = d
        part, at = divmod(h, heads // PARTS)
        adjoints[part][at * dim : (at + 1) * dim, :] = dot(qs2[:, lanes], d, (0, 0)).astype(BF16)
    scores = (dot(grad[...], lead_values[...], (1, 1)) * lead_mixing[...]).astype(BF16)
    tops = dot(scores, q2[...], (0, 0))
    per_part = heads // PARTS
    for i, adjoint in enumerate(adjoints):
        rows = [
            tops[LEAD * h : LEAD * (h + 1), h * dim : (h + 1) * dim]
            for h in range(i * per_part, (i + 1) * per_part)
        ]
        if LEAD * per_part < EDGE:
            rows.append(jnp.zeros((EDGE - LEAD * per_part, dim), F32))
        adjoint[width // PARTS :, :] = jnp.concatenate(rows, 0).astype(BF16)


def inner_grad_kernel(
    attended, scales, q2, kc2, v2, grad, weights, cum, *refs
):
    before, lead_weights = refs[:STEPS], refs[STEPS : 2 * STEPS]
    keep, send, partial, key_grad, vs2, normed = refs[2 * STEPS :]
    size, width = q2.shape
    dim = before[0].shape[1]
    heads = width // dim
    per_step = heads // STEPS
    start = lax.axis_index("ctx") < PAIR
    inverse = scales[...].T[:, 0:1]
    cum_rows = cum[...]
    cols = cum_rows.T
    growth = jnp.exp(cols)
    after = jnp.exp(cols[size - 1 :, :] - cols)
    for h in range(heads):
        lanes = slice(h * dim, (h + 1) * dim)
        vs2[:, lanes] = (v2[:, lanes].astype(F32) * after[:, h : h + 1]).astype(BF16)
        normed[:, lanes] = (attended[:, lanes] * inverse).astype(BF16)
        d = grad[:, lanes]
        scores = dot(d, v2[:, lanes], (1, 1)) * mixing_of(cum_rows, cols, h)
        scores = scores.astype(BF16)
        step, at = divmod(h, per_step)
        state = unless(start, before[step][at * dim : (at + 1) * dim, :])
        query_grad = dot(scores, kc2[:, lanes], (1, 0)) + growth[:, h : h + 1] * dot(
            d, state, (1, 1)
        )
        key_grad[:, lanes] = dot(scores, q2[:, lanes], (0, 0))
        partial[:, lanes] = query_grad + dot(weights[h], d, (0, 0))
    lead = sum(ref[...].astype(F32) for ref in lead_weights).astype(BF16)
    lead = dot(lead, grad[...], (0, 0))
    for h in range(heads):
        lanes = slice(h * dim, (h + 1) * dim)
        partial[:LEAD, lanes] = partial[:LEAD, lanes] + lead[LEAD * h : LEAD * (h + 1), lanes]
    here, there = halves(size // PAIR)
    keep[...] = normed[here, :]
    send[...] = normed[there, :]


def outer_grad_kernel(
    last, part, partial, key_grad, ks2, vs2, behind, more, taps, keep, send, padded, done
):
    size, width = partial.shape
    dim = behind.shape[1]
    heads = width // dim // PARTS
    chunk = width // PARTS
    mine = lax.rem(lax.axis_index("ctx"), PAIR)
    own = pl.ds(pl.multiple_of(mine * width + part * chunk, chunk), chunk)
    ends = lax.axis_index("ctx") >= last
    tops = unless(ends, behind[chunk:, :].astype(F32))
    for h in range(heads):
        at = part * heads + h
        lanes = slice(at * dim, (at + 1) * dim)
        here = slice(h * dim, (h + 1) * dim)
        state = unless(ends, behind[here, :])
        padded[:size, here] = key_grad[:, lanes] + dot(vs2[:, lanes], state, (1, 1))
        done[:, here] = partial[:, lanes] + dot(ks2[:, lanes], state, (1, 0))
        top = jnp.concatenate([tops[4 * h : 4 * h + 4], jnp.zeros((4, dim), F32)], 0)
        padded[size:, here] = top + more[:, lanes]
    total = done[...]
    for j in range(taps.shape[1]):
        total = total + taps[0, j : j + 1, own] * padded[j : j + size, :]
    done[...] = total
    here, there = halves(size // PAIR)
    first = lax.axis_index("pp") == 0
    keep[...] = unless(first, done[here, :]).astype(BF16)
    send[...] = unless(first, done[there, :]).astype(BF16)


def place_kernel(*refs):
    *pieces, out, sems = refs
    kept, got = pieces[: len(pieces) // 2], pieces[len(pieces) // 2 :]
    width = kept[0].shape[1]
    mine = lax.rem(lax.axis_index("ctx"), PAIR)
    pairs = []
    for half, parts in ((mine, kept), (1 - mine, got)):
        for i, part in enumerate(parts):
            start = pl.multiple_of((half * len(parts) + i) * width, width)
            pairs.append((part, out.at[0, :, pl.ds(start, width)]))
    for copy in copy_all(pairs, sems):
        copy.wait()


def placed(kept, got):
    pieces = kept + got
    rows = kept[0].shape[0]
    return call(
        place_kernel,
        [shape((1, rows, sum(piece.shape[1] for piece in pieces)), BF16)],
        *pieces,
        scratch=[pltpu.SemaphoreType.DMA((len(pieces),))],
        out_hbm=True,
    )[0]


def turned(block, axis, distance):
    count = lax.axis_size(axis)
    return lax.ppermute(block, axis, [(i, (i + distance) % count) for i in range(count)])


def swapped(block):
    return lax.ppermute(block, "ctx", [(i, i ^ 1) for i in range(lax.axis_size("ctx"))])


def to_earlier_section(block, flip):
    blocks, sections = lax.axis_size("ctx"), lax.axis_size("pp")
    route = [
        (c * sections + p, (c ^ flip) * sections + (p - 1) % sections)
        for c in range(blocks)
        for p in range(sections)
    ]
    return lax.ppermute(block, ("ctx", "pp"), route)


def summed_parts(part):
    blocks, count = lax.axis_size("ctx"), lax.axis_size("tp")

    def neighbour(block):
        return lax.ppermute(block, "tp", [(i, i ^ 1) for i in range(count)])

    def fetched(block, *ways):
        route = [
            (c * count + t, (c ^ ways[t % len(ways)][0]) * count + (t + ways[t % len(ways)][1]) % count)
            for c in range(blocks)
            for t in range(count)
        ]
        return lax.ppermute(block, ("ctx", "tp"), route)

    pair = part + neighbour(part)
    ways = [(1, 0)] + [(flip, k) for k in range(2, count, 2) for flip in (0, 1)]
    parts = [pair, fetched(pair, ways[-1])]
    shared = [fetched(pair, *ways[i : i + 2]) for i in range(0, len(ways) - 1, 2)]
    for block in shared:
        parts += [block, neighbour(block)]
    return parts


def per_device(queries, key_input, values, log_decay, conv_weight, out_grad):
    rows, width = queries.shape[1], queries.shape[2] // PAIR
    heads = log_decay.shape[2] // PAIR
    dim = width // heads
    size = PAIR * rows
    blocks = lax.axis_size("ctx")
    supers = blocks // PAIR
    width_all = queries.shape[2] * lax.axis_size("tp")
    log_decay = jnp.swapaxes(log_decay, 1, 2)
    arrays = (queries, key_input, values, out_grad, log_decay)
    queries, key_input, values, out_grad, decays = (
        pltpu.with_memory_space_constraint(x, pltpu.HBM) for x in arrays
    )

    step_width = width // STEPS
    *packed, own_cum = call(
        pack_kernel,
        [shape((2 * rows + EDGE, step_width), BF16)]
        + [shape((2 * rows, step_width), BF16)] * (STEPS - 1)
        + [shape((PAIR * heads, rows), F32)],
        key_input, values, decays,
        scratch=[pltpu.VMEM(log_decay.shape, F32), pltpu.SemaphoreType.DMA((1 + 2 * STEPS,))],
        hbm=range(3),
    )
    got = [swapped(part) for part in packed]
    edges = ()
    if supers > 2:
        edge = arrays[1][0, rows - EDGE :]
        near = lax.ppermute(edge[:, :width], "ctx", [(i, i + 1) for i in range(1, blocks - 1, 2)])
        far = lax.ppermute(edge[:, width:], "ctx", [(i, i + 2) for i in range(1, blocks - 2, 2)])
        edges = (near + far,)
    second, third, own = call(
        pack_more_kernel,
        [shape((rows, width), BF16)] * 2 + [shape((4 * rows, width), BF16)],
        queries, key_input, values, out_grad, packed[0][2 * rows :],
        scratch=[pltpu.SemaphoreType.DMA((6,))],
        hbm=range(4),
    )
    got_q, got_g = swapped(second), swapped(third)
    joined = [
        shape((size, width), BF16), shape((size, width), BF16), shape((EDGE, width), F32),
        shape((size, width), BF16), shape((step_width + EDGE, dim), BF16),
    ]
    room = [pltpu.VMEM((EDGE + size, step_width), F32)]
    kc2, v2, top, ks2, state, cum = call(
        join_kernel,
        joined + [shape((8, size), F32)],
        got[0], own, own_cum, conv_weight, *edges,
        scratch=room,
    )
    states = [state]
    for step in range(1, STEPS):
        kc2, v2, top, ks2, state = call(
            lambda *refs, step=step: join_next_kernel(step, *refs),
            joined,
            kc2, v2, top, ks2, got[step], own, cum, conv_weight, *edges,
            scratch=room,
            alias=((0, 0), (1, 1), (2, 2), (3, 3)),
        )
        states.append(state)
    carry = jnp.repeat(jnp.exp(cum[:heads, -1]), dim)[:, None]
    pair_index = lax.axis_index("ctx") // PAIR
    before = []
    for step, state in enumerate(states):
        moved = turned(state, "ctx", PAIR)
        for _ in range(supers - 2):
            earlier = unless(pair_index == 0, moved[:step_width]).astype(F32)
            earlier = carry[step * step_width : (step + 1) * step_width] * earlier
            earlier = (state[:step_width].astype(F32) + earlier).astype(BF16)
            moved = jnp.concatenate([turned(earlier, "ctx", PAIR), moved[step_width:]], 0)
        before.append(moved)

    q2, qs2, weights, inside, lead_mixing, lead_values = call(
        local_kernel,
        [shape((size, width), BF16)] * 2
        + [shape((heads, size, size), BF16), shape((size, width), F32)]
        + [shape((size, LEAD * heads), F32), shape((LEAD * heads, width), BF16)],
        got_q, own, kc2, v2, cum,
        flops=4 * heads * size * size * dim,
    )
    lead_weights = []
    for step in range(STEPS):
        kc2, inside, lead = call(
            lambda *refs, step=step: attend_kernel(step, *refs),
            [shape(kc2.shape, BF16), shape((size, width), F32), shape((size, LEAD * heads), BF16)],
            kc2, inside, q2, qs2, top, conv_weight, lead_mixing, lead_values, before[step],
            scratch=[pltpu.VMEM((4 * LEAD, step_width), F32)],
            alias=((0, 0), (1, 1)),
        )
        lead_weights.append(lead)
    attended = inside
    g2, sums = call(
        lambda *refs: sums_kernel(dim, *refs),
        [shape((size, width), BF16), shape((2, size), F32)],
        attended, own, got_g,
    )
    parts = summed_parts(sums)
    chunk = width // PARTS
    scales, grad, *adjoints = call(
        lambda *refs: grad_kernel(width_all, *refs),
        [shape((8, size), F32), shape((size, width), BF16)]
        + [shape((chunk + EDGE, dim), BF16)] * PARTS,
        attended, q2, qs2, lead_mixing, lead_values, g2, *parts,
    )
    last_pair = pair_index == supers - 1
    behind = []
    for i, adjoint in enumerate(adjoints):
        moved = turned(adjoint, "ctx", -PAIR)
        for _ in range(supers - 2):
            later = unless(last_pair, moved[:chunk]).astype(F32)
            joined = adjoint[:chunk].astype(F32) + carry[i * chunk : (i + 1) * chunk] * later
            state = turned(joined.astype(BF16), "ctx", -PAIR)
            moved = jnp.concatenate([state, moved[chunk:]], 0)
        behind.append(moved)
    more = jnp.zeros((8, width), F32)
    if supers > 2:
        after = jnp.exp(cum[:heads, -1:] - cum[:heads, :8])
        states = jnp.concatenate([part[:chunk] for part in behind], 0)
        state_part = jnp.einsum(
            "shv,hkv->shk",
            v2[:8].reshape(8, heads, dim),
            unless(last_pair, states).reshape(heads, dim, dim),
            preferred_element_type=F32,
        )
        more = turned((after.T[:, :, None] * state_part).reshape(8, width), "ctx", -PAIR)
        more = unless(last_pair, more)

    keep, send, partial, key_grad, vs2 = call(
        inner_grad_kernel,
        [shape((rows, width), BF16)] * 2
        + [shape((size, width), F32)] * 2
        + [shape((size, width), BF16)],
        attended, scales, q2, kc2, v2, grad, weights, cum, *before, *lead_weights,
        scratch=[pltpu.VMEM((size, width), BF16)],
        flops=10 * heads * size * size * dim,
    )
    out_keep, out_send = keep, send
    kept, got = [], []
    for i in range(PARTS):
        keep, send = call(
            lambda *refs, i=i: outer_grad_kernel(blocks - PAIR, i, *refs),
            [shape((rows, chunk), BF16)] * 2,
            partial, key_grad, ks2, vs2, behind[i], more, conv_weight,
            scratch=[pltpu.VMEM((size + 8, chunk), F32), pltpu.VMEM((size, chunk), F32)],
        )
        kept.append(to_earlier_section(keep, 0))
        got.append(to_earlier_section(send, 1))
    input_next = placed(kept, got)
    return (placed([out_keep], [swapped(out_send)]), input_next)


def solution(mesh):
    placed = (
        P("pp", "ctx", "tp"),
        P("pp", "ctx", "tp"),
        P("pp", "ctx", "tp"),
        P("pp", "ctx", "tp"),
        P("pp", None, "tp"),
        P("pp", "ctx", "tp"),
    )
    return jax.shard_map(
        per_device,
        mesh=mesh,
        in_specs=placed,
        out_specs=(P("pp", "ctx", "tp"), P("pp", "ctx", "tp")),
        check_vma=False,
    )
```

```python
import jax
import jax.numpy as jnp
from jax import lax
from jax.experimental import pallas as pl
from jax.experimental.pallas import tpu as pltpu
from jax.sharding import PartitionSpec as P

F32 = jnp.float32
BF16 = jnp.bfloat16
PAIR = 2
EDGE = 16
LEAD = 4
STEPS = 2
PARTS = 1


def call(kernel, outs, *args, scratch=(), flops=0, hbm=(), out_hbm=False, alias=()):
    vmem = pl.BlockSpec(memory_space=pltpu.VMEM)
    moved = sum(a.size * a.dtype.itemsize for a in args) + sum(
        s.size * s.dtype.itemsize for s in outs
    )
    return pl.pallas_call(
        kernel,
        out_shape=outs,
        in_specs=[
            pl.BlockSpec(memory_space=pltpu.HBM) if i in hbm else vmem for i in range(len(args))
        ],
        out_specs=[pl.BlockSpec(memory_space=pltpu.HBM) if out_hbm else vmem] * len(outs),
        scratch_shapes=scratch,
        input_output_aliases=dict(alias),
        compiler_params=pltpu.CompilerParams(vmem_limit_bytes=32 * 1024 * 1024),
        cost_estimate=pl.CostEstimate(flops=flops, bytes_accessed=moved, transcendentals=0),
    )(*args)


def shape(dims, dtype):
    return jax.ShapeDtypeStruct(dims, dtype)


def halves(size):
    mine = lax.rem(lax.axis_index("ctx"), PAIR)
    return (
        pl.ds(pl.multiple_of(mine * size, size), size),
        pl.ds(pl.multiple_of((1 - mine) * size, size), size),
    )


def dot(a, b, contract):
    return lax.dot_general(a, b, ((contract[:1], contract[1:]), ((), ())), preferred_element_type=F32)


def split3(x):
    hi = x.astype(BF16)
    rest = x - hi.astype(F32)
    mid = rest.astype(BF16)
    return hi, mid, (rest - mid.astype(F32)).astype(BF16)


def half_rows(rows, mine, heads):
    return jnp.where(mine == 0, rows[:heads], rows[heads:])


def copy_all(pairs, sems):
    copies = [pltpu.make_async_copy(src, to, sems.at[i]) for i, (src, to) in enumerate(pairs)]
    for copy in copies:
        copy.start()
    return copies


def step_lanes(width, chunk, step, mine):
    return pl.ds(pl.multiple_of(mine * width + step * chunk, chunk), chunk)


def pack_kernel(k, v, log_decay, *refs):
    *outs, cum, decays, sems = refs
    first = outs[0]
    rows, heads = k.shape[1], log_decay.shape[1] // PAIR
    mine = lax.rem(lax.axis_index("ctx"), PAIR)
    chunk = first.shape[1]
    pairs = [(log_decay, decays)]
    for step, out in enumerate(outs):
        other = step_lanes(k.shape[2] // PAIR, chunk, step, 1 - mine)
        for i, ref in enumerate((k, v)):
            pairs.append((ref.at[0, :, other], out.at[i * rows : (i + 1) * rows, :]))
    copies = copy_all(pairs, sems)
    copies[0].wait()
    upto = lax.broadcasted_iota(jnp.int32, (rows, rows), 0) <= lax.broadcasted_iota(
        jnp.int32, (rows, rows), 1
    )
    upto = upto.astype(F32).astype(BF16)
    sums = sum(dot(part, upto, (1, 0)) for part in split3(decays[0]))
    cum[...] = sums
    line = chunk // rows
    parts = [
        jnp.concatenate([part[h : h + 1] for h in range(at, at + line)], 1).astype(F32)
        for part in split3(half_rows(sums, 1 - mine, heads))
        for at in range(0, heads, line)
    ]
    parts.append(jnp.zeros((EDGE - len(parts), chunk), F32))
    first[2 * rows :, :] = jnp.concatenate(parts, 0).astype(BF16)
    for copy in copies[1:]:
        copy.wait()


def pack_more_kernel(q, k, v, g, _, second, third, own, sems):
    rows = q.shape[1]
    lanes_own, other = halves(q.shape[2] // PAIR)
    pairs = [(q.at[0, :, other], second), (g.at[0, :, other], third)]
    pairs += [
        (ref.at[0, :, lanes_own], own.at[i * rows : (i + 1) * rows, :])
        for i, ref in enumerate((k, v, q, g))
    ]
    for copy in copy_all(pairs, sems):
        copy.wait()


def join_step(step, got, own, taps, edges, cum_rows, kc2, v2, top, ks2, state, padded):
    size, width = kc2.shape
    rows, chunk = size // PAIR, got.shape[1]
    dim = state.shape[1]
    heads = chunk // dim
    here, there = halves(rows)
    mine = lax.rem(lax.axis_index("ctx"), PAIR)
    lanes = slice(step * chunk, (step + 1) * chunk)
    v2[here, lanes] = own[rows : 2 * rows, lanes]
    v2[there, lanes] = got[rows : 2 * rows, :]
    padded[:EDGE, :] = edges[0][:, lanes].astype(F32) if edges else jnp.zeros((EDGE, chunk), F32)
    start = pl.multiple_of(EDGE + mine * rows, EDGE)
    padded[pl.ds(start, rows), :] = own[:rows, lanes].astype(F32)
    start = pl.multiple_of(EDGE + (1 - mine) * rows, EDGE)
    padded[pl.ds(start, rows), :] = got[:rows, :].astype(F32)
    total = jnp.zeros((size, chunk), F32)
    taps_at = step_lanes(width, chunk, step, mine)
    for j in range(taps.shape[1]):
        total = total + taps[0, j : j + 1, taps_at] * padded[EDGE - j : EDGE - j + size, :]
    keys = total.astype(BF16)
    kc2[:, lanes] = keys
    top[:, lanes] = total[:EDGE]
    cols = cum_rows.T
    after = jnp.exp(cols[size - 1 :, :] - cols)
    keys = keys.astype(F32)
    for h in range(heads):
        at = step * heads + h
        scaled = (keys[:, h * dim : (h + 1) * dim] * after[:, at : at + 1]).astype(BF16)
        ks2[:, at * dim : (at + 1) * dim] = scaled
        sums = dot(scaled, v2[:, at * dim : (at + 1) * dim], (0, 0))
        state[h * dim : (h + 1) * dim, :] = sums.astype(BF16)
    last = padded[EDGE + size - LEAD : EDGE + size, :]
    last = [last[:, h * dim : (h + 1) * dim] for h in range(heads)]
    if LEAD * heads < EDGE:
        last.append(jnp.zeros((EDGE - LEAD * heads, dim), F32))
    state[chunk:, :] = jnp.concatenate(last, 0).astype(BF16)


def join_kernel(got, own, own_cum, taps, *refs):
    *edges, kc2, v2, top, ks2, state, cum, padded = refs
    rows, heads = own_cum.shape[1], own_cum.shape[0] // PAIR
    mine = lax.rem(lax.axis_index("ctx"), PAIR)
    coded = got[2 * rows :, :].astype(F32)
    lines = heads * rows // coded.shape[1]
    row = coded[:lines] + coded[lines : 2 * lines] + coded[2 * lines : 3 * lines]
    per_line = heads // lines
    other_rows = jnp.concatenate(
        [
            row[h // per_line : h // per_line + 1, h % per_line * rows : (h % per_line + 1) * rows]
            for h in range(heads)
        ],
        0,
    )
    own_rows = half_rows(own_cum[...], mine, heads)
    front = jnp.where(mine == 0, own_rows, other_rows)
    back = jnp.where(mine == 0, other_rows, own_rows) + front[:, rows - 1 :]
    cum_rows = jnp.concatenate([front, back], 1)
    cum_rows = jnp.concatenate([cum_rows, jnp.zeros((8 - heads, PAIR * rows), F32)], 0)
    cum[...] = cum_rows
    join_step(0, got, own, taps, edges, cum_rows, kc2, v2, top, ks2, state, padded)


def join_next_kernel(step, _kc2, _v2, _top, _ks2, got, own, cum, taps, *refs):
    *edges, kc2, v2, top, ks2, state, padded = refs
    join_step(step, got, own, taps, edges, cum[...], kc2, v2, top, ks2, state, padded)


def mixing_of(cum_rows, cols, h, first=0):
    differ = cols[:, h : h + 1] - cum_rows[h : h + 1, :]
    at = lax.broadcasted_iota(jnp.int32, differ.shape, 1)
    causal = (lax.broadcasted_iota(jnp.int32, differ.shape, 0) >= at) & (at >= first)
    return jnp.where(causal, jnp.exp(jnp.where(causal, differ, 0.0)), 0.0)


def lead_mixing_of(cum_rows, cols, heads):
    wide = (cols.shape[0], heads * LEAD)
    lane = lax.broadcasted_iota(jnp.int32, wide, 1)
    late = jnp.zeros(wide, F32)
    for h in range(heads):
        late = jnp.where(lane // LEAD == h, cols[:, h : h + 1], late)
    early = jnp.concatenate([cum_rows[h : h + 1, :LEAD] for h in range(heads)], 1)
    causal = lax.broadcasted_iota(jnp.int32, wide, 0) >= lane % LEAD
    return jnp.where(causal, jnp.exp(jnp.where(causal, late - early, 0.0)), 0.0)


def block_diagonal(rows, dim, heads, first=0):
    wide = jnp.concatenate([rows] * heads, 0)
    head = lax.broadcasted_iota(jnp.int32, wide.shape, 0) // LEAD
    lane = lax.broadcasted_iota(jnp.int32, wide.shape, 1) // dim + first
    return jnp.where(head == lane, wide, 0.0).astype(BF16)


def local_kernel(got, own, kc2, v2, cum, q2, qs2, weights, inside, lead_mixing, lead_values):
    size, width = q2.shape
    heads, dim = weights.shape[0], width // weights.shape[0]
    rows = size // PAIR
    here, there = halves(rows)
    q2[here, :] = own[2 * rows : 3 * rows, :]
    q2[there, :] = got[...]
    cum_rows = cum[...]
    cols = cum_rows.T
    growth = jnp.exp(cols)
    lead_mixing[...] = lead_mixing_of(cum_rows, cols, heads)
    lead_values[...] = block_diagonal(v2[:EDGE, :].astype(F32)[:LEAD], dim, heads)
    for h in range(heads):
        lanes = slice(h * dim, (h + 1) * dim)
        qs2[:, lanes] = (q2[:, lanes].astype(F32) * growth[:, h : h + 1]).astype(BF16)
        scores = dot(q2[:, lanes], kc2[:, lanes], (1, 1))
        w = (scores * mixing_of(cum_rows, cols, h, LEAD)).astype(BF16)
        weights[h] = w
        inside[:, lanes] = dot(w, v2[:, lanes], (1, 0))


def unless(flag, block):
    return jnp.where(flag, jnp.zeros_like(block), block)


def attend_kernel(step, *refs):
    kc2, inside, q2, qs2, top, taps, lead_mixing, lead_values, before, *refs = refs
    kc2_whole, attended, lead_weights, reach = refs
    size, width = q2.shape
    dim = before.shape[1]
    heads = width // dim
    chunk = width // STEPS
    lanes = slice(step * chunk, (step + 1) * chunk)
    mine = lax.rem(lax.axis_index("ctx"), PAIR)
    start = lax.axis_index("ctx") < PAIR
    tail = unless(start, before[chunk:, :].astype(F32))
    reach[...] = jnp.zeros_like(reach)
    for h in range(chunk // dim):
        reach[LEAD : 2 * LEAD, h * dim : (h + 1) * dim] = tail[LEAD * h : LEAD * (h + 1)]
    fixed = top[: 2 * LEAD, lanes]
    taps_at = step_lanes(width, chunk, step, mine)
    for j in range(1, taps.shape[1]):
        fixed = fixed + taps[0, j : j + 1, taps_at] * reach[2 * LEAD - j : 4 * LEAD - j, :]
    rows = jnp.concatenate([fixed, top[2 * LEAD :, lanes]], 0)
    kc2_whole[:EDGE, lanes] = rows.astype(BF16)
    lead_keys = block_diagonal(fixed[:LEAD], dim, heads, step * chunk // dim)
    lead = (dot(q2[:, lanes], lead_keys, (1, 1)) * lead_mixing[...]).astype(BF16)
    lead_weights[...] = lead
    for h in range(chunk // dim):
        at = step * chunk // dim + h
        here = slice(at * dim, (at + 1) * dim)
        state = unless(start, before[h * dim : (h + 1) * dim, :])
        a = inside[:, here] + dot(lead, lead_values[:, here], (1, 0))
        attended[:, here] = a + dot(qs2[:, here], state, (1, 0))


def sums_kernel(dim, attended, own, got, g2, sums):
    size, width = attended.shape
    rows = size // PAIR
    here, there = halves(rows)
    g2[here, :] = own[3 * rows :, :]
    g2[there, :] = got[...]
    squares = jnp.zeros((size, dim), F32)
    products = jnp.zeros((size, dim), F32)
    for at in range(0, width, dim):
        a = attended[:, at : at + dim]
        squares = squares + a * a
        products = products + a * g2[:, at : at + dim].astype(F32)
    ones = jnp.ones((8, dim), BF16)
    both = jnp.concatenate([squares, products], 0)
    line = sum(dot(ones, part, (1, 1)) for part in split3(both))[:1]
    sums[...] = jnp.concatenate([line[:, :size], line[:, size:]], 0)


def grad_kernel(width_all, attended, q2, qs2, lead_mixing, lead_values, g2, *refs):
    *sums, scales, grad = refs[:-PARTS]
    adjoints = refs[-PARTS:]
    size, width = q2.shape
    dim = adjoints[0].shape[1]
    heads = width // dim
    total = sum(ref[...] for ref in sums[1:]) + sums[0][...]
    inverse = 1.0 / jnp.sqrt(total[0:1] / width_all + 1e-06)
    shift = total[1:2] / width_all * inverse
    both = jnp.concatenate([inverse, shift * inverse * inverse, jnp.zeros((6, size), F32)], 0)
    scales[...] = both
    both = both.T
    inverse, pull = both[:, 0:1], both[:, 1:2]
    for h in range(heads):
        lanes = slice(h * dim, (h + 1) * dim)
        d = (g2[:, lanes].astype(F32) * inverse - attended[:, lanes] * pull).astype(BF16)
        grad[:, lanes] = d
        part, at = divmod(h, heads // PARTS)
        adjoints[part][at * dim : (at + 1) * dim, :] = dot(qs2[:, lanes], d, (0, 0)).astype(BF16)
    scores = (dot(grad[...], lead_values[...], (1, 1)) * lead_mixing[...]).astype(BF16)
    tops = dot(scores, q2[...], (0, 0))
    per_part = heads // PARTS
    for i, adjoint in enumerate(adjoints):
        rows = [
            tops[LEAD * h : LEAD * (h + 1), h * dim : (h + 1) * dim]
            for h in range(i * per_part, (i + 1) * per_part)
        ]
        if LEAD * per_part < EDGE:
            rows.append(jnp.zeros((EDGE - LEAD * per_part, dim), F32))
        adjoint[width // PARTS :, :] = jnp.concatenate(rows, 0).astype(BF16)


def inner_grad_kernel(
    attended, scales, q2, kc2, v2, grad, weights, cum, *refs
):
    before, lead_weights = refs[:STEPS], refs[STEPS : 2 * STEPS]
    keep, send, partial, key_grad, vs2, normed = refs[2 * STEPS :]
    size, width = q2.shape
    dim = before[0].shape[1]
    heads = width // dim
    per_step = heads // STEPS
    start = lax.axis_index("ctx") < PAIR
    inverse = scales[...].T[:, 0:1]
    cum_rows = cum[...]
    cols = cum_rows.T
    growth = jnp.exp(cols)
    after = jnp.exp(cols[size - 1 :, :] - cols)
    for h in range(heads):
        lanes = slice(h * dim, (h + 1) * dim)
        vs2[:, lanes] = (v2[:, lanes].astype(F32) * after[:, h : h + 1]).astype(BF16)
        normed[:, lanes] = (attended[:, lanes] * inverse).astype(BF16)
        d = grad[:, lanes]
        scores = dot(d, v2[:, lanes], (1, 1)) * mixing_of(cum_rows, cols, h)
        scores = scores.astype(BF16)
        step, at = divmod(h, per_step)
        state = unless(start, before[step][at * dim : (at + 1) * dim, :])
        query_grad = dot(scores, kc2[:, lanes], (1, 0)) + growth[:, h : h + 1] * dot(
            d, state, (1, 1)
        )
        key_grad[:, lanes] = dot(scores, q2[:, lanes], (0, 0))
        partial[:, lanes] = query_grad + dot(weights[h], d, (0, 0))
    lead = sum(ref[...].astype(F32) for ref in lead_weights).astype(BF16)
    lead = dot(lead, grad[...], (0, 0))
    for h in range(heads):
        lanes = slice(h * dim, (h + 1) * dim)
        partial[:LEAD, lanes] = partial[:LEAD, lanes] + lead[LEAD * h : LEAD * (h + 1), lanes]
    here, there = halves(size // PAIR)
    keep[...] = normed[here, :]
    send[...] = normed[there, :]


def outer_grad_kernel(
    last, part, partial, key_grad, ks2, vs2, behind, more, taps, keep, send, padded, done
):
    size, width = partial.shape
    dim = behind.shape[1]
    heads = width // dim // PARTS
    chunk = width // PARTS
    mine = lax.rem(lax.axis_index("ctx"), PAIR)
    own = pl.ds(pl.multiple_of(mine * width + part * chunk, chunk), chunk)
    ends = lax.axis_index("ctx") >= last
    tops = unless(ends, behind[chunk:, :].astype(F32))
    for h in range(heads):
        at = part * heads + h
        lanes = slice(at * dim, (at + 1) * dim)
        here = slice(h * dim, (h + 1) * dim)
        state = unless(ends, behind[here, :])
        padded[:size, here] = key_grad[:, lanes] + dot(vs2[:, lanes], state, (1, 1))
        done[:, here] = partial[:, lanes] + dot(ks2[:, lanes], state, (1, 0))
        top = jnp.concatenate([tops[4 * h : 4 * h + 4], jnp.zeros((4, dim), F32)], 0)
        padded[size:, here] = top + more[:, lanes]
    total = done[...]
    for j in range(taps.shape[1]):
        total = total + taps[0, j : j + 1, own] * padded[j : j + size, :]
    done[...] = total
    here, there = halves(size // PAIR)
    first = lax.axis_index("pp") == 0
    keep[...] = unless(first, done[here, :]).astype(BF16)
    send[...] = unless(first, done[there, :]).astype(BF16)


def place_kernel(count, *refs):
    pieces, outs, sems = refs[: -1 - count], refs[-1 - count : -1], refs[-1]
    each = len(pieces) // count
    mine = lax.rem(lax.axis_index("ctx"), PAIR)
    pairs = []
    for i, out in enumerate(outs):
        parts = pieces[i * each : (i + 1) * each]
        width = parts[0].shape[1]
        for j, part in enumerate(parts):
            half = mine if j < each // 2 else 1 - mine
            start = pl.multiple_of((half * (each // 2) + j % (each // 2)) * width, width)
            pairs.append((part, out.at[0, :, pl.ds(start, width)]))
    for copy in copy_all(pairs, sems):
        copy.wait()


def placed(*results):
    pieces = [piece for kept, got in results for piece in kept + got]
    rows = pieces[0].shape[0]
    return call(
        lambda *refs: place_kernel(len(results), *refs),
        [
            shape((1, rows, sum(piece.shape[1] for piece in kept + got)), BF16)
            for kept, got in results
        ],
        *pieces,
        scratch=[pltpu.SemaphoreType.DMA((len(pieces),))],
        out_hbm=True,
    )


def turned(block, axis, distance):
    count = lax.axis_size(axis)
    return lax.ppermute(block, axis, [(i, (i + distance) % count) for i in range(count)])


def swapped(block):
    return lax.ppermute(block, "ctx", [(i, i ^ 1) for i in range(lax.axis_size("ctx"))])


def to_earlier_section(block, flip):
    blocks, sections = lax.axis_size("ctx"), lax.axis_size("pp")
    route = [
        (c * sections + p, (c ^ flip) * sections + (p - 1) % sections)
        for c in range(blocks)
        for p in range(sections)
    ]
    return lax.ppermute(block, ("ctx", "pp"), route)


def summed_parts(part):
    blocks, count = lax.axis_size("ctx"), lax.axis_size("tp")

    def neighbour(block):
        return lax.ppermute(block, "tp", [(i, i ^ 1) for i in range(count)])

    def fetched(block, *ways):
        route = [
            (c * count + t, (c ^ ways[t % len(ways)][0]) * count + (t + ways[t % len(ways)][1]) % count)
            for c in range(blocks)
            for t in range(count)
        ]
        return lax.ppermute(block, ("ctx", "tp"), route)

    pair = part + neighbour(part)
    ways = [(1, 0)] + [(flip, k) for k in range(2, count, 2) for flip in (0, 1)]
    shared = [fetched(pair, *ways[i : i + 2]) for i in range(0, len(ways) - 1, 2)]
    parts = [pair, fetched(pair, ways[-1])]
    for block in shared:
        parts += [block, neighbour(block)]
    return parts


def per_device(queries, key_input, values, log_decay, conv_weight, out_grad):
    rows, width = queries.shape[1], queries.shape[2] // PAIR
    heads = log_decay.shape[2] // PAIR
    dim = width // heads
    size = PAIR * rows
    blocks = lax.axis_size("ctx")
    supers = blocks // PAIR
    width_all = queries.shape[2] * lax.axis_size("tp")
    log_decay = jnp.swapaxes(log_decay, 1, 2)
    arrays = (queries, key_input, values, out_grad, log_decay)
    queries, key_input, values, out_grad, decays = (
        pltpu.with_memory_space_constraint(x, pltpu.HBM) for x in arrays
    )

    step_width = width // STEPS
    *packed, own_cum = call(
        pack_kernel,
        [shape((2 * rows + EDGE, step_width), BF16)]
        + [shape((2 * rows, step_width), BF16)] * (STEPS - 1)
        + [shape((PAIR * heads, rows), F32)],
        key_input, values, decays,
        scratch=[pltpu.VMEM(log_decay.shape, F32), pltpu.SemaphoreType.DMA((1 + 2 * STEPS,))],
        hbm=range(3),
    )
    got = [swapped(part) for part in packed]
    edges = ()
    if supers > 2:
        edge = arrays[1][0, rows - EDGE :]
        near = lax.ppermute(edge[:, :width], "ctx", [(i, i + 1) for i in range(1, blocks - 1, 2)])
        far = lax.ppermute(edge[:, width:], "ctx", [(i, i + 2) for i in range(1, blocks - 2, 2)])
        edges = (near + far,)
    second, third, own = call(
        pack_more_kernel,
        [shape((rows, width), BF16)] * 2 + [shape((4 * rows, width), BF16)],
        queries, key_input, values, out_grad, packed[0][2 * rows :],
        scratch=[pltpu.SemaphoreType.DMA((6,))],
        hbm=range(4),
    )
    got_q, got_g = swapped(second), swapped(third)
    joined = [
        shape((size, width), BF16), shape((size, width), BF16), shape((EDGE, width), F32),
        shape((size, width), BF16), shape((step_width + EDGE, dim), BF16),
    ]
    room = [pltpu.VMEM((EDGE + size, step_width), F32)]
    kc2, v2, top, ks2, state, cum = call(
        join_kernel,
        joined + [shape((8, size), F32)],
        got[0], own, own_cum, conv_weight, *edges,
        scratch=room,
    )
    states = [state]
    for step in range(1, STEPS):
        kc2, v2, top, ks2, state = call(
            lambda *refs, step=step: join_next_kernel(step, *refs),
            joined,
            kc2, v2, top, ks2, got[step], own, cum, conv_weight, *edges,
            scratch=room,
            alias=((0, 0), (1, 1), (2, 2), (3, 3)),
        )
        states.append(state)
    carry = jnp.repeat(jnp.exp(cum[:heads, -1]), dim)[:, None]
    pair_index = lax.axis_index("ctx") // PAIR
    before = []
    for step, state in enumerate(states):
        moved = turned(state, "ctx", PAIR)
        for _ in range(supers - 2):
            earlier = unless(pair_index == 0, moved[:step_width]).astype(F32)
            earlier = carry[step * step_width : (step + 1) * step_width] * earlier
            earlier = (state[:step_width].astype(F32) + earlier).astype(BF16)
            moved = jnp.concatenate([turned(earlier, "ctx", PAIR), moved[step_width:]], 0)
        before.append(moved)

    q2, qs2, weights, inside, lead_mixing, lead_values = call(
        local_kernel,
        [shape((size, width), BF16)] * 2
        + [shape((heads, size, size), BF16), shape((size, width), F32)]
        + [shape((size, LEAD * heads), F32), shape((LEAD * heads, width), BF16)],
        got_q, own, kc2, v2, cum,
        flops=4 * heads * size * size * dim,
    )
    lead_weights = []
    for step in range(STEPS):
        kc2, inside, lead = call(
            lambda *refs, step=step: attend_kernel(step, *refs),
            [shape(kc2.shape, BF16), shape((size, width), F32), shape((size, LEAD * heads), BF16)],
            kc2, inside, q2, qs2, top, conv_weight, lead_mixing, lead_values, before[step],
            scratch=[pltpu.VMEM((4 * LEAD, step_width), F32)],
            alias=((0, 0), (1, 1)),
        )
        lead_weights.append(lead)
    attended = inside
    g2, sums = call(
        lambda *refs: sums_kernel(dim, *refs),
        [shape((size, width), BF16), shape((2, size), F32)],
        attended, own, got_g,
    )
    parts = summed_parts(sums)
    chunk = width // PARTS
    scales, grad, *adjoints = call(
        lambda *refs: grad_kernel(width_all, *refs),
        [shape((8, size), F32), shape((size, width), BF16)]
        + [shape((chunk + EDGE, dim), BF16)] * PARTS,
        attended, q2, qs2, lead_mixing, lead_values, g2, *parts,
    )
    last_pair = pair_index == supers - 1
    behind = []
    for i, adjoint in enumerate(adjoints):
        moved = turned(adjoint, "ctx", -PAIR)
        for _ in range(supers - 2):
            later = unless(last_pair, moved[:chunk]).astype(F32)
            joined = adjoint[:chunk].astype(F32) + carry[i * chunk : (i + 1) * chunk] * later
            state = turned(joined.astype(BF16), "ctx", -PAIR)
            moved = jnp.concatenate([state, moved[chunk:]], 0)
        behind.append(moved)
    more = jnp.zeros((8, width), F32)
    if supers > 2:
        after = jnp.exp(cum[:heads, -1:] - cum[:heads, :8])
        states = jnp.concatenate([part[:chunk] for part in behind], 0)
        state_part = jnp.einsum(
            "shv,hkv->shk",
            v2[:8].reshape(8, heads, dim),
            unless(last_pair, states).reshape(heads, dim, dim),
            preferred_element_type=F32,
        )
        more = turned((after.T[:, :, None] * state_part).reshape(8, width), "ctx", -PAIR)
        more = unless(last_pair, more)

    keep, send, partial, key_grad, vs2 = call(
        inner_grad_kernel,
        [shape((rows, width), BF16)] * 2
        + [shape((size, width), F32)] * 2
        + [shape((size, width), BF16)],
        attended, scales, q2, kc2, v2, grad, weights, cum, *before, *lead_weights,
        scratch=[pltpu.VMEM((size, width), BF16)],
        flops=10 * heads * size * size * dim,
    )
    out_keep, out_got = keep, swapped(send)
    kept, got = [], []
    for i in range(PARTS):
        keep, send = call(
            lambda *refs, i=i: outer_grad_kernel(blocks - PAIR, i, *refs),
            [shape((rows, chunk), BF16)] * 2,
            partial, key_grad, ks2, vs2, behind[i], more, conv_weight,
            scratch=[pltpu.VMEM((size + 8, chunk), F32), pltpu.VMEM((size, chunk), F32)],
        )
        kept.append(to_earlier_section(keep, 0))
        got.append(to_earlier_section(send, 1))
    return tuple(placed(([out_keep], [out_got]), (kept, got)))


def solution(mesh):
    placed = (
        P("pp", "ctx", "tp"),
        P("pp", "ctx", "tp"),
        P("pp", "ctx", "tp"),
        P("pp", "ctx", "tp"),
        P("pp", None, "tp"),
        P("pp", "ctx", "tp"),
    )
    return jax.shard_map(
        per_device,
        mesh=mesh,
        in_specs=placed,
        out_specs=(P("pp", "ctx", "tp"), P("pp", "ctx", "tp")),
        check_vma=False,
    )
```

```python
import jax
import jax.numpy as jnp
from jax import lax
from jax.experimental import pallas as pl
from jax.experimental.pallas import tpu as pltpu
from jax.sharding import PartitionSpec as P

F32 = jnp.float32
BF16 = jnp.bfloat16
PAIR = 2
EDGE = 16
LEAD = 4
STEPS = 2
PARTS = 1


def call(kernel, outs, *args, scratch=(), flops=0, hbm=(), out_hbm=False, alias=()):
    vmem = pl.BlockSpec(memory_space=pltpu.VMEM)
    moved = sum(a.size * a.dtype.itemsize for a in args) + sum(
        s.size * s.dtype.itemsize for s in outs
    )
    return pl.pallas_call(
        kernel,
        out_shape=outs,
        in_specs=[
            pl.BlockSpec(memory_space=pltpu.HBM) if i in hbm else vmem for i in range(len(args))
        ],
        out_specs=[pl.BlockSpec(memory_space=pltpu.HBM) if out_hbm else vmem] * len(outs),
        scratch_shapes=scratch,
        input_output_aliases=dict(alias),
        compiler_params=pltpu.CompilerParams(vmem_limit_bytes=32 * 1024 * 1024),
        cost_estimate=pl.CostEstimate(flops=flops, bytes_accessed=moved, transcendentals=0),
    )(*args)


def shape(dims, dtype):
    return jax.ShapeDtypeStruct(dims, dtype)


def halves(size):
    mine = lax.rem(lax.axis_index("ctx"), PAIR)
    return (
        pl.ds(pl.multiple_of(mine * size, size), size),
        pl.ds(pl.multiple_of((1 - mine) * size, size), size),
    )


def dot(a, b, contract):
    return lax.dot_general(a, b, ((contract[:1], contract[1:]), ((), ())), preferred_element_type=F32)


def split3(x):
    hi = x.astype(BF16)
    rest = x - hi.astype(F32)
    mid = rest.astype(BF16)
    return hi, mid, (rest - mid.astype(F32)).astype(BF16)


def half_rows(rows, mine, heads):
    return jnp.where(mine == 0, rows[:heads], rows[heads:])


def copy_all(pairs, sems):
    copies = [pltpu.make_async_copy(src, to, sems.at[i]) for i, (src, to) in enumerate(pairs)]
    for copy in copies:
        copy.start()
    return copies


def step_lanes(width, chunk, step, mine):
    return pl.ds(pl.multiple_of(mine * width + step * chunk, chunk), chunk)


def pack_kernel(k, v, log_decay, *refs):
    *outs, cum, decays, sems = refs
    first = outs[0]
    rows, heads = k.shape[1], log_decay.shape[1] // PAIR
    mine = lax.rem(lax.axis_index("ctx"), PAIR)
    chunk = first.shape[1]
    pairs = [(log_decay, decays)]
    for step, out in enumerate(outs):
        other = step_lanes(k.shape[2] // PAIR, chunk, step, 1 - mine)
        for i, ref in enumerate((k, v)):
            pairs.append((ref.at[0, :, other], out.at[i * rows : (i + 1) * rows, :]))
    copies = copy_all(pairs, sems)
    copies[0].wait()
    upto = lax.broadcasted_iota(jnp.int32, (rows, rows), 0) <= lax.broadcasted_iota(
        jnp.int32, (rows, rows), 1
    )
    upto = upto.astype(F32).astype(BF16)
    sums = sum(dot(part, upto, (1, 0)) for part in split3(decays[0]))
    cum[...] = sums
    line = chunk // rows
    parts = [
        jnp.concatenate([part[h : h + 1] for h in range(at, at + line)], 1).astype(F32)
        for part in split3(half_rows(sums, 1 - mine, heads))
        for at in range(0, heads, line)
    ]
    parts.append(jnp.zeros((EDGE - len(parts), chunk), F32))
    first[2 * rows :, :] = jnp.concatenate(parts, 0).astype(BF16)
    for copy in copies[1:]:
        copy.wait()


def pack_more_kernel(q, k, v, g, _, second, third, own, sems):
    rows = q.shape[1]
    lanes_own, other = halves(q.shape[2] // PAIR)
    pairs = [(q.at[0, :, other], second), (g.at[0, :, other], third)]
    pairs += [
        (ref.at[0, :, lanes_own], own.at[i * rows : (i + 1) * rows, :])
        for i, ref in enumerate((k, v, q, g))
    ]
    for copy in copy_all(pairs, sems):
        copy.wait()


def join_step(step, got, own, taps, edges, cum_rows, kc2, v2, top, ks2, state, padded):
    size, width = kc2.shape
    rows, chunk = size // PAIR, got.shape[1]
    dim = state.shape[1]
    heads = chunk // dim
    here, there = halves(rows)
    mine = lax.rem(lax.axis_index("ctx"), PAIR)
    lanes = slice(step * chunk, (step + 1) * chunk)
    v2[here, lanes] = own[rows : 2 * rows, lanes]
    v2[there, lanes] = got[rows : 2 * rows, :]
    padded[:EDGE, :] = edges[0][:, lanes].astype(F32) if edges else jnp.zeros((EDGE, chunk), F32)
    start = pl.multiple_of(EDGE + mine * rows, EDGE)
    padded[pl.ds(start, rows), :] = own[:rows, lanes].astype(F32)
    start = pl.multiple_of(EDGE + (1 - mine) * rows, EDGE)
    padded[pl.ds(start, rows), :] = got[:rows, :].astype(F32)
    total = jnp.zeros((size, chunk), F32)
    taps_at = step_lanes(width, chunk, step, mine)
    for j in range(taps.shape[1]):
        total = total + taps[0, j : j + 1, taps_at] * padded[EDGE - j : EDGE - j + size, :]
    keys = total.astype(BF16)
    kc2[:, lanes] = keys
    top[:, lanes] = total[:EDGE]
    cols = cum_rows.T
    after = jnp.exp(cols[size - 1 :, :] - cols)
    keys = keys.astype(F32)
    for h in range(heads):
        at = step * heads + h
        scaled = (keys[:, h * dim : (h + 1) * dim] * after[:, at : at + 1]).astype(BF16)
        ks2[:, at * dim : (at + 1) * dim] = scaled
        sums = dot(scaled, v2[:, at * dim : (at + 1) * dim], (0, 0))
        state[h * dim : (h + 1) * dim, :] = sums.astype(BF16)
    last = padded[EDGE + size - LEAD : EDGE + size, :]
    last = [last[:, h * dim : (h + 1) * dim] for h in range(heads)]
    if LEAD * heads < EDGE:
        last.append(jnp.zeros((EDGE - LEAD * heads, dim), F32))
    state[chunk:, :] = jnp.concatenate(last, 0).astype(BF16)


def join_kernel(got, own, own_cum, taps, *refs):
    *edges, kc2, v2, top, ks2, state, cum, padded = refs
    rows, heads = own_cum.shape[1], own_cum.shape[0] // PAIR
    mine = lax.rem(lax.axis_index("ctx"), PAIR)
    coded = got[2 * rows :, :].astype(F32)
    lines = heads * rows // coded.shape[1]
    row = coded[:lines] + coded[lines : 2 * lines] + coded[2 * lines : 3 * lines]
    per_line = heads // lines
    other_rows = jnp.concatenate(
        [
            row[h // per_line : h // per_line + 1, h % per_line * rows : (h % per_line + 1) * rows]
            for h in range(heads)
        ],
        0,
    )
    own_rows = half_rows(own_cum[...], mine, heads)
    front = jnp.where(mine == 0, own_rows, other_rows)
    back = jnp.where(mine == 0, other_rows, own_rows) + front[:, rows - 1 :]
    cum_rows = jnp.concatenate([front, back], 1)
    cum_rows = jnp.concatenate([cum_rows, jnp.zeros((8 - heads, PAIR * rows), F32)], 0)
    cum[...] = cum_rows
    join_step(0, got, own, taps, edges, cum_rows, kc2, v2, top, ks2, state, padded)


def join_next_kernel(step, _kc2, _v2, _top, _ks2, got, own, cum, taps, *refs):
    *edges, kc2, v2, top, ks2, state, padded = refs
    join_step(step, got, own, taps, edges, cum[...], kc2, v2, top, ks2, state, padded)


def mixing_of(cum_rows, cols, h, first=0):
    differ = cols[:, h : h + 1] - cum_rows[h : h + 1, :]
    at = lax.broadcasted_iota(jnp.int32, differ.shape, 1)
    causal = (lax.broadcasted_iota(jnp.int32, differ.shape, 0) >= at) & (at >= first)
    return jnp.where(causal, jnp.exp(jnp.where(causal, differ, 0.0)), 0.0)


def lead_mixing_of(cum_rows, cols, heads):
    wide = (cols.shape[0], heads * LEAD)
    lane = lax.broadcasted_iota(jnp.int32, wide, 1)
    late = jnp.zeros(wide, F32)
    for h in range(heads):
        late = jnp.where(lane // LEAD == h, cols[:, h : h + 1], late)
    early = jnp.concatenate([cum_rows[h : h + 1, :LEAD] for h in range(heads)], 1)
    causal = lax.broadcasted_iota(jnp.int32, wide, 0) >= lane % LEAD
    return jnp.where(causal, jnp.exp(jnp.where(causal, late - early, 0.0)), 0.0)


def block_diagonal(rows, dim, heads, first=0):
    wide = jnp.concatenate([rows] * heads, 0)
    head = lax.broadcasted_iota(jnp.int32, wide.shape, 0) // LEAD
    lane = lax.broadcasted_iota(jnp.int32, wide.shape, 1) // dim + first
    return jnp.where(head == lane, wide, 0.0).astype(BF16)


def local_kernel(
    got, own, kc2, v2, cum, q2, qs2, qst, weights, inside, lead_mixing, lead_mixing_t, lead_values
):
    size, width = q2.shape
    heads, dim = weights.shape[0], width // weights.shape[0]
    rows = size // PAIR
    here, there = halves(rows)
    q2[here, :] = own[2 * rows : 3 * rows, :]
    q2[there, :] = got[...]
    cum_rows = cum[...]
    cols = cum_rows.T
    growth = jnp.exp(cols)
    lead = lead_mixing_of(cum_rows, cols, heads)
    lead_mixing[...] = lead
    wide = jnp.concatenate([lead, jnp.zeros((size, dim - LEAD * heads), F32)], 1)
    lead_mixing_t[...] = wide.T[: LEAD * heads]
    lead_values[...] = block_diagonal(v2[:EDGE, :].astype(F32)[:LEAD], dim, heads)
    for h in range(heads):
        lanes = slice(h * dim, (h + 1) * dim)
        scaled = q2[:, lanes].astype(F32) * growth[:, h : h + 1]
        qs2[:, lanes] = scaled.astype(BF16)
        qst[lanes, :] = scaled.T.astype(BF16)
        scores = dot(q2[:, lanes], kc2[:, lanes], (1, 1))
        w = (scores * mixing_of(cum_rows, cols, h, LEAD)).astype(BF16)
        weights[h] = w
        inside[:, lanes] = dot(w, v2[:, lanes], (1, 0))


def unless(flag, block):
    return jnp.where(flag, jnp.zeros_like(block), block)


def attend_kernel(step, *refs):
    kc2, inside, q2, qs2, top, taps, lead_mixing, lead_values, before, *refs = refs
    kc2_whole, attended, lead_weights, reach = refs
    size, width = q2.shape
    dim = before.shape[1]
    heads = width // dim
    chunk = width // STEPS
    lanes = slice(step * chunk, (step + 1) * chunk)
    mine = lax.rem(lax.axis_index("ctx"), PAIR)
    start = lax.axis_index("ctx") < PAIR
    tail = unless(start, before[chunk:, :].astype(F32))
    reach[...] = jnp.zeros_like(reach)
    for h in range(chunk // dim):
        reach[LEAD : 2 * LEAD, h * dim : (h + 1) * dim] = tail[LEAD * h : LEAD * (h + 1)]
    fixed = top[: 2 * LEAD, lanes]
    taps_at = step_lanes(width, chunk, step, mine)
    for j in range(1, taps.shape[1]):
        fixed = fixed + taps[0, j : j + 1, taps_at] * reach[2 * LEAD - j : 4 * LEAD - j, :]
    rows = jnp.concatenate([fixed, top[2 * LEAD :, lanes]], 0)
    kc2_whole[:EDGE, lanes] = rows.astype(BF16)
    lead_keys = block_diagonal(fixed[:LEAD], dim, heads, step * chunk // dim)
    lead = (dot(q2[:, lanes], lead_keys, (1, 1)) * lead_mixing[...]).astype(BF16)
    lead_weights[...] = lead
    for h in range(chunk // dim):
        at = step * chunk // dim + h
        here = slice(at * dim, (at + 1) * dim)
        state = unless(start, before[h * dim : (h + 1) * dim, :])
        a = inside[:, here] + dot(lead, lead_values[:, here], (1, 0))
        attended[:, here] = a + dot(qs2[:, here], state, (1, 0))


def sums_kernel(dim, attended, own, got, g2, sums):
    size, width = attended.shape
    rows = size // PAIR
    here, there = halves(rows)
    g2[here, :] = own[3 * rows :, :]
    g2[there, :] = got[...]
    squares = jnp.zeros((size, dim), F32)
    products = jnp.zeros((size, dim), F32)
    for at in range(0, width, dim):
        a = attended[:, at : at + dim]
        squares = squares + a * a
        products = products + a * g2[:, at : at + dim].astype(F32)
    ones = jnp.ones((8, dim), BF16)
    both = jnp.concatenate([squares, products], 0)
    line = sum(dot(ones, part, (1, 1)) for part in split3(both))[:1]
    sums[...] = jnp.concatenate([line[:, :size], line[:, size:]], 0)


def grad_kernel(width_all, attended, q2, qst, lead_mixing_t, lead_values, g2, *refs):
    *sums, scales, grad = refs[:-PARTS]
    adjoints = refs[-PARTS:]
    size, width = q2.shape
    dim = adjoints[0].shape[1]
    heads = width // dim
    total = sum(ref[...] for ref in sums[1:]) + sums[0][...]
    inverse = 1.0 / jnp.sqrt(total[0:1] / width_all + 1e-06)
    shift = total[1:2] / width_all * inverse
    both = jnp.concatenate([inverse, shift * inverse * inverse, jnp.zeros((6, size), F32)], 0)
    scales[...] = both
    both = both.T
    inverse, pull = both[:, 0:1], both[:, 1:2]
    for h in range(heads):
        lanes = slice(h * dim, (h + 1) * dim)
        d = (g2[:, lanes].astype(F32) * inverse - attended[:, lanes] * pull).astype(BF16)
        grad[:, lanes] = d
        part, at = divmod(h, heads // PARTS)
        adjoints[part][at * dim : (at + 1) * dim, :] = dot(qst[lanes, :], d, (1, 0)).astype(BF16)
    scores = (dot(lead_values[...], grad[...], (1, 1)) * lead_mixing_t[...]).astype(BF16)
    tops = dot(scores, q2[...], (1, 0))
    per_part = heads // PARTS
    for i, adjoint in enumerate(adjoints):
        rows = [
            tops[LEAD * h : LEAD * (h + 1), h * dim : (h + 1) * dim]
            for h in range(i * per_part, (i + 1) * per_part)
        ]
        if LEAD * per_part < EDGE:
            rows.append(jnp.zeros((EDGE - LEAD * per_part, dim), F32))
        adjoint[width // PARTS :, :] = jnp.concatenate(rows, 0).astype(BF16)


def inner_grad_kernel(
    attended, scales, q2, kc2, v2, grad, weights, cum, *refs
):
    before, lead_weights = refs[:STEPS], refs[STEPS : 2 * STEPS]
    keep, send, partial, key_grad, vs2, normed = refs[2 * STEPS :]
    size, width = q2.shape
    dim = before[0].shape[1]
    heads = width // dim
    per_step = heads // STEPS
    start = lax.axis_index("ctx") < PAIR
    inverse = scales[...].T[:, 0:1]
    cum_rows = cum[...]
    cols = cum_rows.T
    growth = jnp.exp(cols)
    after = jnp.exp(cols[size - 1 :, :] - cols)
    for h in range(heads):
        lanes = slice(h * dim, (h + 1) * dim)
        vs2[:, lanes] = (v2[:, lanes].astype(F32) * after[:, h : h + 1]).astype(BF16)
        normed[:, lanes] = (attended[:, lanes] * inverse).astype(BF16)
        d = grad[:, lanes]
        scores = dot(d, v2[:, lanes], (1, 1)) * mixing_of(cum_rows, cols, h)
        scores = scores.astype(BF16)
        step, at = divmod(h, per_step)
        state = unless(start, before[step][at * dim : (at + 1) * dim, :])
        query_grad = dot(scores, kc2[:, lanes], (1, 0)) + growth[:, h : h + 1] * dot(
            d, state, (1, 1)
        )
        key_grad[:, lanes] = dot(scores, q2[:, lanes], (0, 0))
        partial[:, lanes] = query_grad + dot(weights[h], d, (0, 0))
    lead = sum(ref[...].astype(F32) for ref in lead_weights).astype(BF16)
    lead = dot(lead, grad[...], (0, 0))
    for h in range(heads):
        lanes = slice(h * dim, (h + 1) * dim)
        partial[:LEAD, lanes] = partial[:LEAD, lanes] + lead[LEAD * h : LEAD * (h + 1), lanes]
    here, there = halves(size // PAIR)
    keep[...] = normed[here, :]
    send[...] = normed[there, :]


def outer_grad_kernel(
    last, part, partial, key_grad, ks2, vs2, behind, more, taps, keep, send, padded, done
):
    size, width = partial.shape
    dim = behind.shape[1]
    heads = width // dim // PARTS
    chunk = width // PARTS
    mine = lax.rem(lax.axis_index("ctx"), PAIR)
    own = pl.ds(pl.multiple_of(mine * width + part * chunk, chunk), chunk)
    ends = lax.axis_index("ctx") >= last
    tops = unless(ends, behind[chunk:, :].astype(F32))
    for h in range(heads):
        at = part * heads + h
        lanes = slice(at * dim, (at + 1) * dim)
        here = slice(h * dim, (h + 1) * dim)
        state = unless(ends, behind[here, :])
        padded[:size, here] = key_grad[:, lanes] + dot(vs2[:, lanes], state, (1, 1))
        done[:, here] = partial[:, lanes] + dot(ks2[:, lanes], state, (1, 0))
        top = jnp.concatenate([tops[4 * h : 4 * h + 4], jnp.zeros((4, dim), F32)], 0)
        padded[size:, here] = top + more[:, lanes]
    total = done[...]
    for j in range(taps.shape[1]):
        total = total + taps[0, j : j + 1, own] * padded[j : j + size, :]
    done[...] = total
    here, there = halves(size // PAIR)
    first = lax.axis_index("pp") == 0
    keep[...] = unless(first, done[here, :]).astype(BF16)
    send[...] = unless(first, done[there, :]).astype(BF16)


def place_kernel(*refs):
    *pieces, out, sems = refs
    kept, got = pieces[: len(pieces) // 2], pieces[len(pieces) // 2 :]
    width = kept[0].shape[1]
    mine = lax.rem(lax.axis_index("ctx"), PAIR)
    pairs = []
    for half, parts in ((mine, kept), (1 - mine, got)):
        for i, part in enumerate(parts):
            start = pl.multiple_of((half * len(parts) + i) * width, width)
            pairs.append((part, out.at[0, :, pl.ds(start, width)]))
    for copy in copy_all(pairs, sems):
        copy.wait()


def placed(kept, got):
    pieces = kept + got
    rows = kept[0].shape[0]
    return call(
        place_kernel,
        [shape((1, rows, sum(piece.shape[1] for piece in pieces)), BF16)],
        *pieces,
        scratch=[pltpu.SemaphoreType.DMA((len(pieces),))],
        out_hbm=True,
    )[0]


def turned(block, axis, distance):
    count = lax.axis_size(axis)
    return lax.ppermute(block, axis, [(i, (i + distance) % count) for i in range(count)])


def swapped(block):
    return lax.ppermute(block, "ctx", [(i, i ^ 1) for i in range(lax.axis_size("ctx"))])


def to_earlier_section(block, flip):
    blocks, sections = lax.axis_size("ctx"), lax.axis_size("pp")
    route = [
        (c * sections + p, (c ^ flip) * sections + (p - 1) % sections)
        for c in range(blocks)
        for p in range(sections)
    ]
    return lax.ppermute(block, ("ctx", "pp"), route)


def summed_parts(part):
    blocks, count = lax.axis_size("ctx"), lax.axis_size("tp")

    def neighbour(block):
        return lax.ppermute(block, "tp", [(i, i ^ 1) for i in range(count)])

    def fetched(block, *ways):
        route = [
            (c * count + t, (c ^ ways[t % len(ways)][0]) * count + (t + ways[t % len(ways)][1]) % count)
            for c in range(blocks)
            for t in range(count)
        ]
        return lax.ppermute(block, ("ctx", "tp"), route)

    pair = part + neighbour(part)
    ways = [(1, 0)] + [(flip, k) for k in range(2, count, 2) for flip in (0, 1)]
    shared = [fetched(pair, *ways[i : i + 2]) for i in range(0, len(ways) - 1, 2)]
    parts = [pair, fetched(pair, ways[-1])]
    for block in shared:
        parts += [block, neighbour(block)]
    return parts


def per_device(queries, key_input, values, log_decay, conv_weight, out_grad):
    rows, width = queries.shape[1], queries.shape[2] // PAIR
    heads = log_decay.shape[2] // PAIR
    dim = width // heads
    size = PAIR * rows
    blocks = lax.axis_size("ctx")
    supers = blocks // PAIR
    width_all = queries.shape[2] * lax.axis_size("tp")
    log_decay = jnp.swapaxes(log_decay, 1, 2)
    arrays = (queries, key_input, values, out_grad, log_decay)
    queries, key_input, values, out_grad, decays = (
        pltpu.with_memory_space_constraint(x, pltpu.HBM) for x in arrays
    )

    step_width = width // STEPS
    *packed, own_cum = call(
        pack_kernel,
        [shape((2 * rows + EDGE, step_width), BF16)]
        + [shape((2 * rows, step_width), BF16)] * (STEPS - 1)
        + [shape((PAIR * heads, rows), F32)],
        key_input, values, decays,
        scratch=[pltpu.VMEM(log_decay.shape, F32), pltpu.SemaphoreType.DMA((1 + 2 * STEPS,))],
        hbm=range(3),
    )
    got = [swapped(part) for part in packed]
    edges = ()
    if supers > 2:
        edge = arrays[1][0, rows - EDGE :]
        near = lax.ppermute(edge[:, :width], "ctx", [(i, i + 1) for i in range(1, blocks - 1, 2)])
        far = lax.ppermute(edge[:, width:], "ctx", [(i, i + 2) for i in range(1, blocks - 2, 2)])
        edges = (near + far,)
    second, third, own = call(
        pack_more_kernel,
        [shape((rows, width), BF16)] * 2 + [shape((4 * rows, width), BF16)],
        queries, key_input, values, out_grad, packed[0][2 * rows :],
        scratch=[pltpu.SemaphoreType.DMA((6,))],
        hbm=range(4),
    )
    got_q, got_g = swapped(second), swapped(third)
    joined = [
        shape((size, width), BF16), shape((size, width), BF16), shape((EDGE, width), F32),
        shape((size, width), BF16), shape((step_width + EDGE, dim), BF16),
    ]
    room = [pltpu.VMEM((EDGE + size, step_width), F32)]
    kc2, v2, top, ks2, state, cum = call(
        join_kernel,
        joined + [shape((8, size), F32)],
        got[0], own, own_cum, conv_weight, *edges,
        scratch=room,
    )
    states = [state]
    for step in range(1, STEPS):
        kc2, v2, top, ks2, state = call(
            lambda *refs, step=step: join_next_kernel(step, *refs),
            joined,
            kc2, v2, top, ks2, got[step], own, cum, conv_weight, *edges,
            scratch=room,
            alias=((0, 0), (1, 1), (2, 2), (3, 3)),
        )
        states.append(state)
    carry = jnp.repeat(jnp.exp(cum[:heads, -1]), dim)[:, None]
    pair_index = lax.axis_index("ctx") // PAIR
    before = []
    for step, state in enumerate(states):
        moved = turned(state, "ctx", PAIR)
        for _ in range(supers - 2):
            earlier = unless(pair_index == 0, moved[:step_width]).astype(F32)
            earlier = carry[step * step_width : (step + 1) * step_width] * earlier
            earlier = (state[:step_width].astype(F32) + earlier).astype(BF16)
            moved = jnp.concatenate([turned(earlier, "ctx", PAIR), moved[step_width:]], 0)
        before.append(moved)

    q2, qs2, qst, weights, inside, lead_mixing, lead_mixing_t, lead_values = call(
        local_kernel,
        [shape((size, width), BF16)] * 2
        + [shape((width, size), BF16)]
        + [shape((heads, size, size), BF16), shape((size, width), F32)]
        + [shape((size, LEAD * heads), F32), shape((LEAD * heads, size), F32)]
        + [shape((LEAD * heads, width), BF16)],
        got_q, own, kc2, v2, cum,
        flops=4 * heads * size * size * dim,
    )
    lead_weights = []
    for step in range(STEPS):
        kc2, inside, lead = call(
            lambda *refs, step=step: attend_kernel(step, *refs),
            [shape(kc2.shape, BF16), shape((size, width), F32), shape((size, LEAD * heads), BF16)],
            kc2, inside, q2, qs2, top, conv_weight, lead_mixing, lead_values, before[step],
            scratch=[pltpu.VMEM((4 * LEAD, step_width), F32)],
            alias=((0, 0), (1, 1)),
        )
        lead_weights.append(lead)
    attended = inside
    g2, sums = call(
        lambda *refs: sums_kernel(dim, *refs),
        [shape((size, width), BF16), shape((2, size), F32)],
        attended, own, got_g,
    )
    parts = summed_parts(sums)
    chunk = width // PARTS
    scales, grad, *adjoints = call(
        lambda *refs: grad_kernel(width_all, *refs),
        [shape((8, size), F32), shape((size, width), BF16)]
        + [shape((chunk + EDGE, dim), BF16)] * PARTS,
        attended, q2, qst, lead_mixing_t, lead_values, g2, *parts,
    )
    last_pair = pair_index == supers - 1
    behind = []
    for i, adjoint in enumerate(adjoints):
        moved = turned(adjoint, "ctx", -PAIR)
        for _ in range(supers - 2):
            later = unless(last_pair, moved[:chunk]).astype(F32)
            joined = adjoint[:chunk].astype(F32) + carry[i * chunk : (i + 1) * chunk] * later
            state = turned(joined.astype(BF16), "ctx", -PAIR)
            moved = jnp.concatenate([state, moved[chunk:]], 0)
        behind.append(moved)
    more = jnp.zeros((8, width), F32)
    if supers > 2:
        after = jnp.exp(cum[:heads, -1:] - cum[:heads, :8])
        states = jnp.concatenate([part[:chunk] for part in behind], 0)
        state_part = jnp.einsum(
            "shv,hkv->shk",
            v2[:8].reshape(8, heads, dim),
            unless(last_pair, states).reshape(heads, dim, dim),
            preferred_element_type=F32,
        )
        more = turned((after.T[:, :, None] * state_part).reshape(8, width), "ctx", -PAIR)
        more = unless(last_pair, more)

    keep, send, partial, key_grad, vs2 = call(
        inner_grad_kernel,
        [shape((rows, width), BF16)] * 2
        + [shape((size, width), F32)] * 2
        + [shape((size, width), BF16)],
        attended, scales, q2, kc2, v2, grad, weights, cum, *before, *lead_weights,
        scratch=[pltpu.VMEM((size, width), BF16)],
        flops=10 * heads * size * size * dim,
    )
    layer_output = placed([keep], [swapped(send)])
    kept, got = [], []
    for i in range(PARTS):
        keep, send = call(
            lambda *refs, i=i: outer_grad_kernel(blocks - PAIR, i, *refs),
            [shape((rows, chunk), BF16)] * 2,
            partial, key_grad, ks2, vs2, behind[i], more, conv_weight,
            scratch=[pltpu.VMEM((size + 8, chunk), F32), pltpu.VMEM((size, chunk), F32)],
        )
        kept.append(to_earlier_section(keep, 0))
        got.append(to_earlier_section(send, 1))
    return (layer_output, placed(kept, got))


def solution(mesh):
    placed = (
        P("pp", "ctx", "tp"),
        P("pp", "ctx", "tp"),
        P("pp", "ctx", "tp"),
        P("pp", "ctx", "tp"),
        P("pp", None, "tp"),
        P("pp", "ctx", "tp"),
    )
    return jax.shard_map(
        per_device,
        mesh=mesh,
        in_specs=placed,
        out_specs=(P("pp", "ctx", "tp"), P("pp", "ctx", "tp")),
        check_vma=False,
    )
```

```python
import jax
import jax.numpy as jnp
from jax import lax
from jax.experimental import pallas as pl
from jax.experimental.pallas import tpu as pltpu
from jax.sharding import PartitionSpec as P

F32 = jnp.float32
BF16 = jnp.bfloat16
PAIR = 2
EDGE = 16
LEAD = 4
STEPS = 2
PARTS = 1


def call(kernel, outs, *args, scratch=(), flops=0, hbm=(), out_hbm=False, alias=()):
    vmem = pl.BlockSpec(memory_space=pltpu.VMEM)
    moved = sum(a.size * a.dtype.itemsize for a in args) + sum(
        s.size * s.dtype.itemsize for s in outs
    )
    return pl.pallas_call(
        kernel,
        out_shape=outs,
        in_specs=[
            pl.BlockSpec(memory_space=pltpu.HBM) if i in hbm else vmem for i in range(len(args))
        ],
        out_specs=[pl.BlockSpec(memory_space=pltpu.HBM) if out_hbm else vmem] * len(outs),
        scratch_shapes=scratch,
        input_output_aliases=dict(alias),
        compiler_params=pltpu.CompilerParams(vmem_limit_bytes=32 * 1024 * 1024),
        cost_estimate=pl.CostEstimate(flops=flops, bytes_accessed=moved, transcendentals=0),
    )(*args)


def shape(dims, dtype):
    return jax.ShapeDtypeStruct(dims, dtype)


def halves(size):
    mine = lax.rem(lax.axis_index("ctx"), PAIR)
    return (
        pl.ds(pl.multiple_of(mine * size, size), size),
        pl.ds(pl.multiple_of((1 - mine) * size, size), size),
    )


def dot(a, b, contract):
    return lax.dot_general(a, b, ((contract[:1], contract[1:]), ((), ())), preferred_element_type=F32)


def split3(x):
    hi = x.astype(BF16)
    rest = x - hi.astype(F32)
    mid = rest.astype(BF16)
    return hi, mid, (rest - mid.astype(F32)).astype(BF16)


def half_rows(rows, mine, heads):
    return jnp.where(mine == 0, rows[:heads], rows[heads:])


def copy_all(pairs, sems):
    copies = [pltpu.make_async_copy(src, to, sems.at[i]) for i, (src, to) in enumerate(pairs)]
    for copy in copies:
        copy.start()
    return copies


def step_lanes(width, chunk, step, mine):
    return pl.ds(pl.multiple_of(mine * width + step * chunk, chunk), chunk)


def pack_kernel(k, v, log_decay, *refs):
    *outs, cum, decays, sems = refs
    first = outs[0]
    rows, heads = k.shape[1], log_decay.shape[1] // PAIR
    mine = lax.rem(lax.axis_index("ctx"), PAIR)
    chunk = first.shape[1]
    pairs = [(log_decay, decays)]
    for step, out in enumerate(outs):
        other = step_lanes(k.shape[2] // PAIR, chunk, step, 1 - mine)
        for i, ref in enumerate((k, v)):
            pairs.append((ref.at[0, :, other], out.at[i * rows : (i + 1) * rows, :]))
    copies = copy_all(pairs, sems)
    copies[0].wait()
    upto = lax.broadcasted_iota(jnp.int32, (rows, rows), 0) <= lax.broadcasted_iota(
        jnp.int32, (rows, rows), 1
    )
    upto = upto.astype(F32).astype(BF16)
    sums = sum(dot(part, upto, (1, 0)) for part in split3(decays[0]))
    cum[...] = sums
    line = chunk // rows
    parts = [
        jnp.concatenate([part[h : h + 1] for h in range(at, at + line)], 1).astype(F32)
        for part in split3(half_rows(sums, 1 - mine, heads))
        for at in range(0, heads, line)
    ]
    parts.append(jnp.zeros((EDGE - len(parts), chunk), F32))
    first[2 * rows :, :] = jnp.concatenate(parts, 0).astype(BF16)
    for copy in copies[1:]:
        copy.wait()


def pack_more_kernel(q, k, v, g, _, second, third, own, sems):
    rows = q.shape[1]
    lanes_own, other = halves(q.shape[2] // PAIR)
    pairs = [(q.at[0, :, other], second), (g.at[0, :, other], third)]
    pairs += [
        (ref.at[0, :, lanes_own], own.at[i * rows : (i + 1) * rows, :])
        for i, ref in enumerate((k, v, q, g))
    ]
    for copy in copy_all(pairs, sems):
        copy.wait()


def join_step(step, got, own, taps, edges, cum_rows, kc2, v2, top, ks2, state, padded):
    size, width = kc2.shape
    rows, chunk = size // PAIR, got.shape[1]
    dim = state.shape[1]
    heads = chunk // dim
    here, there = halves(rows)
    mine = lax.rem(lax.axis_index("ctx"), PAIR)
    lanes = slice(step * chunk, (step + 1) * chunk)
    v2[here, lanes] = own[rows : 2 * rows, lanes]
    v2[there, lanes] = got[rows : 2 * rows, :]
    padded[:EDGE, :] = edges[0][:, lanes].astype(F32) if edges else jnp.zeros((EDGE, chunk), F32)
    start = pl.multiple_of(EDGE + mine * rows, EDGE)
    padded[pl.ds(start, rows), :] = own[:rows, lanes].astype(F32)
    start = pl.multiple_of(EDGE + (1 - mine) * rows, EDGE)
    padded[pl.ds(start, rows), :] = got[:rows, :].astype(F32)
    total = jnp.zeros((size, chunk), F32)
    taps_at = step_lanes(width, chunk, step, mine)
    for j in range(taps.shape[1]):
        total = total + taps[0, j : j + 1, taps_at] * padded[EDGE - j : EDGE - j + size, :]
    keys = total.astype(BF16)
    kc2[:, lanes] = keys
    top[:, lanes] = total[:EDGE]
    cols = cum_rows.T
    after = jnp.exp(cols[size - 1 :, :] - cols)
    keys = keys.astype(F32)
    for h in range(heads):
        at = step * heads + h
        scaled = (keys[:, h * dim : (h + 1) * dim] * after[:, at : at + 1]).astype(BF16)
        ks2[:, at * dim : (at + 1) * dim] = scaled
        sums = dot(scaled, v2[:, at * dim : (at + 1) * dim], (0, 0))
        state[h * dim : (h + 1) * dim, :] = sums.astype(BF16)
    last = padded[EDGE + size - LEAD : EDGE + size, :]
    last = [last[:, h * dim : (h + 1) * dim] for h in range(heads)]
    if LEAD * heads < EDGE:
        last.append(jnp.zeros((EDGE - LEAD * heads, dim), F32))
    state[chunk:, :] = jnp.concatenate(last, 0).astype(BF16)


def join_kernel(got, own, own_cum, taps, *refs):
    *edges, kc2, v2, top, ks2, state, cum, padded = refs
    rows, heads = own_cum.shape[1], own_cum.shape[0] // PAIR
    mine = lax.rem(lax.axis_index("ctx"), PAIR)
    coded = got[2 * rows :, :].astype(F32)
    lines = heads * rows // coded.shape[1]
    row = coded[:lines] + coded[lines : 2 * lines] + coded[2 * lines : 3 * lines]
    per_line = heads // lines
    other_rows = jnp.concatenate(
        [
            row[h // per_line : h // per_line + 1, h % per_line * rows : (h % per_line + 1) * rows]
            for h in range(heads)
        ],
        0,
    )
    own_rows = half_rows(own_cum[...], mine, heads)
    front = jnp.where(mine == 0, own_rows, other_rows)
    back = jnp.where(mine == 0, other_rows, own_rows) + front[:, rows - 1 :]
    cum_rows = jnp.concatenate([front, back], 1)
    cum_rows = jnp.concatenate([cum_rows, jnp.zeros((8 - heads, PAIR * rows), F32)], 0)
    cum[...] = cum_rows
    join_step(0, got, own, taps, edges, cum_rows, kc2, v2, top, ks2, state, padded)


def join_next_kernel(step, _kc2, _v2, _top, _ks2, got, own, cum, taps, *refs):
    *edges, kc2, v2, top, ks2, state, padded = refs
    join_step(step, got, own, taps, edges, cum[...], kc2, v2, top, ks2, state, padded)


def mixing_of(cum_rows, cols, h, first=0):
    differ = cols[:, h : h + 1] - cum_rows[h : h + 1, :]
    at = lax.broadcasted_iota(jnp.int32, differ.shape, 1)
    causal = (lax.broadcasted_iota(jnp.int32, differ.shape, 0) >= at) & (at >= first)
    return jnp.where(causal, jnp.exp(jnp.where(causal, differ, 0.0)), 0.0)


def lead_mixing_of(cum_rows, cols, heads):
    wide = (cols.shape[0], heads * LEAD)
    lane = lax.broadcasted_iota(jnp.int32, wide, 1)
    late = jnp.zeros(wide, F32)
    for h in range(heads):
        late = jnp.where(lane // LEAD == h, cols[:, h : h + 1], late)
    early = jnp.concatenate([cum_rows[h : h + 1, :LEAD] for h in range(heads)], 1)
    causal = lax.broadcasted_iota(jnp.int32, wide, 0) >= lane % LEAD
    return jnp.where(causal, jnp.exp(jnp.where(causal, late - early, 0.0)), 0.0)


def block_diagonal(rows, dim, heads, first=0):
    wide = jnp.concatenate([rows] * heads, 0)
    head = lax.broadcasted_iota(jnp.int32, wide.shape, 0) // LEAD
    lane = lax.broadcasted_iota(jnp.int32, wide.shape, 1) // dim + first
    return jnp.where(head == lane, wide, 0.0).astype(BF16)


def local_kernel(got, own, kc2, v2, cum, q2, qs2, weights, inside, lead_mixing, lead_values):
    size, width = q2.shape
    heads, dim = weights.shape[0], width // weights.shape[0]
    rows = size // PAIR
    here, there = halves(rows)
    q2[here, :] = own[2 * rows : 3 * rows, :]
    q2[there, :] = got[...]
    cum_rows = cum[...]
    cols = cum_rows.T
    growth = jnp.exp(cols)
    lead_mixing[...] = lead_mixing_of(cum_rows, cols, heads)
    lead_values[...] = block_diagonal(v2[:EDGE, :].astype(F32)[:LEAD], dim, heads)
    for h in range(heads):
        lanes = slice(h * dim, (h + 1) * dim)
        qs2[:, lanes] = (q2[:, lanes].astype(F32) * growth[:, h : h + 1]).astype(BF16)
        scores = dot(q2[:, lanes], kc2[:, lanes], (1, 1))
        w = (scores * mixing_of(cum_rows, cols, h, LEAD)).astype(BF16)
        weights[h] = w
        inside[:, lanes] = dot(w, v2[:, lanes], (1, 0))


def unless(flag, block):
    return jnp.where(flag, jnp.zeros_like(block), block)


def attend_kernel(step, *refs):
    kc2, inside, q2, qs2, top, taps, lead_mixing, lead_values, before, *refs = refs
    kc2_whole, attended, lead_weights, reach = refs
    size, width = q2.shape
    dim = before.shape[1]
    heads = width // dim
    chunk = width // STEPS
    lanes = slice(step * chunk, (step + 1) * chunk)
    mine = lax.rem(lax.axis_index("ctx"), PAIR)
    start = lax.axis_index("ctx") < PAIR
    tail = unless(start, before[chunk:, :].astype(F32))
    reach[...] = jnp.zeros_like(reach)
    for h in range(chunk // dim):
        reach[LEAD : 2 * LEAD, h * dim : (h + 1) * dim] = tail[LEAD * h : LEAD * (h + 1)]
    fixed = top[: 2 * LEAD, lanes]
    taps_at = step_lanes(width, chunk, step, mine)
    for j in range(1, taps.shape[1]):
        fixed = fixed + taps[0, j : j + 1, taps_at] * reach[2 * LEAD - j : 4 * LEAD - j, :]
    rows = jnp.concatenate([fixed, top[2 * LEAD :, lanes]], 0)
    kc2_whole[:EDGE, lanes] = rows.astype(BF16)
    lead_keys = block_diagonal(fixed[:LEAD], dim, heads, step * chunk // dim)
    lead = (dot(q2[:, lanes], lead_keys, (1, 1)) * lead_mixing[...]).astype(BF16)
    lead_weights[...] = lead
    for h in range(chunk // dim):
        at = step * chunk // dim + h
        here = slice(at * dim, (at + 1) * dim)
        state = unless(start, before[h * dim : (h + 1) * dim, :])
        a = inside[:, here] + dot(lead, lead_values[:, here], (1, 0))
        attended[:, here] = a + dot(qs2[:, here], state, (1, 0))


def sums_kernel(dim, attended, own, got, g2, sums):
    size, width = attended.shape
    rows = size // PAIR
    here, there = halves(rows)
    g2[here, :] = own[3 * rows :, :]
    g2[there, :] = got[...]
    squares = jnp.zeros((size, dim), F32)
    products = jnp.zeros((size, dim), F32)
    for at in range(0, width, dim):
        a = attended[:, at : at + dim]
        squares = squares + a * a
        products = products + a * g2[:, at : at + dim].astype(F32)
    ones = jnp.ones((8, dim), BF16)
    both = jnp.concatenate([squares, products], 0)
    line = sum(dot(ones, part, (1, 1)) for part in split3(both))[:1]
    sums[...] = jnp.concatenate([line[:, :size], line[:, size:]], 0)


def grad_kernel(width_all, attended, q2, qs2, lead_mixing, lead_values, g2, *refs):
    *sums, scales, grad = refs[:-PARTS]
    adjoints = refs[-PARTS:]
    size, width = q2.shape
    dim = adjoints[0].shape[1]
    heads = width // dim
    total = sum(ref[...] for ref in sums[1:]) + sums[0][...]
    inverse = 1.0 / jnp.sqrt(total[0:1] / width_all + 1e-06)
    shift = total[1:2] / width_all * inverse
    both = jnp.concatenate([inverse, shift * inverse * inverse, jnp.zeros((6, size), F32)], 0)
    scales[...] = both
    both = both.T
    inverse, pull = both[:, 0:1], both[:, 1:2]
    for h in range(heads):
        lanes = slice(h * dim, (h + 1) * dim)
        d = (g2[:, lanes].astype(F32) * inverse - attended[:, lanes] * pull).astype(BF16)
        grad[:, lanes] = d
        part, at = divmod(h, heads // PARTS)
        adjoints[part][at * dim : (at + 1) * dim, :] = dot(qs2[:, lanes], d, (0, 0)).astype(BF16)
    scores = (dot(grad[...], lead_values[...], (1, 1)) * lead_mixing[...]).astype(BF16)
    tops = dot(scores, q2[...], (0, 0))
    per_part = heads // PARTS
    for i, adjoint in enumerate(adjoints):
        rows = [
            tops[LEAD * h : LEAD * (h + 1), h * dim : (h + 1) * dim]
            for h in range(i * per_part, (i + 1) * per_part)
        ]
        if LEAD * per_part < EDGE:
            rows.append(jnp.zeros((EDGE - LEAD * per_part, dim), F32))
        adjoint[width // PARTS :, :] = jnp.concatenate(rows, 0).astype(BF16)


def inner_grad_kernel(
    attended, scales, q2, kc2, v2, grad, weights, cum, *refs
):
    before, lead_weights = refs[:STEPS], refs[STEPS : 2 * STEPS]
    keep, send, partial, key_grad, vs2, normed = refs[2 * STEPS :]
    size, width = q2.shape
    dim = before[0].shape[1]
    heads = width // dim
    per_step = heads // STEPS
    start = lax.axis_index("ctx") < PAIR
    inverse = scales[...].T[:, 0:1]
    cum_rows = cum[...]
    cols = cum_rows.T
    growth = jnp.exp(cols)
    after = jnp.exp(cols[size - 1 :, :] - cols)
    for h in range(heads):
        lanes = slice(h * dim, (h + 1) * dim)
        vs2[:, lanes] = (v2[:, lanes].astype(F32) * after[:, h : h + 1]).astype(BF16)
        normed[:, lanes] = (attended[:, lanes] * inverse).astype(BF16)
        d = grad[:, lanes]
        scores = dot(d, v2[:, lanes], (1, 1)) * mixing_of(cum_rows, cols, h)
        scores = scores.astype(BF16)
        step, at = divmod(h, per_step)
        state = unless(start, before[step][at * dim : (at + 1) * dim, :])
        query_grad = dot(scores, kc2[:, lanes], (1, 0)) + growth[:, h : h + 1] * dot(
            d, state, (1, 1)
        )
        key_grad[:, lanes] = dot(scores, q2[:, lanes], (0, 0))
        partial[:, lanes] = query_grad + dot(weights[h], d, (0, 0))
    lead = sum(ref[...].astype(F32) for ref in lead_weights).astype(BF16)
    lead = dot(lead, grad[...], (0, 0))
    for h in range(heads):
        lanes = slice(h * dim, (h + 1) * dim)
        partial[:LEAD, lanes] = partial[:LEAD, lanes] + lead[LEAD * h : LEAD * (h + 1), lanes]
    here, there = halves(size // PAIR)
    keep[...] = normed[here, :]
    send[...] = normed[there, :]


def outer_grad_kernel(
    last, part, partial, key_grad, ks2, vs2, behind, more, taps, keep, send, padded, done
):
    size, width = partial.shape
    dim = behind.shape[1]
    heads = width // dim // PARTS
    chunk = width // PARTS
    mine = lax.rem(lax.axis_index("ctx"), PAIR)
    own = pl.ds(pl.multiple_of(mine * width + part * chunk, chunk), chunk)
    ends = lax.axis_index("ctx") >= last
    tops = unless(ends, behind[chunk:, :].astype(F32))
    for h in range(heads):
        at = part * heads + h
        lanes = slice(at * dim, (at + 1) * dim)
        here = slice(h * dim, (h + 1) * dim)
        state = unless(ends, behind[here, :])
        padded[:size, here] = key_grad[:, lanes] + dot(vs2[:, lanes], state, (1, 1))
        done[:, here] = partial[:, lanes] + dot(ks2[:, lanes], state, (1, 0))
        top = jnp.concatenate([tops[4 * h : 4 * h + 4], jnp.zeros((4, dim), F32)], 0)
        padded[size:, here] = top + more[:, lanes]
    total = done[...]
    for j in range(taps.shape[1]):
        total = total + taps[0, j : j + 1, own] * padded[j : j + size, :]
    done[...] = total
    here, there = halves(size // PAIR)
    first = lax.axis_index("pp") == 0
    keep[...] = unless(first, done[here, :]).astype(BF16)
    send[...] = unless(first, done[there, :]).astype(BF16)


def place_kernel(*refs):
    *pieces, out, sems = refs
    kept, got = pieces[: len(pieces) // 2], pieces[len(pieces) // 2 :]
    width = kept[0].shape[1]
    mine = lax.rem(lax.axis_index("ctx"), PAIR)
    pairs = []
    for half, parts in ((mine, kept), (1 - mine, got)):
        for i, part in enumerate(parts):
            start = pl.multiple_of((half * len(parts) + i) * width, width)
            pairs.append((part, out.at[0, :, pl.ds(start, width)]))
    for copy in copy_all(pairs, sems):
        copy.wait()


def placed(kept, got):
    pieces = kept + got
    rows = kept[0].shape[0]
    return call(
        place_kernel,
        [shape((1, rows, sum(piece.shape[1] for piece in pieces)), BF16)],
        *pieces,
        scratch=[pltpu.SemaphoreType.DMA((len(pieces),))],
        out_hbm=True,
    )[0]


def turned(block, axis, distance):
    count = lax.axis_size(axis)
    return lax.ppermute(block, axis, [(i, (i + distance) % count) for i in range(count)])


def swapped(block):
    return lax.ppermute(block, "ctx", [(i, i ^ 1) for i in range(lax.axis_size("ctx"))])


def to_earlier_section(block, flip):
    blocks, sections = lax.axis_size("ctx"), lax.axis_size("pp")
    route = [
        (c * sections + p, (c ^ flip) * sections + (p - 1) % sections)
        for c in range(blocks)
        for p in range(sections)
    ]
    return lax.ppermute(block, ("ctx", "pp"), route)


def summed_parts(part):
    blocks, count = lax.axis_size("ctx"), lax.axis_size("tp")

    def neighbour(block):
        return lax.ppermute(block, "tp", [(i, i ^ 1) for i in range(count)])

    def fetched(block, *ways):
        route = [
            (c * count + t, (c ^ ways[t % len(ways)][0]) * count + (t + ways[t % len(ways)][1]) % count)
            for c in range(blocks)
            for t in range(count)
        ]
        return lax.ppermute(block, ("ctx", "tp"), route)

    pair = part + neighbour(part)
    ways = [(1, 0)] + [(flip, k) for k in range(2, count, 2) for flip in (0, 1)]
    shared = [fetched(pair, *ways[i : i + 2]) for i in range(0, len(ways) - 1, 2)]
    parts = [pair, fetched(pair, ways[-1])]
    for block in shared:
        parts += [block, neighbour(block)]
    return parts


def per_device(queries, key_input, values, log_decay, conv_weight, out_grad):
    rows, width = queries.shape[1], queries.shape[2] // PAIR
    heads = log_decay.shape[2] // PAIR
    dim = width // heads
    size = PAIR * rows
    blocks = lax.axis_size("ctx")
    supers = blocks // PAIR
    width_all = queries.shape[2] * lax.axis_size("tp")
    log_decay = jnp.swapaxes(log_decay, 1, 2)
    arrays = (queries, key_input, values, out_grad, log_decay)
    queries, key_input, values, out_grad, decays = (
        pltpu.with_memory_space_constraint(x, pltpu.HBM) for x in arrays
    )

    step_width = width // STEPS
    *packed, own_cum = call(
        pack_kernel,
        [shape((2 * rows + EDGE, step_width), BF16)]
        + [shape((2 * rows, step_width), BF16)] * (STEPS - 1)
        + [shape((PAIR * heads, rows), F32)],
        key_input, values, decays,
        scratch=[pltpu.VMEM(log_decay.shape, F32), pltpu.SemaphoreType.DMA((1 + 2 * STEPS,))],
        hbm=range(3),
    )
    got = [swapped(part) for part in packed]
    edges = ()
    if supers > 2:
        edge = arrays[1][0, rows - EDGE :]
        near = lax.ppermute(edge[:, :width], "ctx", [(i, i + 1) for i in range(1, blocks - 1, 2)])
        far = lax.ppermute(edge[:, width:], "ctx", [(i, i + 2) for i in range(1, blocks - 2, 2)])
        edges = (near + far,)
    second, third, own = call(
        pack_more_kernel,
        [shape((rows, width), BF16)] * 2 + [shape((4 * rows, width), BF16)],
        queries, key_input, values, out_grad, packed[0][2 * rows :],
        scratch=[pltpu.SemaphoreType.DMA((6,))],
        hbm=range(4),
    )
    got_q, got_g = swapped(second), swapped(third)
    joined = [
        shape((size, width), BF16), shape((size, width), BF16), shape((EDGE, width), F32),
        shape((size, width), BF16), shape((step_width + EDGE, dim), BF16),
    ]
    room = [pltpu.VMEM((EDGE + size, step_width), F32)]
    kc2, v2, top, ks2, state, cum = call(
        join_kernel,
        joined + [shape((8, size), F32)],
        got[0], own, own_cum, conv_weight, *edges,
        scratch=room,
    )
    states = [state]
    for step in range(1, STEPS):
        kc2, v2, top, ks2, state = call(
            lambda *refs, step=step: join_next_kernel(step, *refs),
            joined,
            kc2, v2, top, ks2, got[step], own, cum, conv_weight, *edges,
            scratch=room,
            alias=((0, 0), (1, 1), (2, 2), (3, 3)),
        )
        states.append(state)
    carry = jnp.repeat(jnp.exp(cum[:heads, -1]), dim)[:, None]
    pair_index = lax.axis_index("ctx") // PAIR
    before = []
    for step, state in enumerate(states):
        moved = turned(state, "ctx", PAIR)
        for _ in range(supers - 2):
            earlier = unless(pair_index == 0, moved[:step_width]).astype(F32)
            earlier = carry[step * step_width : (step + 1) * step_width] * earlier
            earlier = (state[:step_width].astype(F32) + earlier).astype(BF16)
            moved = jnp.concatenate([turned(earlier, "ctx", PAIR), moved[step_width:]], 0)
        before.append(moved)

    q2, qs2, weights, inside, lead_mixing, lead_values = call(
        local_kernel,
        [shape((size, width), BF16)] * 2
        + [shape((heads, size, size), BF16), shape((size, width), F32)]
        + [shape((size, LEAD * heads), F32), shape((LEAD * heads, width), BF16)],
        got_q, own, kc2, v2, cum,
        flops=4 * heads * size * size * dim,
    )
    lead_weights = []
    for step in range(STEPS):
        kc2, inside, lead = call(
            lambda *refs, step=step: attend_kernel(step, *refs),
            [shape(kc2.shape, BF16), shape((size, width), F32), shape((size, LEAD * heads), BF16)],
            kc2, inside, q2, qs2, top, conv_weight, lead_mixing, lead_values, before[step],
            scratch=[pltpu.VMEM((4 * LEAD, step_width), F32)],
            alias=((0, 0), (1, 1)),
        )
        lead_weights.append(lead)
    attended = inside
    g2, sums = call(
        lambda *refs: sums_kernel(dim, *refs),
        [shape((size, width), BF16), shape((2, size), F32)],
        attended, own, got_g,
    )
    parts = summed_parts(sums)
    chunk = width // PARTS
    scales, grad, *adjoints = call(
        lambda *refs: grad_kernel(width_all, *refs),
        [shape((8, size), F32), shape((size, width), BF16)]
        + [shape((chunk + EDGE, dim), BF16)] * PARTS,
        attended, q2, qs2, lead_mixing, lead_values, g2, *parts,
    )
    last_pair = pair_index == supers - 1
    behind = []
    for i, adjoint in enumerate(adjoints):
        moved = turned(adjoint, "ctx", -PAIR)
        for _ in range(supers - 2):
            later = unless(last_pair, moved[:chunk]).astype(F32)
            joined = adjoint[:chunk].astype(F32) + carry[i * chunk : (i + 1) * chunk] * later
            state = turned(joined.astype(BF16), "ctx", -PAIR)
            moved = jnp.concatenate([state, moved[chunk:]], 0)
        behind.append(moved)
    more = jnp.zeros((8, width), F32)
    if supers > 2:
        after = jnp.exp(cum[:heads, -1:] - cum[:heads, :8])
        states = jnp.concatenate([part[:chunk] for part in behind], 0)
        state_part = jnp.einsum(
            "shv,hkv->shk",
            v2[:8].reshape(8, heads, dim),
            unless(last_pair, states).reshape(heads, dim, dim),
            preferred_element_type=F32,
        )
        more = turned((after.T[:, :, None] * state_part).reshape(8, width), "ctx", -PAIR)
        more = unless(last_pair, more)

    keep, send, partial, key_grad, vs2 = call(
        inner_grad_kernel,
        [shape((rows, width), BF16)] * 2
        + [shape((size, width), F32)] * 2
        + [shape((size, width), BF16)],
        attended, scales, q2, kc2, v2, grad, weights, cum, *before, *lead_weights,
        scratch=[pltpu.VMEM((size, width), BF16)],
        flops=10 * heads * size * size * dim,
    )
    out_keep, out_send = keep, send
    kept, got = [], []
    for i in range(PARTS):
        keep, send = call(
            lambda *refs, i=i: outer_grad_kernel(blocks - PAIR, i, *refs),
            [shape((rows, chunk), BF16)] * 2,
            partial, key_grad, ks2, vs2, behind[i], more, conv_weight,
            scratch=[pltpu.VMEM((size + 8, chunk), F32), pltpu.VMEM((size, chunk), F32)],
        )
        kept.append(to_earlier_section(keep, 0))
        got.append(to_earlier_section(send, 1))
    input_next = placed(kept, got)
    return (placed([out_keep], [swapped(out_send)]), input_next)


def solution(mesh):
    placed = (
        P("pp", "ctx", "tp"),
        P("pp", "ctx", "tp"),
        P("pp", "ctx", "tp"),
        P("pp", "ctx", "tp"),
        P("pp", None, "tp"),
        P("pp", "ctx", "tp"),
    )
    return jax.shard_map(
        per_device,
        mesh=mesh,
        in_specs=placed,
        out_specs=(P("pp", "ctx", "tp"), P("pp", "ctx", "tp")),
        check_vma=False,
    )
```
